32 devices in a mesh: batch: 8 (over y, x, core), seq: 4 (over z).
Axes of the slice: x: 2, y: 2, z: 4, core: 2. Of those that a mesh axis runs over, the one named last changes fastest.
Arguments:
- tokens: bfloat16 [16, 1024, 1024], P('batch', 'seq'), may hold values from -6 to 6
- segment_ids: int32 [16, 1024], P('batch', 'seq'), may hold values from 0 to 3, as said below
- padding_mask: int32 [16, 1024], P('batch', 'seq'), may hold values from 0 to 1, as said below
- qkv_weight: bfloat16 [1024, 3072], P(('batch', 'seq')), may hold values from -0.1875 to 0.1875
- out_weight: bfloat16 [1024, 1024], P(('batch', 'seq')), may hold values from -1 to 1
- wide_weight: bfloat16 [1024, 5248], P(('batch', 'seq')), may hold values from -0.1875 to 0.1875
- narrow_weight: bfloat16 [1024, 2624], P(('batch', 'seq')), may hold values from -0.25 to 0.25
- first_gain: bfloat16 [1024], P(('batch', 'seq')), may hold values from 0.099609375 to 1.8984375
- second_gain: bfloat16 [1024], P(('batch', 'seq')), may hold values from 0.099609375 to 1.8984375
- cotangent: bfloat16 [16, 1024, 1024], P('batch', 'seq'), may hold values from -6 to 6
Outputs:
- outputs: bfloat16 [16, 1024, 1024], P('batch', 'seq')
- grad_tokens: bfloat16 [16, 1024, 1024], P('batch', 'seq')
- grad_qkv: float32 [1024, 3072], P(('batch', 'seq'))
- grad_out: float32 [1024, 1024], P(('batch', 'seq'))
- grad_wide: float32 [1024, 5248], P(('batch', 'seq'))
- grad_narrow: float32 [1024, 2624], P(('batch', 'seq'))
- grad_first_gain: float32 [1024], P(('batch', 'seq'))
- grad_second_gain: float32 [1024], P(('batch', 'seq'))
The draws below stay inside these ranges and needn't reach their ends.
Inputs may be any that keep to these rules, and one draw needn't show every extreme that they name: `segment_ids`: in every sequence the document numbers start at 0, never fall, and rise by one where a new document begins; in each group of 2 sequences that share a batch index one sequence is a single document. `padding_mask`: Padding, where a sequence has any, fills its last positions, fewer than 129 of them; single-document sequences have none.
All inputs are finite; a program needn't handle non-finite values.
Results may differ from the reference program's by a relative error of at most 0.017.
Values may be sent and summed in bfloat16 or wider, within the bound.
A program may use at most 192 MiB of HBM per device.

```python
import jax
import jax.numpy as jnp
from jax import lax

D = 1024
HEADS = 16
HDIM = 64
FF = 2624
ROWS_DEV = 2
SEQ_DEV = 256
HALF = 64
SEQS = 16
LEN = 1024
N_SEQ = 4


def row_plan(key):
    groups = SEQS // ROWS_DEV
    spanning = jax.random.randint(jax.random.fold_in(key, 1), (groups,), 0, ROWS_DEV)
    owner = jnp.arange(SEQS, dtype=jnp.int32)
    whole_doc = owner % ROWS_DEV == jnp.repeat(spanning, ROWS_DEV)
    return (owner, whole_doc)


def draw_segment_ids(key, part):
    owner, whole_doc = row_plan(key)
    key = jax.random.fold_in(key, 21)
    offsets = jax.random.randint(jax.random.fold_in(key, 1), (SEQS, N_SEQ), 0, SEQ_DEV)
    coins = jax.random.randint(jax.random.fold_in(key, 2), (SEQS, N_SEQ), 0, 2)
    coins = jnp.where((owner < ROWS_DEV)[:, None], 1, coins)
    place = jnp.arange(LEN, dtype=jnp.int32)
    block_of = place // SEQ_DEV
    starts = place[None, :] % SEQ_DEV == jnp.repeat(offsets, SEQ_DEV, axis=1)
    starts = starts & (jnp.repeat(coins, SEQ_DEV, axis=1) == 1)
    starts = starts & (block_of[None, :] >= 1) & jnp.logical_not(whole_doc)[:, None]
    return jnp.cumsum(starts.astype(jnp.int32), axis=1).astype(jnp.int32)


def draw_padding_mask(key, part):
    owner, whole_doc = row_plan(key)
    key = jax.random.fold_in(key, 22)
    cut_len = jax.random.randint(key, (SEQS,), 1, SEQ_DEV // 2 + 1)
    cut_len = jnp.where(whole_doc, 0, cut_len)
    place = jnp.arange(LEN, dtype=jnp.int32)
    return (place[None, :] < LEN - cut_len[:, None]).astype(jnp.int32)


def shard_levels(key, dims, split, smallest, largest):
    def one(dim, parts):
        steps = jax.random.uniform(jax.random.fold_in(jax.random.fold_in(key, 6), dim), (parts,), jnp.float32, smallest / len(split), largest / len(split))
        return jnp.repeat(jnp.exp(steps), dims[dim] // parts).reshape((-1,) + (1,) * (len(dims) - dim - 1))

    factor_of = one(*split[0])
    for cut in split[1:]:
        factor_of = factor_of * one(*cut)
    return factor_of


def bell_draw(key, shape, deviation, most, pieces=(), kind=jnp.bfloat16):
    level = shard_levels(key, shape, pieces, -0.22, 0.18) if pieces else 1.0
    array = jax.random.normal(key, shape, jnp.float32) * deviation * level
    return jnp.minimum(jnp.maximum(array, -most), most).astype(kind)


def setup_inputs(seed: int = 0) -> dict:
    key_list = jax.random.split(jax.random.key(seed), 11)
    tokens = bell_draw(key_list[0], (SEQS, LEN, D), 1.0, 6.0, ((0, 8), (1, 4)))
    segment_ids = draw_segment_ids(jax.random.fold_in(key_list[10], 71), 0)
    padding_mask = draw_padding_mask(jax.random.fold_in(key_list[10], 71), 0)
    qkv_weight = bell_draw(key_list[3], (D, 3 * D), D ** -0.5, 0.1875, ((0, 32),))
    out_weight = bell_draw(key_list[4], (D, D), (D // 32) ** -0.5, 1.0, ((0, 32),))
    wide_weight = bell_draw(key_list[5], (D, 2 * FF), D ** -0.5, 0.1875, ((0, 32),))
    narrow_weight = bell_draw(key_list[6], (D, FF), (FF // 4) ** -0.5, 0.25, ((0, 32),))
    first_gain = jnp.clip(1.0 + 0.18 * jax.random.normal(key_list[7], (D,), jnp.float32), 0.099609375, 1.8984375).astype(jnp.bfloat16)
    second_gain = jnp.clip(1.0 + 0.18 * jax.random.normal(key_list[8], (D,), jnp.float32), 0.099609375, 1.8984375).astype(jnp.bfloat16)
    cotangent = bell_draw(key_list[9], (SEQS, LEN, D), 1.0, 6.0, ((0, 8), (1, 4)))
    return {"tokens": tokens, "segment_ids": segment_ids, "padding_mask": padding_mask, "qkv_weight": qkv_weight, "out_weight": out_weight, "wide_weight": wide_weight, "narrow_weight": narrow_weight, "first_gain": first_gain, "second_gain": second_gain, "cotangent": cotangent}


@jax.custom_vjp
def low(v):
    return lax.optimization_barrier(v.astype(jnp.bfloat16)).astype(jnp.float32)

@jax.custom_vjp
def low_back(v):
    return v

def low_keep(v):
    return (low(v), None)

def low_pass(kept, grad):
    return (grad,)

def back_keep(v):
    return (v, None)

def back_low(kept, grad):
    return (low(grad),)
low.defvjp(low_keep, low_pass)
low_back.defvjp(back_keep, back_low)
NORM_EPS = 1e-05
MASK_FILL = -1e+30
ROPE_BASE = 10000.0
HIGHEST = lax.Precision.HIGHEST

def layer_norm(values, norm_gain):
    center = values - lax.optimization_barrier(jnp.mean(values, -1, keepdims=True))
    spread = lax.optimization_barrier(jnp.mean(center * center, -1, keepdims=True))
    return center * lax.rsqrt(spread + NORM_EPS) * norm_gain

def rope_angles(positions):
    half_dim = HDIM // 2
    frequency = ROPE_BASE ** (-(2.0 * jnp.arange(half_dim, dtype=jnp.float32)) / HDIM)
    return positions[:, None] * frequency[None, :]

def rotate(vectors, angles):
    half_dim = vectors.shape[-1] // 2
    cosine = jnp.cos(angles)[:, None, :]
    sine = jnp.sin(angles)[:, None, :]
    first_half = vectors[..., :half_dim]
    second_half = vectors[..., half_dim:]
    return jnp.concatenate([first_half * cosine - second_half * sine, second_half * cosine + first_half * sine], -1)

def attend(queries, key_rows, values, segments, key_tags):
    length = queries.shape[0]
    block_len = min(512, length)
    block_count = length // block_len
    score_scale = HDIM ** (-0.5)
    pad_keys = jnp.pad(key_rows, ((HALF, HALF), (0, 0), (0, 0)))
    pad_values = jnp.pad(values, ((HALF, HALF), (0, 0), (0, 0)))
    pad_tags = jnp.pad(key_tags, (HALF, HALF))

    def one_block(block_index):
        first_row = (block_index * block_len).astype(jnp.int32)
        block_queries = lax.dynamic_slice_in_dim(queries, first_row, block_len, 0)
        block_segs = lax.dynamic_slice_in_dim(segments, first_row, block_len, 0)
        block_keys = lax.dynamic_slice_in_dim(pad_keys, first_row, block_len + 2 * HALF, 0)
        block_values = lax.dynamic_slice_in_dim(pad_values, first_row, block_len + 2 * HALF, 0)
        block_tags = lax.dynamic_slice_in_dim(pad_tags, first_row, block_len + 2 * HALF, 0)
        query_pos = first_row + jnp.arange(block_len, dtype=jnp.int32)
        key_pos = first_row - HALF + jnp.arange(block_len + 2 * HALF, dtype=jnp.int32)
        offsets = key_pos[None, :] - query_pos[:, None]
        in_band = jnp.abs(offsets) <= HALF
        same_doc = (block_tags[None, :] == block_segs[:, None] + 1) | (offsets == 0)
        allowed = (in_band & same_doc)[None]
        scores = low_back(jnp.einsum('qhd,khd->hqk', block_queries, block_keys, precision=HIGHEST) * score_scale)
        masked = jnp.where(allowed, scores, MASK_FILL)
        row_max = lax.optimization_barrier(jnp.max(masked, -1, keepdims=True))
        weights = jnp.where(allowed, jnp.exp(masked - row_max), 0.0)
        totals = lax.optimization_barrier(jnp.sum(weights, -1, keepdims=True))
        attn_probs = low(weights / totals)
        return jnp.einsum('hqk,khd->qhd', attn_probs, block_values, precision=HIGHEST)
    blocks = lax.map(jax.checkpoint(one_block), jnp.arange(block_count, dtype=jnp.int32))
    return blocks.reshape(length, D)

def forward(hidden, segments, key_tags, qkv_weight, out_weight, wide_weight, narrow_weight, first_gain, second_gain):
    length = hidden.shape[0]
    normed = low(layer_norm(hidden, first_gain))
    projected = low_back(jnp.dot(normed, qkv_weight, precision=HIGHEST))
    angles = rope_angles(jnp.arange(length, dtype=jnp.int32).astype(jnp.float32))
    queries = low(rotate(projected[:, :D].reshape(length, HEADS, HDIM), angles))
    key_rows = low(rotate(projected[:, D:2 * D].reshape(length, HEADS, HDIM), angles))
    values = low(projected[:, 2 * D:].reshape(length, HEADS, HDIM))
    attended = low_back(low(attend(queries, key_rows, values, segments, key_tags)))
    branch = low_back(jnp.dot(attended, out_weight, precision=HIGHEST))
    middle = hidden + branch
    second = low(layer_norm(middle, second_gain))
    expanded = low_back(jnp.dot(second, wide_weight, precision=HIGHEST))
    activated = low(jax.nn.gelu(expanded[:, :FF], approximate=False) * expanded[:, FF:])
    return middle + jnp.dot(activated, narrow_weight.T, precision=HIGHEST)

def reference(tokens, segment_ids, padding_mask, qkv_weight, out_weight, wide_weight, narrow_weight, first_gain, second_gain, cotangent):
    params = (qkv_weight.astype(jnp.float32), out_weight.astype(jnp.float32), wide_weight.astype(jnp.float32), narrow_weight.astype(jnp.float32), first_gain.astype(jnp.float32), second_gain.astype(jnp.float32))
    key_tags = jnp.where(padding_mask == 1, segment_ids + 1, 0).astype(jnp.int32)

    def one_sequence(running, sequence):
        hidden, segments, tags_row, upstream = sequence
        produced, pullback = jax.vjp(lambda inputs, *weights: forward(inputs, segments, tags_row, *weights), hidden, *params)
        gradients = pullback(upstream)
        running = tuple((total_sum + piece for total_sum, piece in zip(running, gradients[1:])))
        return (running, (produced, gradients[0]))
    start_sums = tuple((jnp.zeros_like(weight_arr) for weight_arr in params))
    sums, (produced, grad_tokens) = lax.scan(one_sequence, start_sums, (tokens.astype(jnp.float32), segment_ids, key_tags, cotangent.astype(jnp.float32)))
    return (produced.astype(jnp.bfloat16), grad_tokens.astype(jnp.bfloat16), sums[0], sums[1], sums[2], sums[3], sums[4], sums[5])
```

```python
import functools

import jax
import jax.numpy as jnp
from jax import lax
from jax.experimental import pallas as pl
from jax.experimental.pallas import tpu as pltpu
from jax.sharding import PartitionSpec as P

MESH = pl.DeviceIdType.MESH
HDIM = 64
FF = 2624
PADDED = 2688
HALF = 64
NORM_EPS = 1e-05
MASK_FILL = -1e30
ROPE_BASE = 10000.0


GATHER_STREAMS = (
    ("zxy", "g", 0, 128),
    ("zxy", "q", 0, 768),
    ("zyx", "q", 768, 640),
    ("yxz", "q", 1408, 128),
    ("zxy", "q", 1536, 640),
    ("zyx", "q", 2176, 640),
    ("xyz", "q", 2816, 128),
    ("yxz", "q", 2944, 128),
    ("zxy", "o", 0, 384),
    ("zyx", "o", 384, 384),
    ("yxz", "o", 768, 256),
    ("zxy", "w", 0, 640),
    ("zyx", "w", 640, 640),
    ("xyz", "w", 1280, 384),
    ("yxz", "w", 1664, 128),
    ("zxy", "w", 1792, 640),
    ("zyx", "w", 2432, 640),
    ("xyz", "w", 3072, 384),
    ("yxz", "w", 3456, 128),
    ("zxy", "w", 3584, 768),
    ("zyx", "w", 4352, 768),
    ("xyz", "w", 5120, 128),
    ("yxz", "w", 5248, 128),
    ("zxy", "n", 0, 640),
    ("zyx", "n", 640, 512),
    ("xyz", "n", 1152, 256),
    ("yxz", "n", 1408, 384),
    ("zxy", "n", 1792, 256),
    ("zyx", "n", 2048, 128),
    ("yxz", "n", 2176, 512),
)
GATHER_ORDER = (
    0, 7, 14, 21, 28, 42, 49, 70, 91, 98, 1, 119, 35, 22, 126, 43, 50, 147, 154, 8, 71, 99, 175, 92,
    182, 15, 127, 2, 120, 23, 155, 203, 29, 44, 9, 3, 51, 56, 16, 63, 24, 4, 10, 17, 25, 72, 5, 36,
    77, 30, 6, 84, 26, 37, 45, 27, 18, 52, 11, 100, 93, 46, 31, 53, 47, 54, 38, 57, 105, 48, 64, 58,
    55, 65, 19, 73, 112, 59, 128, 12, 74, 20, 32, 121, 75, 78, 13, 85, 39, 76, 133, 79, 86, 66, 101,
    140, 60, 94, 80, 156, 102, 33, 161, 87, 40, 95, 168, 67, 103, 34, 189, 196, 41, 104, 96, 81,
    106, 61, 113, 97, 107, 114, 62, 129, 68, 88, 122, 69, 115, 108, 130, 123, 131, 82, 132, 89, 148,
    124, 134, 83, 183, 116, 141, 90, 135, 109, 125, 142, 157, 149, 136, 143, 150, 184, 158, 159,
    151, 117, 162, 160, 169, 110, 152, 176, 163, 118, 170, 204, 164, 137, 111, 153, 144, 185, 177,
    171, 186, 205, 187, 165, 178, 190, 188, 138, 197, 191, 198, 192, 179, 172, 139, 145, 206, 199,
    193, 180, 146, 181, 207, 166, 173, 200, 208, 167, 201, 194, 174, 209, 202, 195,
)
SCATTER_STREAMS = (
    ("zxy", "n", 1792, 384),
    ("zyx", "n", 2176, 384),
    ("yxz", "n", 2560, 128),
    ("zxy", "n", 0, 768),
    ("zyx", "n", 768, 640),
    ("xyz", "n", 1408, 128),
    ("yxz", "n", 1536, 256),
    ("zxy", "w", 3584, 640),
    ("zyx", "w", 4224, 640),
    ("xyz", "w", 4864, 256),
    ("yxz", "w", 5120, 256),
    ("zxy", "w", 1792, 640),
    ("zyx", "w", 2432, 640),
    ("xyz", "w", 3072, 384),
    ("yxz", "w", 3456, 128),
    ("zxy", "w", 0, 640),
    ("zyx", "w", 640, 640),
    ("xyz", "w", 1280, 128),
    ("yxz", "w", 1408, 384),
    ("zxy", "o", 0, 512),
    ("zyx", "o", 512, 256),
    ("xyz", "o", 768, 256),
    ("zxy", "q", 1536, 640),
    ("zyx", "q", 2176, 512),
    ("xyz", "q", 2688, 384),
    ("zxy", "q", 0, 640),
    ("zyx", "q", 640, 768),
    ("xyz", "q", 1408, 128),
    ("yxz", "g", 0, 128),
)
SCATTER_ORDER = (
    0, 7, 14, 21, 1, 28, 8, 15, 35, 42, 49, 22, 16, 56, 29, 36, 43, 17, 63, 70, 77, 37, 84, 44, 38,
    91, 64, 98, 2, 105, 45, 71, 9, 112, 18, 30, 65, 119, 23, 126, 133, 72, 3, 10, 140, 147, 19, 39,
    46, 154, 50, 57, 4, 66, 161, 11, 20, 31, 168, 24, 175, 5, 12, 182, 32, 6, 13, 25, 189, 47, 196,
    67, 40, 33, 78, 73, 85, 92, 26, 48, 41, 34, 99, 27, 93, 58, 100, 51, 94, 120, 74, 127, 101, 86,
    68, 79, 59, 52, 69, 75, 95, 102, 113, 106, 60, 76, 53, 87, 80, 61, 54, 88, 62, 81, 96, 103, 134,
    55, 141, 121, 89, 128, 82, 104, 97, 107, 90, 122, 83, 114, 129, 148, 162, 108, 123, 142, 149,
    155, 115, 130, 109, 124, 135, 116, 150, 110, 125, 143, 183, 169, 117, 111, 131, 151, 144, 136,
    163, 118, 145, 132, 170, 176, 146, 137, 152, 156, 164, 171, 138, 153, 190, 165, 172, 197, 139,
    184, 191, 166, 157, 177, 192, 198, 167, 158, 173, 193, 199, 159, 178, 185, 174, 194, 200, 179,
    160, 195, 201, 186, 180, 202, 187, 181, 188,
)


def place():
    b=lax.axis_index("batch"); z=lax.axis_index("seq")
    return b, z, b//4, (b//2)%2, b%2

def enter(zn):
    bar=pltpu.get_barrier_semaphore()
    b,z,_,_,_=place()
    for m in (1,2,4):
        pl.semaphore_signal(bar,1,device_id=(b^m,z),device_id_type=MESH)
    @pl.when(z<zn-1)
    def _(): pl.semaphore_signal(bar,1,device_id=(b,z+1),device_id_type=MESH)
    @pl.when(z>0)
    def _(): pl.semaphore_signal(bar,1,device_id=(b,z-1),device_id_type=MESH)
    pl.semaphore_wait(bar,3+(z<zn-1).astype(jnp.int32)+(z>0).astype(jnp.int32))

class Counter:
    def __init__(self): self.n=0
    def take(self,k=1):
        r=self.n; self.n+=k; return r

def gather_steps(streams, shards, fulls, ssem, rsem, ctr):
    b,z,y,x,c=place()
    out=[]; finals=[]
    def rdma(src,dst,i,dev):
        return pltpu.make_async_remote_copy(src,dst,ssem.at[i],rsem.at[i],device_id=dev,device_id_type=MESH)
    for (order,name,c0,cn) in streams:
        full=fulls[name]; cols=pl.ds(c0,cn)
        region={}
        def idx(region, zz=None, flip=None):
            yy=slice(None) if 'y' in region else ((1-y) if flip=='y' else y)
            xx=slice(None) if 'x' in region else ((1-x) if flip=='x' else x)
            if zz is None: zi=slice(None) if 'z' in region else pl.ds(pl.multiple_of(z*32,32),32)
            else: zi=pl.ds(pl.multiple_of(zz*32,32),32)
            return full.at[yy,xx,c,zi,cols]
        steps=[]; pending=None; first=True
        for d in order:
            own=shards[name].at[:,cols] if not region else None
            if d in 'xy':
                i=ctr.take(); dev=(b^(2 if d=='x' else 4), z)
                cp=rdma(idx(region) if own is None else own, idx(region), i, dev)
                rc=rdma(idx(region,flip=d),idx(region,flip=d),i,dev)
                def fn(pending=pending,cp=cp):
                    if pending: pending()
                    cp.start()
                steps.append(fn); pending=rc.wait_recv
                finals.append(cp.wait_send)
                region=dict(region); region[d]=True
            else:
                for hop in range(3):
                    i=ctr.take(2)
                    cu=jnp.logical_and(z-hop>=0, z<3); cd=jnp.logical_and(z+hop<=3, z>0)
                    pu=jnp.maximum(z-hop,0); pd=jnp.minimum(z+hop,3)
                    o=own if hop==0 else None
                    up=rdma(o if o is not None else idx(region,pu), idx(region,pu), i, (b,jnp.minimum(z+1,3)))
                    dn=rdma(o if o is not None else idx(region,pd), idx(region,pd), i+1, (b,jnp.maximum(z-1,0)))
                    ru=z-1-hop>=0; rd=z+1+hop<=3
                    rpu=jnp.maximum(z-1-hop,0); rpd=jnp.minimum(z+1+hop,3)
                    wu=rdma(idx(region,rpu),idx(region,rpu),i,(b,jnp.minimum(z+1,3)))
                    wd=rdma(idx(region,rpd),idx(region,rpd),i+1,(b,jnp.maximum(z-1,0)))
                    def fn(pending=pending,up=up,dn=dn,cu=cu,cd=cd):
                        if pending: pending()
                        pl.when(cu)(up.start); pl.when(cd)(dn.start)
                    steps.append(fn)
                    def pending(wu=wu,wd=wd,ru=ru,rd=rd):
                        pl.when(ru)(wu.wait_recv); pl.when(rd)(wd.wait_recv)
                    def fin(up=up,dn=dn,cu=cu,cd=cd):
                        pl.when(cu)(up.wait_send); pl.when(cd)(dn.wait_send)
                    finals.append(fin)
                region=dict(region); region['z']=True
        i=ctr.take(); dev=(b^1,z)
        cp=rdma(full.at[:,:,c,:,cols],full.at[:,:,c,:,cols],i,dev)
        rc=rdma(full.at[:,:,1-c,:,cols],full.at[:,:,1-c,:,cols],i,dev)
        def fn(pending=pending,cp=cp):
            pending(); cp.start()
        steps.append(fn)
        steps.append(rc.wait_recv)
        finals.append(cp.wait_send)
        out.append(steps)
    return out, finals

def add_into(dst, a, b, rows, width):
    def body(r):
        s=pl.ds(pl.multiple_of(r*16,16),16)
        dst[s,:]=a[s,:]+b[s,:]
    if rows<=32:
        for r in range(rows//16): body(r)
    else:
        pl.loop(0,rows//16)(body)

def scatter_steps(streams, grads, acc, bufs, outs, ssem, rsem, ctr):
    b,z,y,x,c=place()
    out=[]; finals=[]
    def rdma(src,dst,i,dev):
        return pltpu.make_async_remote_copy(src,dst,ssem.at[i],rsem.at[i],device_id=dev,device_id_type=MESH)
    def one(j,order,name,c0,cn):
        G=grads[name]; A=acc[name]; cols=pl.ds(c0,cn); B=bufs[j]; O=outs[name]
        steps=[]
        i=ctr.take(); dev=(b^1,z)
        cp=rdma(G.at[:,:,1-c,:,cols],B['c'],i,dev)
        steps.append(cp.start); finals.append(cp.wait_send)
        def pending(cp=cp):
            cp.wait_recv()
            for yy in range(2):
                for xx in range(2):
                    add_into(A.at[yy,xx,:,cols],A.at[yy,xx,:,cols],B['c'].at[yy,xx],128,cn)
        whole={'x','y','z'}
        def idx(fix, zz=None):
            return A.at[fix.get('y',slice(None)),fix.get('x',slice(None)),(pl.ds(pl.multiple_of(zz*32,32),32) if zz is not None else fix.get('z',slice(None))),cols]
        fix={}
        rev=order[::-1]
        for n,d in enumerate(rev):
            last=n==2
            if d in 'xy':
                i=ctr.take(); mine=y if d=='y' else x
                dev=(b^(2 if d=='x' else 4), z)
                f_other=dict(fix); f_other[d]=1-mine
                f_own=dict(fix); f_own[d]=mine
                cp=rdma(idx(f_other),B[d],i,dev)
                def fn(pending=pending,cp=cp):
                    pending(); cp.start()
                steps.append(fn); finals.append(cp.wait_send)
                def pending(cp=cp,f_own=f_own,d=d,last=last):
                    cp.wait_recv()
                    dst=idx(f_own)
                    if last:
                        O[:,cols]=dst[...].astype(jnp.float32)+B[d][...].astype(jnp.float32)
                    elif len(dst.shape)==2: add_into(dst,dst,B[d],dst.shape[0],cn)
                    else:
                        for q in range(2): add_into(dst.at[q],dst.at[q],B[d].at[q],dst.shape[1],cn)
                fix=f_own
            else:
                lead=[q for q in 'yx' if q not in fix]
                def acc_add(t,buf,fix=fix,lead=lead):
                    dst=idx(fix,t); s=pl.ds(pl.multiple_of(t*32,32),32)
                    if not lead: add_into(dst,dst,buf.at[s],32,cn)
                    elif len(lead)==2:
                        for yy in range(2):
                            for xx in range(2): add_into(dst.at[yy,xx],dst.at[yy,xx],buf.at[yy,xx,s],32,cn)
                    else:
                        for q in range(2): add_into(dst.at[q],dst.at[q],buf.at[q,s],32,cn)
                def bat(buf,t,lead=lead):
                    return buf.at[tuple([slice(None)]*len(lead))+(pl.ds(pl.multiple_of(t*32,32),32),)]
                prev=None
                for h in (2,1,0):
                    i=ctr.take(2)
                    td=jnp.maximum(z-1-h,0); tu=jnp.minimum(z+1+h,3)
                    cd=z-1-h>=0; cu=z+1+h<=3
                    dn=rdma(idx(fix,td),bat(B['d'],td),i,(b,jnp.maximum(z-1,0)))
                    up=rdma(idx(fix,tu),bat(B['u'],tu),i+1,(b,jnp.minimum(z+1,3)))
                    rd=jnp.logical_and(z<3, z-h>=0); ru=jnp.logical_and(z>0, z+h<=3)
                    rtd=jnp.maximum(z-h,0); rtu=jnp.minimum(z+h,3)
                    wd=rdma(idx(fix,rtd),bat(B['d'],rtd),i,(b,jnp.maximum(z-1,0)))
                    wu=rdma(idx(fix,rtu),bat(B['u'],rtu),i+1,(b,jnp.minimum(z+1,3)))
                    def fn(pending=pending,up=up,dn=dn,cu=cu,cd=cd):
                        pending()
                        pl.when(cd)(dn.start); pl.when(cu)(up.start)
                    steps.append(fn)
                    def fin(up=up,dn=dn,cu=cu,cd=cd):
                        pl.when(cd)(dn.wait_send); pl.when(cu)(up.wait_send)
                    finals.append(fin)
                    def pending(wd=wd,wu=wu,rd=rd,ru=ru,rtd=rtd,rtu=rtu,acc_add=acc_add):
                        @pl.when(rd)
                        def _():
                            wd.wait_recv(); acc_add(rtd,B['d'])
                        @pl.when(ru)
                        def _():
                            wu.wait_recv(); acc_add(rtu,B['u'])
                fix=dict(fix); fix['z']=pl.ds(pl.multiple_of(z*32,32),32)
                if last:
                    def pending(pending=pending,fix=fix):
                        pending()
                        O[:,cols]=idx(fix)[...].astype(jnp.float32)
        steps.append(pending)
        out.append(steps)
    for j,s in enumerate(streams): one(j,*s)
    return out, finals

def landing(streams):
    res=[]
    for (order,name,c0,cn) in streams:
        d={'c':(2,2,128,cn)}
        have={'x':2,'y':2}; zr=128
        for q in order[::-1]:
            if q in 'xy':
                del have[q]
                d[q]=tuple(have.values())+(zr,cn)
            else:
                d['d']=tuple(have.values())+(128,cn); d['u']=d['d']; zr=32
        res.append(d)
    return res


WIDTHS = {"q": 3072, "g": 128, "o": 1024, "w": 2 * PADDED, "n": PADDED}
NAMES = tuple(WIDTHS)


def gather_kernel(*refs):
    count = len(NAMES)
    shards = dict(zip(NAMES, refs[:count]))
    fulls = dict(zip(NAMES, refs[count : 2 * count]))
    ssem, rsem, lsem = refs[2 * count :]
    b, z, y, x, c = place()
    local = [
        pltpu.make_async_copy(
            shards[n], fulls[n].at[y, x, c, pl.ds(pl.multiple_of(z * 32, 32), 32), :], lsem.at[i]
        )
        for i, n in enumerate(NAMES)
    ]
    for copy in local:
        copy.start()
    enter(4)
    steps, finals = gather_steps(GATHER_STREAMS, shards, fulls, ssem, rsem, Counter())
    flat = [f for s in steps for f in s]
    for copy in local:
        copy.wait()
    for i in GATHER_ORDER:
        flat[i]()
    for f in finals:
        f()


def gather_weights(*shards):
    fulls = pl.pallas_call(
        gather_kernel,
        out_shape=tuple(jax.ShapeDtypeStruct((2, 2, 2, 128, WIDTHS[n]), jnp.bfloat16) for n in NAMES),
        in_specs=[pl.BlockSpec(memory_space=pltpu.VMEM)] * len(NAMES),
        out_specs=tuple(pl.BlockSpec(memory_space=pl.ANY) for _ in NAMES),
        scratch_shapes=[
            pltpu.SemaphoreType.DMA((400,)),
            pltpu.SemaphoreType.DMA((400,)),
            pltpu.SemaphoreType.DMA((8,)),
        ],
        compiler_params=pltpu.CompilerParams(
            collective_id=1, has_side_effects=True, vmem_limit_bytes=32 << 20
        ),
    )(*shards)
    return [f.reshape(1024, f.shape[-1]) for f in fulls]


def scatter_kernel(shapes, *refs):
    count = len(NAMES)
    grads = dict(zip(NAMES, refs[:count]))
    outs = dict(zip(NAMES, refs[count : 2 * count]))
    acc = dict(zip(NAMES, refs[2 * count : 3 * count]))
    rest = list(refs[3 * count :])
    bufs = []
    for s in shapes:
        bufs.append(dict(zip(s, rest[: len(s)])))
        rest = rest[len(s) :]
    ssem, rsem, lsem = rest
    b, z, y, x, c = place()
    local = [
        pltpu.make_async_copy(grads[n].at[:, :, c], acc[n], lsem.at[i]) for i, n in enumerate(NAMES)
    ]
    for copy in local:
        copy.start()
    enter(4)
    steps, finals = scatter_steps(SCATTER_STREAMS, grads, acc, bufs, outs, ssem, rsem, Counter())
    flat = [f for s in steps for f in s]
    for copy in local:
        copy.wait()
    for i in SCATTER_ORDER:
        flat[i]()
    for f in finals:
        f()


def scatter_grads(*grads):
    shapes = landing(SCATTER_STREAMS)
    grads = [g.reshape(2, 2, 2, 128, g.shape[-1]) for g in grads]
    return pl.pallas_call(
        functools.partial(scatter_kernel, shapes),
        out_shape=tuple(jax.ShapeDtypeStruct((32, WIDTHS[n]), jnp.float32) for n in NAMES),
        in_specs=[pl.BlockSpec(memory_space=pl.ANY)] * len(NAMES),
        out_specs=tuple(pl.BlockSpec(memory_space=pltpu.VMEM) for n in NAMES),
        scratch_shapes=[pltpu.VMEM((2, 2, 128, WIDTHS[n]), jnp.bfloat16) for n in NAMES]
        + [pltpu.VMEM(v, jnp.bfloat16) for s in shapes for v in s.values()]
        + [
            pltpu.SemaphoreType.DMA((500,)),
            pltpu.SemaphoreType.DMA((500,)),
            pltpu.SemaphoreType.DMA((8,)),
        ],
        compiler_params=pltpu.CompilerParams(
            collective_id=2, has_side_effects=True, vmem_limit_bytes=60 << 20
        ),
    )(*grads)


def pad_halves(array):
    lead = array.shape[:-1]
    array = array.reshape(lead + (2, FF))
    array = jnp.pad(array, [(0, 0)] * len(lead) + [(0, 0), (0, PADDED - FF)])
    return array.reshape(lead + (2 * PADDED,))


def with_halo(array, sides, width):
    for axis, dim in sides:
        size, length = (lax.axis_size(axis), array.shape[dim])
        up = [(i, (i + 1) % size) for i in range(size - 1)]
        down = [(j, i) for i, j in up]
        last = lax.slice_in_dim(array, length - width, length, axis=dim)
        first = lax.slice_in_dim(array, 0, width, axis=dim)
        before = lax.ppermute(last, axis, up)
        after = lax.ppermute(first, axis, down)
        array = jnp.concatenate([before, array, after], axis=dim)
    return array


def norm_forward(values, norm_gain):
    center = values - jnp.mean(values, -1, keepdims=True)
    spread = jnp.mean(center * center, -1, keepdims=True)
    inverse = lax.rsqrt(spread + NORM_EPS)
    unit_part = center * inverse
    return (unit_part * norm_gain, unit_part, inverse)


def norm_backward(upstream, unit_part, inverse, norm_gain):
    scaled = upstream * norm_gain
    grad_gain = jnp.sum(upstream * unit_part, 0)
    grad_values = inverse * (
        scaled
        - jnp.mean(scaled, -1, keepdims=True)
        - unit_part * jnp.mean(scaled * unit_part, -1, keepdims=True)
    )
    return (grad_values, grad_gain)


def rope_angles(positions):
    half_dim = HDIM // 2
    frequency = ROPE_BASE ** (-(2.0 * jnp.arange(half_dim, dtype=jnp.float32)) / HDIM)
    return positions[:, None] * frequency[None, :]


def rotate(vectors, angles):
    half_dim = vectors.shape[-1] // 2
    cosine = jnp.cos(angles)[:, None, :]
    sine = jnp.sin(angles)[:, None, :]
    first_half = vectors[..., :half_dim]
    second_half = vectors[..., half_dim:]
    return jnp.concatenate(
        [first_half * cosine - second_half * sine, second_half * cosine + first_half * sine], -1
    )


def gated_unit(gate_in, gate_up):
    return jax.nn.gelu(gate_in, approximate=False) * gate_up


def band_scores(queries, key_rows, allowed):
    scores = jnp.einsum(
        "qhd,khd->hqk", queries, key_rows, preferred_element_type=jnp.float32
    ) * HDIM ** (-0.5)
    return jnp.where(allowed[None], scores, MASK_FILL)


def row_forward(entries):
    queries, key_rows, values, allowed = entries
    masked = band_scores(queries, key_rows, allowed)
    row_max = jnp.max(masked, -1, keepdims=True)
    weights = jnp.where(allowed[None], jnp.exp(masked - row_max), 0.0)
    totals = jnp.sum(weights, -1, keepdims=True)
    attn_probs = (weights / totals).astype(jnp.bfloat16)
    mixture = jnp.einsum("hqk,khd->qhd", attn_probs, values, preferred_element_type=jnp.float32)
    return (mixture.astype(jnp.bfloat16), row_max + jnp.log(totals))


def row_backward(entries):
    queries, key_rows, values, allowed, log_total, grad_mixture = entries
    masked = band_scores(queries, key_rows, allowed)
    attn_probs = jnp.where(allowed[None], jnp.exp(masked - log_total), 0.0)
    grad_probs = jnp.einsum(
        "qhd,khd->hqk", grad_mixture, values, preferred_element_type=jnp.float32
    )
    grad_values = jnp.einsum(
        "hqk,qhd->khd",
        attn_probs.astype(jnp.bfloat16),
        grad_mixture,
        preferred_element_type=jnp.float32,
    )
    inner = jnp.sum(grad_probs * attn_probs, -1, keepdims=True)
    grad_scores = (attn_probs * (grad_probs - inner)).astype(jnp.bfloat16)
    grad_queries = jnp.einsum(
        "hqk,khd->qhd", grad_scores, key_rows, preferred_element_type=jnp.float32
    ) * HDIM ** (-0.5)
    grad_keys = jnp.einsum(
        "hqk,qhd->khd", grad_scores, queries, preferred_element_type=jnp.float32
    ) * HDIM ** (-0.5)
    return (grad_queries, grad_keys, grad_values)


def unpack_edges(extended, row_count, extent, head_count):
    key_ext = extended[0][0].reshape(row_count, extent, head_count, HDIM)
    value_ext = extended[0][1].reshape(row_count, extent, head_count, HDIM)
    tag_ext = extended[1][0].astype(jnp.float32)
    return (key_ext, value_ext, tag_ext)


def body(
    tokens,
    segment_ids,
    padding_mask,
    qkv_weight,
    out_weight,
    wide_weight,
    narrow_weight,
    first_gain,
    second_gain,
    cotangent,
):
    row_count, seq_span, model_width = tokens.shape
    head_count = model_width // HDIM
    token_count = row_count * seq_span
    extent = seq_span + 2 * HALF
    direct = (lax.axis_size("batch"), lax.axis_size("seq")) == (8, 4)
    gains = jnp.stack([first_gain, second_gain], axis=1)
    shards = (
        qkv_weight,
        jnp.pad(gains, ((0, 0), (0, 126))),
        out_weight,
        pad_halves(wide_weight),
        jnp.pad(narrow_weight, ((0, 0), (0, PADDED - FF))),
    )
    if direct:
        gathered = gather_weights(*shards)
    else:
        gathered = [lax.all_gather(s, ("batch", "seq"), axis=0, tiled=True) for s in shards]
    qkv_full, gains_full, out_full, wide_full, narrow_full = gathered
    gain_one = gains_full[:, 0].astype(jnp.float32)
    gain_two = gains_full[:, 1].astype(jnp.float32)
    hidden = tokens.reshape(token_count, model_width).astype(jnp.float32)
    normed, unit_one, inv_one = norm_forward(hidden, gain_one)
    normed_low = normed.astype(jnp.bfloat16)
    projected = jnp.dot(normed_low, qkv_full, preferred_element_type=jnp.float32)
    positions = (lax.axis_index("seq") * seq_span + jnp.arange(seq_span, dtype=jnp.int32)).astype(
        jnp.float32
    )
    angles = rope_angles(positions)
    shaped = projected.reshape(row_count, seq_span, 3, head_count, HDIM)
    queries = rotate(shaped[:, :, 0], angles).astype(jnp.bfloat16)
    key_rows = rotate(shaped[:, :, 1], angles).astype(jnp.bfloat16)
    values = shaped[:, :, 2].astype(jnp.bfloat16)
    key_tags = (
        jnp.where(padding_mask == 1, segment_ids + 1, 0).astype(jnp.float32).astype(jnp.bfloat16)
    )
    tag_rows = key_tags[None]
    packed = jnp.stack(
        [
            key_rows.reshape(row_count, seq_span, model_width),
            values.reshape(row_count, seq_span, model_width),
        ]
    )
    extended = (with_halo(packed, (("seq", 2),), HALF), with_halo(tag_rows, (("seq", 2),), HALF))
    key_ext, value_ext, tag_ext = unpack_edges(extended, row_count, extent, head_count)
    offsets = (
        jnp.arange(extent, dtype=jnp.int32)[None, :]
        - HALF
        - jnp.arange(seq_span, dtype=jnp.int32)[:, None]
    )
    in_band = jnp.abs(offsets) <= HALF
    query_tags = (segment_ids + 1).astype(jnp.float32)
    same_doc = tag_ext[:, None, :] == query_tags[:, :, None]
    allowed = in_band[None] & (same_doc | (offsets == 0)[None])
    mixture, log_total = lax.map(row_forward, (queries, key_ext, value_ext, allowed))
    attended = mixture.reshape(token_count, model_width)
    branch = jnp.dot(attended, out_full, preferred_element_type=jnp.float32)
    middle = hidden + branch
    second, unit_two, inv_two = norm_forward(middle, gain_two)
    second_low = second.astype(jnp.bfloat16)
    expanded = jnp.dot(second_low, wide_full, preferred_element_type=jnp.float32)
    gate_in = expanded[:, :PADDED]
    gate_up = expanded[:, PADDED:]
    activated = gated_unit(gate_in, gate_up).astype(jnp.bfloat16)
    result = middle + jnp.einsum(
        "nf,df->nd", activated, narrow_full, preferred_element_type=jnp.float32
    )
    outputs = result.astype(jnp.bfloat16).reshape(row_count, seq_span, model_width)
    cot_low = cotangent.reshape(token_count, model_width)
    grad_act = jnp.einsum("nd,df->nf", cot_low, narrow_full, preferred_element_type=jnp.float32)
    grad_narrow = jnp.einsum("nd,nf->df", cot_low, activated, preferred_element_type=jnp.float32)
    _, pullback = jax.vjp(gated_unit, gate_in, gate_up)
    grad_gate_in, grad_gate_up = pullback(grad_act)
    grad_expanded = jnp.concatenate([grad_gate_in, grad_gate_up], -1).astype(jnp.bfloat16)
    grad_wide = jnp.einsum(
        "nd,nf->df", second_low, grad_expanded, preferred_element_type=jnp.float32
    )
    grad_second = jnp.einsum(
        "nf,df->nd", grad_expanded, wide_full, preferred_element_type=jnp.float32
    )
    grad_mid_norm, grad_gain_two = norm_backward(grad_second, unit_two, inv_two, gain_two)
    grad_middle = cot_low.astype(jnp.float32) + grad_mid_norm
    grad_branch = grad_middle.astype(jnp.bfloat16)
    grad_out_weight = jnp.einsum(
        "nd,ne->de", attended, grad_branch, preferred_element_type=jnp.float32
    )
    grad_attended = jnp.einsum(
        "ne,de->nd", grad_branch, out_full, preferred_element_type=jnp.float32
    ).astype(jnp.bfloat16)
    grad_attended = grad_attended.reshape(row_count, seq_span, head_count, HDIM)
    grad_queries, grad_key_ext, grad_value_ext = lax.map(
        row_backward, (queries, key_ext, value_ext, allowed, log_total, grad_attended)
    )
    edge_stack = jnp.stack(
        [
            grad_key_ext.reshape(row_count, extent, model_width),
            grad_value_ext.reshape(row_count, extent, model_width),
        ]
    )
    outgoing = jnp.concatenate([edge_stack[:, :, :HALF], edge_stack[:, :, extent - HALF :]], axis=2)
    incoming = with_halo(outgoing.astype(jnp.bfloat16), (("seq", 2),), HALF).astype(outgoing.dtype)
    owned_grads = edge_stack[:, :, HALF : HALF + seq_span]
    owned_grads = jnp.concatenate(
        [
            owned_grads[:, :, :HALF] + incoming[:, :, :HALF],
            owned_grads[:, :, HALF : seq_span - HALF],
            owned_grads[:, :, seq_span - HALF :] + incoming[:, :, 3 * HALF :],
        ],
        axis=2,
    )
    grad_keys = owned_grads[0].reshape(row_count, seq_span, head_count, HDIM)
    grad_values = owned_grads[1].reshape(row_count, seq_span, head_count, HDIM)
    grad_q_pre = rotate(grad_queries, -angles)
    grad_k_pre = rotate(grad_keys, -angles)
    grad_projected = (
        jnp.stack([grad_q_pre, grad_k_pre, grad_values], axis=2)
        .reshape(token_count, 3 * model_width)
        .astype(jnp.bfloat16)
    )
    grad_qkv = jnp.einsum(
        "nd,ne->de", normed_low, grad_projected, preferred_element_type=jnp.float32
    )
    grad_normed = jnp.einsum(
        "ne,de->nd", grad_projected, qkv_full, preferred_element_type=jnp.float32
    )
    grad_in_norm, grad_gain_one = norm_backward(grad_normed, unit_one, inv_one, gain_one)
    grad_tokens = (
        (grad_middle + grad_in_norm).astype(jnp.bfloat16).reshape(row_count, seq_span, model_width)
    )
    grad_gains = jnp.pad(jnp.stack([grad_gain_one, grad_gain_two], axis=1), ((0, 0), (0, 126)))
    grads = [
        g.astype(jnp.bfloat16)
        for g in (grad_qkv, grad_gains, grad_out_weight, grad_wide, grad_narrow)
    ]
    if direct:
        sums = scatter_grads(*grads)
    else:
        sums = [
            lax.psum_scatter(g, ("batch", "seq"), scatter_dimension=0, tiled=True).astype(jnp.float32)
            for g in grads
        ]
    sum_qkv, sum_gains, sum_out, sum_wide, sum_narrow = sums
    return (
        outputs,
        grad_tokens,
        sum_qkv,
        sum_out,
        jnp.concatenate([sum_wide[:, :FF], sum_wide[:, PADDED : PADDED + FF]], axis=1),
        sum_narrow[:, :FF],
        sum_gains[:, 0],
        sum_gains[:, 1],
    )


def solution(mesh):
    placed = (
        P("batch", "seq", None),
        P("batch", "seq"),
        P("batch", "seq"),
        P(("batch", "seq"), None),
        P(("batch", "seq"), None),
        P(("batch", "seq"), None),
        P(("batch", "seq"), None),
        P(("batch", "seq")),
        P(("batch", "seq")),
        P("batch", "seq", None),
    )
    return jax.shard_map(
        body,
        mesh=mesh,
        in_specs=placed,
        out_specs=(
            P("batch", "seq", None),
            P("batch", "seq", None),
            P(("batch", "seq"), None),
            P(("batch", "seq"), None),
            P(("batch", "seq"), None),
            P(("batch", "seq"), None),
            P(("batch", "seq")),
            P(("batch", "seq")),
        ),
        check_vma=False,
    )
```

```python
import functools

import jax
import jax.numpy as jnp
from jax import lax
from jax.experimental import pallas as pl
from jax.experimental.pallas import tpu as pltpu
from jax.sharding import PartitionSpec as P

MESH = pl.DeviceIdType.MESH
HDIM = 64
FF = 2624
PADDED = 2688
HALF = 64
NORM_EPS = 1e-05
MASK_FILL = -1e30
ROPE_BASE = 10000.0
INV_SQRT_2PI = 0.3989422804014327

GATHER_STREAMS = (
    ("zxy", "g", 0, 128),
    ("zxy", "q", 0, 768),
    ("zyx", "q", 768, 640),
    ("yxz", "q", 1408, 128),
    ("zxy", "q", 1536, 640),
    ("zyx", "q", 2176, 640),
    ("xyz", "q", 2816, 128),
    ("yxz", "q", 2944, 128),
    ("zxy", "o", 0, 384),
    ("zyx", "o", 384, 384),
    ("yxz", "o", 768, 256),
    ("zxy", "w", 0, 640),
    ("zyx", "w", 640, 640),
    ("xyz", "w", 1280, 384),
    ("yxz", "w", 1664, 128),
    ("zxy", "w", 1792, 640),
    ("zyx", "w", 2432, 640),
    ("xyz", "w", 3072, 384),
    ("yxz", "w", 3456, 128),
    ("zxy", "w", 3584, 768),
    ("zyx", "w", 4352, 768),
    ("xyz", "w", 5120, 128),
    ("yxz", "w", 5248, 128),
    ("zxy", "n", 0, 640),
    ("zyx", "n", 640, 512),
    ("xyz", "n", 1152, 256),
    ("yxz", "n", 1408, 384),
    ("zxy", "n", 1792, 256),
    ("zyx", "n", 2048, 128),
    ("yxz", "n", 2176, 512),
)
FORWARD_ORDER = (
    0, 1, 8, 15, 22, 29, 36, 43, 50, 57, 2, 64, 71, 23, 78, 92, 44, 51, 9, 99, 120, 72, 16, 127,
    148, 93, 100, 155, 24, 30, 121, 3, 128, 149, 176, 37, 183, 204, 45, 156, 211, 10, 177, 17, 184,
    205, 25, 4, 31, 38, 52, 11, 5, 46, 18, 26, 32, 6, 39, 58, 27, 65, 73, 53, 85, 7, 212, 28, 47,
    12, 54, 48, 19, 59, 66, 79, 213, 49, 74, 86, 55, 40, 56, 80, 75, 94, 33, 87, 20, 76, 101, 13,
    60, 21, 215, 77, 95, 81, 102, 106, 67, 14, 214, 113, 122, 41, 61, 96, 103, 34, 97, 68, 42, 88,
    104, 35, 216, 217, 98, 82, 105, 218, 219, 62, 69, 89, 63, 107, 70, 114, 129, 123, 83, 108, 220,
    221, 134, 90, 115, 84, 222, 130, 91, 109, 116, 124, 141, 131, 223, 135, 150, 157, 224, 110, 117,
    125, 132, 142, 136, 162, 225, 126, 133, 143, 151, 158, 169, 178, 226, 137, 144, 163, 152, 185,
    111, 227, 118, 159, 170, 164, 228, 112, 145, 138, 153, 160, 171, 179, 229, 119, 154, 161, 186,
    190, 197, 180, 206, 165, 172, 230, 187, 231, 146, 139, 191, 198, 232, 181, 207, 173, 233, 147,
    140, 166, 188, 192, 182, 199, 234, 189, 193, 208, 235, 174, 200, 236, 194, 209, 237, 167, 175,
    238, 201, 210, 168, 239, 195, 202, 240, 241, 196, 203, 242,
)
SCATTER_STREAMS = (
    ("zxy", "n", 1792, 384),
    ("zyx", "n", 2176, 384),
    ("yxz", "n", 2560, 128),
    ("zxy", "n", 0, 768),
    ("zyx", "n", 768, 640),
    ("xyz", "n", 1408, 128),
    ("yxz", "n", 1536, 256),
    ("zxy", "w", 3584, 896),
    ("zyx", "w", 4480, 512),
    ("yxz", "w", 4992, 384),
    ("zxy", "w", 1792, 640),
    ("zyx", "w", 2432, 768),
    ("xyz", "w", 3200, 128),
    ("yxz", "w", 3328, 256),
    ("zxy", "w", 0, 512),
    ("zyx", "w", 512, 896),
    ("yxz", "w", 1408, 384),
    ("zxy", "o", 0, 512),
    ("zyx", "o", 512, 256),
    ("xyz", "o", 768, 128),
    ("yxz", "o", 896, 128),
    ("zxy", "q", 2048, 640),
    ("xyz", "q", 2688, 384),
    ("zxy", "q", 1024, 256),
    ("zyx", "q", 1280, 640),
    ("xyz", "q", 1920, 128),
    ("zxy", "q", 0, 384),
    ("zyx", "q", 384, 384),
    ("xyz", "q", 768, 128),
    ("yxz", "q", 896, 128),
    ("xyz", "g", 0, 128),
)
SCATTER_ORDER = (
    0, 7, 14, 21, 1, 28, 8, 15, 35, 42, 49, 22, 16, 29, 36, 56, 43, 17, 63, 37, 70, 44, 77, 38, 64,
    84, 91, 2, 98, 45, 9, 105, 18, 30, 23, 112, 65, 119, 3, 126, 10, 133, 19, 39, 140, 147, 50, 46,
    66, 57, 154, 4, 31, 11, 20, 161, 24, 168, 5, 175, 182, 12, 32, 189, 25, 6, 40, 67, 196, 203,
    210, 13, 85, 78, 33, 92, 26, 41, 47, 58, 34, 86, 27, 93, 48, 87, 68, 71, 113, 94, 69, 59, 51,
    114, 60, 79, 95, 106, 134, 115, 52, 61, 88, 96, 99, 53, 62, 80, 97, 54, 141, 81, 135, 120, 72,
    55, 142, 82, 155, 136, 89, 143, 100, 83, 107, 73, 90, 156, 116, 127, 101, 74, 117, 121, 137,
    157, 148, 75, 102, 108, 144, 118, 138, 169, 76, 103, 139, 109, 122, 104, 128, 176, 110, 145,
    158, 123, 162, 149, 197, 177, 111, 129, 146, 124, 204, 170, 178, 198, 159, 130, 125, 190, 205,
    131, 150, 179, 199, 160, 183, 206, 132, 163, 151, 171, 180, 207, 211, 191, 152, 172, 164, 181,
    200, 153, 208, 184, 212, 173, 165, 192, 201, 213, 209, 166, 185, 174, 202, 193, 214, 167, 186,
    194, 215, 187, 216, 195, 188,
)


def place():
    b = lax.axis_index("batch")
    z = lax.axis_index("seq")
    return b, z, b // 4, (b // 2) % 2, b % 2


def remote(src, dst, sems, i, device):
    return pltpu.make_async_remote_copy(
        src_ref=src,
        dst_ref=dst,
        send_sem=sems[0].at[i],
        recv_sem=sems[1].at[i],
        device_id=device,
        device_id_type=MESH,
    )


def piece(t, n=32):
    return pl.ds(pl.multiple_of(t * n, n), n)


def enter(direct, n_seq):
    barrier = pltpu.get_barrier_semaphore()
    b, z = lax.axis_index("batch"), lax.axis_index("seq")

    def greet(device):
        pl.semaphore_signal(barrier, inc=1, device_id=device, device_id_type=MESH)

    if direct:
        for bit in (1, 2, 4):
            greet((b ^ bit, z))
    pl.when(z < n_seq - 1)(lambda: greet((b, z + 1)))
    pl.when(z > 0)(lambda: greet((b, z - 1)))
    near = (z < n_seq - 1).astype(jnp.int32) + (z > 0).astype(jnp.int32)
    pl.semaphore_wait(barrier, near + (3 if direct else 0))


class Tasks:
    def __init__(self):
        self.steps, self.names, self.finals, self.semaphores = [], [], [], 0

    def take(self, count=1):
        first = self.semaphores
        self.semaphores += count
        return first

    def add(self, name, step):
        self.names.append(name)
        self.steps.append(step)

    def run(self, order):
        for i in order:
            self.steps[i]()
        for final in self.finals:
            final()


def add_gather(tasks, streams, shards, fulls, sems):
    b, z, y, x, c = place()

    def one(j, order, name, first, count):
        full, cols = fulls[name], pl.ds(first, count)
        whole = set()

        def view(at=None, other=None):
            yy = slice(None) if "y" in whole else (1 - y if other == "y" else y)
            xx = slice(None) if "x" in whole else (1 - x if other == "x" else x)
            zz = piece(z if at is None else at) if "z" not in whole else slice(None)
            return full.at[yy, xx, c, zz, cols]

        pending, sub = None, 0
        for axis in order:
            own = None if whole else shards[name].at[:, cols]
            if axis in "xy":
                i, device = tasks.take(), (b ^ (2 if axis == "x" else 4), z)
                out = remote(view() if own is None else own, view(), sems, i, device)
                into = remote(view(other=axis), view(other=axis), sems, i, device)

                def step(pending=pending, out=out):
                    if pending:
                        pending()
                    out.start()

                tasks.add(f"g{j}.{sub}", step)
                tasks.finals.append(out.wait_send)
                pending, sub = into.wait_recv, sub + 1
            else:
                for hop in range(3):
                    i = tasks.take(2)
                    has_up, has_down = (z >= hop) & (z < 3), (z + hop <= 3) & (z > 0)
                    up_piece, down_piece = jnp.maximum(z - hop, 0), jnp.minimum(z + hop, 3)
                    above, below = (b, jnp.minimum(z + 1, 3)), (b, jnp.maximum(z - 1, 0))
                    start = own if hop == 0 else None
                    up = remote(view(up_piece) if start is None else start, view(up_piece), sems, i, above)
                    down = remote(
                        view(down_piece) if start is None else start, view(down_piece), sems, i + 1, below
                    )
                    from_below, from_above = z - 1 - hop >= 0, z + 1 + hop <= 3
                    low, high = jnp.maximum(z - 1 - hop, 0), jnp.minimum(z + 1 + hop, 3)
                    rise = remote(view(low), view(low), sems, i, above)
                    fall = remote(view(high), view(high), sems, i + 1, below)

                    def step(pending=pending, up=up, down=down, has_up=has_up, has_down=has_down):
                        if pending:
                            pending()
                        pl.when(has_up)(up.start)
                        pl.when(has_down)(down.start)

                    def pending(rise=rise, fall=fall, from_below=from_below, from_above=from_above):
                        pl.when(from_below)(rise.wait_recv)
                        pl.when(from_above)(fall.wait_recv)

                    def final(up=up, down=down, has_up=has_up, has_down=has_down):
                        pl.when(has_up)(up.wait_send)
                        pl.when(has_down)(down.wait_send)

                    tasks.add(f"g{j}.{sub}", step)
                    tasks.finals.append(final)
                    sub += 1
            whole.add(axis)
        i, device = tasks.take(), (b ^ 1, z)
        out = remote(full.at[:, :, c, :, cols], full.at[:, :, c, :, cols], sems, i, device)
        into = remote(full.at[:, :, 1 - c, :, cols], full.at[:, :, 1 - c, :, cols], sems, i, device)

        def step(pending=pending, out=out):
            pending()
            out.start()

        tasks.add(f"g{j}.{sub}", step)
        tasks.add(f"g{j}.{sub + 1}", into.wait_recv)
        tasks.finals.append(out.wait_send)

    for j, stream in enumerate(streams):
        one(j, *stream)


def dot(a, b):
    return jnp.dot(a, b, preferred_element_type=jnp.float32)


def dot_rows(a, b):
    return lax.dot_general(a, b, (((1,), (1,)), ((), ())), preferred_element_type=jnp.float32)


def dot_columns(a, b):
    return lax.dot_general(a, b, (((0,), (0,)), ((), ())), preferred_element_type=jnp.float32)


def tile(j, n):
    return pl.ds(pl.multiple_of(j * n, n), n)


def norm_parts(values):
    center = values - jnp.mean(values, -1, keepdims=True)
    inverse = lax.rsqrt(jnp.mean(center * center, -1, keepdims=True) + NORM_EPS)
    return center * inverse, inverse


def norm_rows(source, gain, target, n=64):
    @pl.loop(0, source.shape[0] // n)
    def _(i):
        unit, _ = norm_parts(source[tile(i, n), :].astype(jnp.float32))
        target[tile(i, n), :] = (unit * gain).astype(jnp.bfloat16)


def lanes(n):
    return lax.broadcasted_iota(jnp.int32, (n, 128), 1)


def rotate(u, cosine, sine):
    partner = jnp.where(lanes(u.shape[0]) % HDIM < HDIM // 2, pltpu.roll(u, 96, 1), pltpu.roll(u, 32, 1))
    return u * cosine + partner * sine


def pair_rows(block):
    zero, first = jnp.zeros_like(block), lanes(block.shape[0]) < HDIM
    return jnp.concatenate([jnp.where(first, block, zero), jnp.where(first, zero, block)], 0)


def weight_tile(full, cols):
    block = full[:, :, :, :, cols]
    return block.reshape(1024, block.shape[-1])


def forward_kernel(direct, n_seq, *refs):
    names = ("g", "q", "o", "w", "n")
    shards, refs = dict(zip(names, refs[:5])), refs[5:]
    tokens, cotangent, cosine, sine, tag_center, tag_edge, query_tag = refs[:7]
    refs = refs[7:]
    saved_names = ("q", "o", "w", "n", "normed", "queries", "keys", "values", "probs", "attended", "middle", "second")
    saved_names += ("slopes", "active", "own", "other", "gains")
    saved, refs = dict(zip(saved_names, refs[:17])), refs[17:]
    fulls, refs = dict(zip(names, refs[:5])), refs[5:]
    normed, queries, keys, values, probs, attended, middle, second, slopes, active, own, other, gains = refs[:13]
    flipped, bias, tag_prev, tag_next, send_sems, recv_sems, local_sems = refs[13:]
    sems = (send_sems, recv_sems)
    held = dict(fulls)
    held.update(normed=normed, queries=queries, keys=keys, values=values, probs=probs, attended=attended)
    held.update(middle=middle, second=second, slopes=slopes, active=active, own=own, other=other, gains=gains)
    b, z, y, x, c = place() if direct else (lax.axis_index("batch"), lax.axis_index("seq"), 0, 0, 0)
    rows, span = 2, 256
    tasks = Tasks()
    copies = {}

    def save(name):
        copies[name] = pltpu.make_async_copy(held[name], saved[name], local_sems.at[saved_names.index(name)])
        copies[name].start()

    def add_halo(name, wait_name, parts):
        (up_src, up_dst), (down_src, down_dst) = parts
        i = tasks.take(2)
        up = remote(up_src, up_dst, sems, i, (b, jnp.minimum(z + 1, n_seq - 1)))
        down = remote(down_src, down_dst, sems, i + 1, (b, jnp.maximum(z - 1, 0)))

        def start():
            pl.when(z < n_seq - 1)(up.start)
            pl.when(z > 0)(down.start)

        def wait():
            pl.when(z > 0)(up.wait_recv)
            pl.when(z < n_seq - 1)(down.wait_recv)

        def final():
            pl.when(z < n_seq - 1)(up.wait_send)
            pl.when(z > 0)(down.wait_send)

        tasks.finals.append(final)
        tasks.add(name, start)
        return wait

    wait_tags = add_halo("tags", None, ((tag_edge, tag_prev), (tag_edge, tag_next)))
    if direct:
        add_gather(tasks, GATHER_STREAMS, shards, fulls, sems)

    def edge_parts(ext):
        return (
            (ext.at[:, pl.ds(span, HALF), :], ext.at[:, pl.ds(0, HALF), :]),
            (ext.at[:, pl.ds(HALF, HALF), :], ext.at[:, pl.ds(span + HALF, HALF), :]),
        )

    def prepare():
        for k in range(8):
            place_at = (k // 2) + 4 * jnp.where(c == k % 2, 0, 1)
            flipped[tile(place_at, 128), :] = cotangent[:, k * 128 : (k + 1) * 128].T
        for ext in (keys, values):
            @pl.when(z == 0)
            def _():
                ext[:, 0:HALF, :] = jnp.zeros((rows, HALF, 1024), jnp.bfloat16)

            @pl.when(z == n_seq - 1)
            def _():
                ext[:, span + HALF :, :] = jnp.zeros((rows, HALF, 1024), jnp.bfloat16)

        @pl.when(z == 0)
        def _():
            tag_prev[...] = jnp.zeros_like(tag_prev)

        @pl.when(z == n_seq - 1)
        def _():
            tag_next[...] = jnp.zeros_like(tag_next)

    def gain_rows():
        columns = weight_tile(fulls["g"], slice(None)).astype(jnp.float32)
        gains[...] = columns.T[:8]
        save("gains")

    def first_norm():
        norm_rows(tokens, gains[0:1, :], normed)
        save("normed")

    def project(first, count, put, done=None):
        def run():
            @pl.loop(first, first + count)
            def _(j):
                out = dot(normed[...], weight_tile(fulls["q"], tile(j, 256)))
                put(j, out)

            if done:
                save(done)

        return run

    def put_query(j, out):
        for half in range(2):
            for r in range(rows):
                u = out[r * span : (r + 1) * span, half * 128 : (half + 1) * 128]
                turned = rotate(u, cosine[...], sine[...]) * HDIM**-0.5
                queries[r * span : (r + 1) * span, tile(2 * j + half, 128)] = turned.astype(jnp.bfloat16)

    def put_key(j, out):
        for half in range(2):
            for r in range(rows):
                u = out[r * span : (r + 1) * span, half * 128 : (half + 1) * 128]
                turned = rotate(u, cosine[...], sine[...]).astype(jnp.bfloat16)
                keys[r, HALF : HALF + span, tile(2 * (j - 4) + half, 128)] = turned

    def put_value(j, out):
        for r in range(rows):
            values[r, HALF : HALF + span, tile(j - 8, 256)] = out[r * span : (r + 1) * span].astype(jnp.bfloat16)

    tasks.add("prep", prepare)
    tasks.add("gain", gain_rows)
    tasks.add("norm", first_norm)
    tasks.add("q", project(0, 4, put_query))
    tasks.add("k0", project(4, 2, put_key))
    tasks.add("k1", project(6, 2, put_key))
    wait_keys = add_halo("hk", None, edge_parts(keys))
    tasks.add("v", project(8, 4, put_value, "q"))
    wait_values = add_halo("hv", None, edge_parts(values))

    def wait_halo():
        wait_tags()
        wait_keys()
        wait_values()

    tasks.add("hw", wait_halo)

    def masks():
        first = lax.broadcasted_iota(jnp.int32, (8, 128), 1) < HALF
        zero = jnp.zeros((8, 128), jnp.float32)
        low = jnp.where(first, tag_prev[...], zero) + tag_center[:, 0:128]
        high = jnp.where(first, zero, tag_next[...]) + tag_center[:, 256:384]
        ext = jnp.concatenate([low, tag_center[:, 128:256], high], 1)
        offset = lax.broadcasted_iota(jnp.int32, (128, 256), 1) - lax.broadcasted_iota(jnp.int32, (128, 256), 0)
        band, self_pair = (offset >= 0) & (offset <= 2 * HALF), offset == HALF
        for r in range(rows):
            for k in range(2):
                key_tag = ext[r : r + 1, k * 128 : k * 128 + 256]
                same = key_tag == query_tag[r * span + k * 128 : r * span + (k + 1) * 128, :]
                bias[r, k] = jnp.where(band & (same | self_pair), 0.0, MASK_FILL)
        save("queries")
        save("keys")
        save("values")

    tasks.add("bias", masks)

    def attend(r, k, first):
        def run():
            row, window = slice(r * span + k * 128, r * span + (k + 1) * 128), slice(k * 128, k * 128 + 256)

            @pl.loop(first, first + 4)
            def _(p):
                cols = tile(p, 128)
                scores = dot_rows(queries[row, cols], pair_rows(keys[r, window, cols]))
                parts = []
                for h in range(2):
                    s = scores[:, h * 256 : (h + 1) * 256] + bias[r, k]
                    weights = jnp.exp(s - jnp.max(s, -1, keepdims=True))
                    parts.append((weights * (1.0 / jnp.sum(weights, -1, keepdims=True))).astype(jnp.bfloat16))
                pair = jnp.concatenate(parts, 1)
                probs[r, k, p] = pair
                attended[row, cols] = dot(pair, pair_rows(values[r, window, cols])).astype(jnp.bfloat16)

        return run

    for i in range(8):
        tasks.add(f"att{i}", attend(i // 4, (i // 2) % 2, 4 * (i % 2)))

    def project_out():
        @pl.loop(0, 4)
        def _(j):
            cols = tile(j, 256)
            middle[:, cols] = tokens[:, cols].astype(jnp.float32) + dot(attended[...], weight_tile(fulls["o"], cols))

        for name in ("o", "probs", "attended", "middle"):
            save(name)

    def second_norm():
        norm_rows(middle, gains[1:2, :], second)
        save("second")

    tasks.add("out", project_out)
    tasks.add("norm2", second_norm)

    def gated(first):
        def run():
            @pl.loop(first, first + 3)
            def _(j):
                out = dot(second[...], weight_tile(fulls["w"], tile(j, 256)))
                gate_in, gate_up = out[:, :128], out[:, 128:]
                mass = 0.5 * (1.0 + lax.erf(gate_in * 0.5**0.5))
                density = jnp.exp(-0.5 * gate_in * gate_in) * INV_SQRT_2PI
                gelu = gate_in * mass
                slope = gate_up * (mass + gate_in * density)
                slopes[:, tile(j, 256)] = jnp.concatenate([slope, gelu], 1).astype(jnp.bfloat16)
                active[:, tile(j, 128)] = (gelu * gate_up).astype(jnp.bfloat16)

            if first == 18:
                for name in ("w", "slopes", "active"):
                    save(name)

        return run

    for i in range(7):
        tasks.add(f"w{i}", gated(3 * i))

    def grad_narrow(first, count):
        def run():
            def part(cols):
                out = dot(flipped[...], active[:, cols]).astype(jnp.bfloat16)
                own[:, cols], other[:, cols] = out[:512], out[512:]

            pl.loop(first, first + count)(lambda j: part(tile(j, 256)))
            if first + count == 10:
                part(pl.ds(2560, 128))
                save("own")
                save("other")

        return run

    for i, (first, count) in enumerate(((0, 3), (3, 3), (6, 2), (8, 2))):
        tasks.add(f"gn{i}", grad_narrow(first, count))

    if direct:
        local = [
            pltpu.make_async_copy(shards[n], fulls[n].at[y, x, c, piece(z), :], local_sems.at[17 + i])
            for i, n in enumerate(names)
        ]
    else:
        local = [pltpu.make_async_copy(shards[n], fulls[n], local_sems.at[17 + i]) for i, n in enumerate(names)]
    for copy in local:
        copy.start()
    enter(direct, n_seq)
    for copy in local:
        copy.wait()
    FORWARD_NAMES[:] = tasks.names
    tasks.run(FORWARD_ORDER if direct else range(len(tasks.steps)))
    save("n")
    for copy in copies.values():
        copy.wait()


FORWARD_NAMES = []


def forward(direct, n_seq, shards, tokens, cotangent, cosine, sine, tag_center, tag_edge, query_tag):
    bf, f32 = jnp.bfloat16, jnp.float32
    shapes = {
        "q": ((2, 2, 2, 128, 3072), bf),
        "o": ((2, 2, 2, 128, 1024), bf),
        "w": ((2, 2, 2, 128, 2 * PADDED), bf),
        "n": ((2, 2, 2, 128, PADDED), bf),
        "normed": ((512, 1024), bf),
        "queries": ((512, 1024), bf),
        "keys": ((2, 384, 1024), bf),
        "values": ((2, 384, 1024), bf),
        "probs": ((2, 2, 8, 128, 512), bf),
        "attended": ((512, 1024), bf),
        "middle": ((512, 1024), f32),
        "second": ((512, 1024), bf),
        "slopes": ((512, 2 * PADDED), bf),
        "active": ((512, PADDED), bf),
        "own": ((512, PADDED), bf),
        "other": ((512, PADDED), bf),
        "gains": ((8, 1024), f32),
    }
    vmem, anywhere = pl.BlockSpec(memory_space=pltpu.VMEM), pl.BlockSpec(memory_space=pl.ANY)
    full = [pltpu.VMEM((2, 2, 2, 128, 128), bf)] + [pltpu.VMEM(*shapes[n]) for n in ("q", "o", "w", "n")]
    rest = [pltpu.VMEM(*s) for n, s in shapes.items() if n not in ("q", "o", "w", "n")]
    out = pl.pallas_call(
        functools.partial(forward_kernel, direct, n_seq),
        out_shape=tuple(jax.ShapeDtypeStruct(*s) for s in shapes.values()),
        in_specs=[vmem if direct else anywhere] * 5 + [vmem] * 7,
        out_specs=(anywhere,) * len(shapes),
        scratch_shapes=full
        + rest
        + [
            pltpu.VMEM((1024, 512), bf),
            pltpu.VMEM((2, 2, 128, 256), f32),
            pltpu.VMEM((8, 128), f32),
            pltpu.VMEM((8, 128), f32),
            pltpu.SemaphoreType.DMA((400 if direct else 16,)),
            pltpu.SemaphoreType.DMA((400 if direct else 16,)),
            pltpu.SemaphoreType.DMA((24,)),
        ],
        compiler_params=pltpu.CompilerParams(collective_id=1, has_side_effects=True, vmem_limit_bytes=62 << 20),
    )(*shards, tokens, cotangent, cosine, sine, tag_center, tag_edge, query_tag)
    return dict(zip(shapes, out))


class Counter:
    def __init__(self): self.n=0
    def take(self,k=1):
        r=self.n; self.n+=k; return r

def add_into(dst, a, b, rows, width):
    def body(r):
        s=pl.ds(pl.multiple_of(r*16,16),16)
        dst[s,:]=a[s,:]+b[s,:]
    if rows<=32:
        for r in range(rows//16): body(r)
    else:
        pl.loop(0,rows//16)(body)

def scatter_steps(streams, grads, acc, bufs, outs, ssem, rsem, ctr):
    b,z,y,x,c=place()
    out=[]; finals=[]
    def rdma(src,dst,i,dev):
        return pltpu.make_async_remote_copy(src,dst,ssem.at[i],rsem.at[i],device_id=dev,device_id_type=MESH)
    def one(j,order,name,c0,cn):
        G=grads[name]; A=acc[name]; cols=pl.ds(c0,cn); B=bufs[j]; O=outs[name]
        steps=[]
        i=ctr.take(); dev=(b^1,z)
        cp=rdma(G.at[:,:,1-c,:,cols],B['c'],i,dev)
        steps.append(cp.start); finals.append(cp.wait_send)
        def pending(cp=cp):
            cp.wait_recv()
            for yy in range(2):
                for xx in range(2):
                    add_into(A.at[yy,xx,:,cols],A.at[yy,xx,:,cols],B['c'].at[yy,xx],128,cn)
        whole={'x','y','z'}
        def idx(fix, zz=None):
            return A.at[fix.get('y',slice(None)),fix.get('x',slice(None)),(pl.ds(pl.multiple_of(zz*32,32),32) if zz is not None else fix.get('z',slice(None))),cols]
        fix={}
        rev=order[::-1]
        for n,d in enumerate(rev):
            last=n==2
            if d in 'xy':
                i=ctr.take(); mine=y if d=='y' else x
                dev=(b^(2 if d=='x' else 4), z)
                f_other=dict(fix); f_other[d]=1-mine
                f_own=dict(fix); f_own[d]=mine
                cp=rdma(idx(f_other),B[d],i,dev)
                def fn(pending=pending,cp=cp):
                    pending(); cp.start()
                steps.append(fn); finals.append(cp.wait_send)
                def pending(cp=cp,f_own=f_own,d=d,last=last):
                    cp.wait_recv()
                    dst=idx(f_own)
                    if last:
                        O[:,cols]=dst[...].astype(jnp.float32)+B[d][...].astype(jnp.float32)
                    elif len(dst.shape)==2: add_into(dst,dst,B[d],dst.shape[0],cn)
                    else:
                        for q in range(2): add_into(dst.at[q],dst.at[q],B[d].at[q],dst.shape[1],cn)
                fix=f_own
            else:
                lead=[q for q in 'yx' if q not in fix]
                def acc_add(t,buf,fix=fix,lead=lead):
                    dst=idx(fix,t); s=pl.ds(pl.multiple_of(t*32,32),32)
                    if not lead: add_into(dst,dst,buf.at[s],32,cn)
                    elif len(lead)==2:
                        for yy in range(2):
                            for xx in range(2): add_into(dst.at[yy,xx],dst.at[yy,xx],buf.at[yy,xx,s],32,cn)
                    else:
                        for q in range(2): add_into(dst.at[q],dst.at[q],buf.at[q,s],32,cn)
                def bat(buf,t,lead=lead):
                    return buf.at[tuple([slice(None)]*len(lead))+(pl.ds(pl.multiple_of(t*32,32),32),)]
                prev=None
                for h in (2,1,0):
                    i=ctr.take(2)
                    td=jnp.maximum(z-1-h,0); tu=jnp.minimum(z+1+h,3)
                    cd=z-1-h>=0; cu=z+1+h<=3
                    dn=rdma(idx(fix,td),bat(B['d'],td),i,(b,jnp.maximum(z-1,0)))
                    up=rdma(idx(fix,tu),bat(B['u'],tu),i+1,(b,jnp.minimum(z+1,3)))
                    rd=jnp.logical_and(z<3, z-h>=0); ru=jnp.logical_and(z>0, z+h<=3)
                    rtd=jnp.maximum(z-h,0); rtu=jnp.minimum(z+h,3)
                    wd=rdma(idx(fix,rtd),bat(B['d'],rtd),i,(b,jnp.maximum(z-1,0)))
                    wu=rdma(idx(fix,rtu),bat(B['u'],rtu),i+1,(b,jnp.minimum(z+1,3)))
                    def fn(pending=pending,up=up,dn=dn,cu=cu,cd=cd):
                        pending()
                        pl.when(cd)(dn.start); pl.when(cu)(up.start)
                    steps.append(fn)
                    def fin(up=up,dn=dn,cu=cu,cd=cd):
                        pl.when(cd)(dn.wait_send); pl.when(cu)(up.wait_send)
                    finals.append(fin)
                    def pending(wd=wd,wu=wu,rd=rd,ru=ru,rtd=rtd,rtu=rtu,acc_add=acc_add):
                        @pl.when(rd)
                        def _():
                            wd.wait_recv(); acc_add(rtd,B['d'])
                        @pl.when(ru)
                        def _():
                            wu.wait_recv(); acc_add(rtu,B['u'])
                fix=dict(fix); fix['z']=pl.ds(pl.multiple_of(z*32,32),32)
                if last:
                    def pending(pending=pending,fix=fix):
                        pending()
                        O[:,cols]=idx(fix)[...].astype(jnp.float32)
        steps.append(pending)
        out.append(steps)
    for j,s in enumerate(streams): one(j,*s)
    return out, finals

def landing(streams):
    res=[]
    for (order,name,c0,cn) in streams:
        d={'c':(2,2,128,cn)}
        have={'x':2,'y':2}; zr=128
        for q in order[::-1]:
            if q in 'xy':
                del have[q]
                d[q]=tuple(have.values())+(zr,cn)
            else:
                d['d']=tuple(have.values())+(128,cn); d['u']=d['d']; zr=32
        res.append(d)
    return res


WIDTHS = {"q": 3072, "g": 128, "o": 1024, "w": 2 * PADDED, "n": PADDED}
NAMES = tuple(WIDTHS)


def scatter_kernel(shapes, *refs):
    count = len(NAMES)
    grads = dict(zip(NAMES, refs[:count]))
    outs = dict(zip(NAMES, refs[count : 2 * count]))
    acc = dict(zip(NAMES, refs[2 * count : 3 * count]))
    rest = list(refs[3 * count :])
    bufs = []
    for s in shapes:
        bufs.append(dict(zip(s, rest[: len(s)])))
        rest = rest[len(s) :]
    ssem, rsem, lsem = rest
    b, z, y, x, c = place()
    local = [
        pltpu.make_async_copy(grads[n].at[:, :, c], acc[n], lsem.at[i]) for i, n in enumerate(NAMES)
    ]
    for copy in local:
        copy.start()
    enter(True, 4)
    steps, finals = scatter_steps(SCATTER_STREAMS, grads, acc, bufs, outs, ssem, rsem, Counter())
    flat = [f for s in steps for f in s]
    for copy in local:
        copy.wait()
    for i in SCATTER_ORDER:
        flat[i]()
    for f in finals:
        f()


def scatter_grads(*grads):
    shapes = landing(SCATTER_STREAMS)
    grads = [g.reshape(2, 2, 2, 128, g.shape[-1]) for g in grads]
    return pl.pallas_call(
        functools.partial(scatter_kernel, shapes),
        out_shape=tuple(jax.ShapeDtypeStruct((32, WIDTHS[n]), jnp.float32) for n in NAMES),
        in_specs=[pl.BlockSpec(memory_space=pl.ANY)] * len(NAMES),
        out_specs=tuple(pl.BlockSpec(memory_space=pltpu.VMEM) for n in NAMES),
        scratch_shapes=[pltpu.VMEM((2, 2, 128, WIDTHS[n]), jnp.bfloat16) for n in NAMES]
        + [pltpu.VMEM(v, jnp.bfloat16) for s in shapes for v in s.values()]
        + [
            pltpu.SemaphoreType.DMA((500,)),
            pltpu.SemaphoreType.DMA((500,)),
            pltpu.SemaphoreType.DMA((8,)),
        ],
        compiler_params=pltpu.CompilerParams(
            collective_id=2, has_side_effects=True, vmem_limit_bytes=60 << 20
        ),
    )(*grads)


def with_halo(array, sides, width):
    for axis, dim in sides:
        size, length = (lax.axis_size(axis), array.shape[dim])
        up = [(i, (i + 1) % size) for i in range(size - 1)]
        down = [(j, i) for i, j in up]
        last = lax.slice_in_dim(array, length - width, length, axis=dim)
        first = lax.slice_in_dim(array, 0, width, axis=dim)
        before = lax.ppermute(last, axis, up)
        after = lax.ppermute(first, axis, down)
        array = jnp.concatenate([before, array, after], axis=dim)
    return array


def norm_backward(upstream, unit, inverse, gain):
    scaled = upstream * gain
    grad_gain = jnp.sum(upstream * unit, 0)
    grad = inverse * (
        scaled - jnp.mean(scaled, -1, keepdims=True) - unit * jnp.mean(scaled * unit, -1, keepdims=True)
    )
    return grad, grad_gain


def attend_back_kernel(queries, keys, values, probs, grads, grad_q, grad_k, grad_v):
    for r in range(2):
        for k in range(2):
            row, window = slice(r * 256 + k * 128, r * 256 + (k + 1) * 128), slice(k * 128, k * 128 + 256)

            @pl.loop(0, 8)
            def _(p, r=r, k=k, row=row, window=window):
                cols = tile(p, 128)
                first = lanes(256) < HDIM
                upstream, pair = grads[row, cols], probs[r, k, p]
                key_pair = pair_rows(keys[r, window, cols])
                grad_p = dot_rows(upstream, pair_rows(values[r, window, cols]))
                parts = []
                for h in range(2):
                    span = slice(h * 256, (h + 1) * 256)
                    weights = pair[:, span].astype(jnp.float32)
                    inner = jnp.sum(grad_p[:, span] * weights, -1, keepdims=True)
                    parts.append((weights * (grad_p[:, span] - inner)).astype(jnp.bfloat16))
                grad_s = jnp.concatenate(parts, 1)
                grad_q[row, cols] = dot(grad_s, key_pair) * HDIM**-0.5
                back_v = dot_columns(pair, upstream)
                back_k = dot_columns(grad_s, queries[row, cols])
                back_v = jnp.where(first, back_v[:256], back_v[256:])
                back_k = jnp.where(first, back_k[:256], back_k[256:])
                if k == 0:
                    grad_k[r, window, cols], grad_v[r, window, cols] = back_k, back_v
                else:
                    for out, back in ((grad_k, back_k), (grad_v, back_v)):
                        out[r, 128:256, cols] += back[:128]
                        out[r, 256:384, cols] = back[128:]


def attend_back(*args):
    vmem, f32 = pl.BlockSpec(memory_space=pltpu.VMEM), jnp.float32
    return pl.pallas_call(
        attend_back_kernel,
        out_shape=(
            jax.ShapeDtypeStruct((512, 1024), f32),
            jax.ShapeDtypeStruct((2, 384, 1024), f32),
            jax.ShapeDtypeStruct((2, 384, 1024), f32),
        ),
        in_specs=[vmem] * 5,
        out_specs=(vmem,) * 3,
        compiler_params=pltpu.CompilerParams(vmem_limit_bytes=50 << 20),
    )(*args)


def tables(span):
    frequency = ROPE_BASE ** (-(2.0 * jnp.arange(HDIM // 2, dtype=jnp.float32)) / HDIM)
    positions = (lax.axis_index("seq") * span + jnp.arange(span, dtype=jnp.int32)).astype(jnp.float32)
    angles = positions[:, None] * frequency[None, :]
    cosine, sine = jnp.cos(angles), jnp.sin(angles)
    return jnp.concatenate([cosine] * 4, 1), jnp.concatenate([-sine, sine, -sine, sine], 1)


def interleave(wide):
    lead = wide.shape[0]
    wide = jnp.pad(wide.reshape(lead, 2, FF), ((0, 0), (0, 0), (0, PADDED - FF)))
    return wide.reshape(lead, 2, PADDED // 128, 128).swapaxes(1, 2).reshape(lead, 2 * PADDED)


def separate(wide):
    lead = wide.shape[0]
    wide = wide.reshape(lead, PADDED // 128, 2, 128).swapaxes(1, 2).reshape(lead, 2, PADDED)
    return wide[:, :, :FF].reshape(lead, 2 * FF)


def body(
    tokens,
    segment_ids,
    padding_mask,
    qkv_weight,
    out_weight,
    wide_weight,
    narrow_weight,
    first_gain,
    second_gain,
    cotangent,
):
    row_count, span, width = tokens.shape
    count = row_count * span
    n_seq = lax.axis_size("seq")
    direct = (lax.axis_size("batch"), n_seq) == (8, 4)
    gains = jnp.stack([first_gain, second_gain], axis=1)
    shards = (
        jnp.pad(gains, ((0, 0), (0, 126))),
        qkv_weight,
        out_weight,
        interleave(wide_weight),
        jnp.pad(narrow_weight, ((0, 0), (0, PADDED - FF))),
    )
    if not direct:
        shards = [
            lax.all_gather(s, ("batch", "seq"), axis=0, tiled=True).reshape(2, 2, 2, 128, s.shape[-1]) for s in shards
        ]
    tags = jnp.where(padding_mask == 1, segment_ids + 1, 0).astype(jnp.float32)
    tag_center = jnp.pad(tags, ((0, 8 - row_count), (HALF, HALF)))
    tag_edge = jnp.pad(
        jnp.concatenate([tags[:, span - HALF :], tags[:, :HALF]], 1), ((0, 8 - row_count), (0, 0))
    )
    query_tag = (segment_ids + 1).astype(jnp.float32).reshape(count, 1)
    cosine, sine = tables(span)
    hidden = tokens.reshape(count, width)
    cot_low = cotangent.reshape(count, width)
    saved = forward(direct, n_seq, shards, hidden, cot_low, cosine, sine, tag_center, tag_edge, query_tag)
    qkv_full, out_full, wide_full, narrow_full = (saved[n].reshape(1024, -1) for n in ("q", "o", "w", "n"))
    gain_one, gain_two = saved["gains"][0:1], saved["gains"][1:2]
    hidden = hidden.astype(jnp.float32)
    middle, attended = saved["middle"], saved["attended"]
    result = middle + jnp.einsum("nf,df->nd", saved["active"], narrow_full, preferred_element_type=jnp.float32)
    outputs = result.astype(jnp.bfloat16).reshape(tokens.shape)
    grad_act = jnp.dot(cot_low, narrow_full, preferred_element_type=jnp.float32)
    slopes = saved["slopes"].astype(jnp.float32).reshape(count, PADDED // 128, 2, 128)
    grad_expanded = slopes * grad_act.reshape(count, PADDED // 128, 1, 128)
    grad_expanded = grad_expanded.astype(jnp.bfloat16).reshape(count, 2 * PADDED)
    grad_wide = jnp.einsum("nd,nf->df", saved["second"], grad_expanded, preferred_element_type=jnp.float32)
    grad_second = jnp.einsum("nf,df->nd", grad_expanded, wide_full, preferred_element_type=jnp.float32)
    unit_two, inv_two = norm_parts(middle)
    grad_mid_norm, grad_gain_two = norm_backward(grad_second, unit_two, inv_two, gain_two)
    grad_middle = cot_low.astype(jnp.float32) + grad_mid_norm
    grad_branch = grad_middle.astype(jnp.bfloat16)
    grad_out = jnp.einsum("nd,ne->de", attended, grad_branch, preferred_element_type=jnp.float32)
    grad_attended = jnp.einsum("ne,de->nd", grad_branch, out_full, preferred_element_type=jnp.float32).astype(
        jnp.bfloat16
    )
    grad_q, grad_k, grad_v = attend_back(
        saved["queries"], saved["keys"], saved["values"], saved["probs"], grad_attended
    )
    stack = jnp.stack([grad_k, grad_v])
    extent = span + 2 * HALF
    outgoing = jnp.concatenate([stack[:, :, :HALF], stack[:, :, extent - HALF :]], axis=2)
    incoming = with_halo(outgoing.astype(jnp.bfloat16), (("seq", 2),), HALF).astype(outgoing.dtype)
    owned = stack[:, :, HALF : HALF + span]
    owned = jnp.concatenate(
        [
            owned[:, :, :HALF] + incoming[:, :, :HALF],
            owned[:, :, HALF : span - HALF],
            owned[:, :, span - HALF :] + incoming[:, :, 3 * HALF :],
        ],
        axis=2,
    )

    def turn_back(u):
        u = u.reshape(row_count, span, width // HDIM, 2, HDIM // 2)
        co = cosine[:, : HDIM // 2][None, :, None, :]
        si = sine[:, HDIM // 2 : HDIM][None, :, None, :]
        a, b = u[..., 0, :], u[..., 1, :]
        return jnp.stack([a * co + b * si, b * co - a * si], 3).reshape(count, width)

    grad_projected = jnp.concatenate(
        [turn_back(grad_q), turn_back(owned[0]), owned[1].reshape(count, width)], 1
    ).astype(jnp.bfloat16)
    grad_qkv = jnp.einsum("nd,ne->de", saved["normed"], grad_projected, preferred_element_type=jnp.float32)
    grad_normed = jnp.einsum("ne,de->nd", grad_projected, qkv_full, preferred_element_type=jnp.float32)
    unit_one, inv_one = norm_parts(hidden)
    grad_in_norm, grad_gain_one = norm_backward(grad_normed, unit_one, inv_one, gain_one)
    grad_tokens = (grad_middle + grad_in_norm).astype(jnp.bfloat16).reshape(tokens.shape)
    grad_gains = jnp.pad(jnp.stack([grad_gain_one, grad_gain_two], axis=1), ((0, 0), (0, 126)))
    low = [g.astype(jnp.bfloat16) for g in (grad_qkv, grad_gains, grad_out, grad_wide)]
    mine = (lax.axis_index("batch") % 2 if direct else 0) == 0
    own, other = (saved[n].reshape(4, 128, PADDED) for n in ("own", "other"))
    grad_narrow = jnp.stack([jnp.where(mine, own, other), jnp.where(mine, other, own)], 1).reshape(1024, PADDED)
    grads = low + [grad_narrow]
    if direct:
        sums = scatter_grads(*grads)
    else:
        sums = [
            lax.psum_scatter(g, ("batch", "seq"), scatter_dimension=0, tiled=True).astype(jnp.float32) for g in grads
        ]
    sum_qkv, sum_gains, sum_out, sum_wide, sum_narrow = sums
    return (
        outputs,
        grad_tokens,
        sum_qkv,
        sum_out,
        separate(sum_wide),
        sum_narrow[:, :FF],
        sum_gains[:, 0],
        sum_gains[:, 1],
    )


def solution(mesh):
    placed = (
        P("batch", "seq", None),
        P("batch", "seq"),
        P("batch", "seq"),
        P(("batch", "seq"), None),
        P(("batch", "seq"), None),
        P(("batch", "seq"), None),
        P(("batch", "seq"), None),
        P(("batch", "seq")),
        P(("batch", "seq")),
        P("batch", "seq", None),
    )
    return jax.shard_map(
        body,
        mesh=mesh,
        in_specs=placed,
        out_specs=(
            P("batch", "seq", None),
            P("batch", "seq", None),
            P(("batch", "seq"), None),
            P(("batch", "seq"), None),
            P(("batch", "seq"), None),
            P(("batch", "seq"), None),
            P(("batch", "seq")),
            P(("batch", "seq")),
        ),
        check_vma=False,
    )
```

```python
import functools
from typing import Any, NamedTuple

import jax
import jax.numpy as jnp
from jax import lax
from jax.experimental import pallas as pl
from jax.experimental.pallas import tpu as pltpu
from jax.sharding import PartitionSpec as P

MESH = pl.DeviceIdType.MESH
HDIM = 64
FF = 2624
PADDED = 2688
HALF = 64
BATCH, SEQ = "batch", "seq"
ORDERS = ("zxy", "zyx", "xyz", "yxz")
FULL = ("g", "q", "o", "w", "n")
NORM_EPS = 1e-05
MASK_FILL = -1e30
ROPE_BASE = 10000.0
INV_SQRT_2PI = 0.3989422804014327

GATHER_STREAMS = (
    (0, 0, 0, 128),
    (0, 1, 0, 512),
    (1, 1, 512, 512),
    (0, 1, 1024, 512),
    (1, 1, 1536, 512),
    (0, 1, 2048, 512),
    (1, 1, 2560, 512),
    (0, 2, 0, 512),
    (1, 2, 512, 512),
    (0, 4, 0, 640),
    (1, 4, 640, 640),
    (2, 4, 1280, 128),
    (3, 4, 1408, 128),
    (0, 4, 1536, 512),
    (1, 4, 2048, 512),
    (3, 4, 2560, 128),
    (0, 3, 0, 640),
    (1, 3, 640, 640),
    (2, 3, 1280, 128),
    (3, 3, 1408, 128),
    (0, 3, 1536, 640),
    (1, 3, 2176, 640),
    (2, 3, 2816, 128),
    (3, 3, 2944, 128),
    (0, 3, 3072, 640),
    (1, 3, 3712, 640),
    (2, 3, 4352, 128),
    (3, 3, 4480, 128),
    (0, 3, 4608, 384),
    (1, 3, 4992, 384),
)
FORWARD_ORDER = (
    0, 1, 8, 15, 22, 29, 78, 85, 36, 106, 127, 43, 134, 211, 2, 155, 162, 183, 190, 9, 79, 86, 16,
    107, 128, 135, 23, 30, 50, 37, 156, 163, 57, 3, 184, 44, 64, 71, 10, 17, 191, 24, 4, 31, 38, 45,
    11, 5, 80, 92, 18, 99, 87, 25, 6, 32, 51, 113, 120, 58, 12, 7, 65, 212, 39, 19, 72, 213, 108,
    26, 52, 59, 33, 81, 46, 66, 73, 129, 88, 13, 93, 141, 148, 53, 40, 20, 14, 100, 136, 67, 82, 21,
    214, 60, 89, 157, 27, 83, 169, 176, 94, 34, 109, 90, 114, 164, 101, 47, 74, 28, 215, 121, 84,
    197, 204, 54, 35, 216, 91, 185, 95, 110, 41, 217, 115, 192, 61, 68, 42, 48, 130, 102, 49, 218,
    111, 55, 122, 116, 112, 219, 75, 96, 137, 62, 56, 142, 149, 63, 158, 220, 221, 222, 69, 131,
    123, 117, 103, 165, 223, 138, 76, 132, 170, 143, 177, 150, 70, 139, 224, 133, 159, 97, 144, 225,
    140, 77, 186, 104, 151, 124, 166, 160, 98, 226, 193, 171, 105, 167, 198, 145, 161, 205, 227,
    178, 168, 118, 172, 228, 187, 152, 125, 229, 194, 179, 188, 119, 230, 126, 195, 199, 206, 173,
    189, 231, 146, 200, 196, 232, 233, 207, 153, 180, 147, 234, 201, 235, 236, 154, 237, 238, 174,
    239, 240, 208, 181, 241, 175, 202, 242, 182, 243, 244, 245, 209, 203, 246, 247, 248, 210, 249,
    250, 251, 252, 253, 254, 255, 256, 257, 258, 259, 260,
)
SCATTER_CHUNKS = (
    (4, 0, 1536),
    (4, 1536, 1152),
    (3, 0, 1536),
    (3, 1536, 1536),
    (3, 3072, 1536),
    (3, 4608, 768),
    (2, 0, 1024),
    (1, 0, 1024),
    (1, 1024, 1024),
    (1, 2048, 1024),
)
SCATTER_STREAMS = (
    (0, 4, 0, 768),
    (1, 4, 768, 768),
    (0, 4, 1536, 512),
    (1, 4, 2048, 512),
    (3, 4, 2560, 128),
    (0, 3, 0, 768),
    (1, 3, 768, 768),
    (0, 3, 1536, 768),
    (1, 3, 2304, 768),
    (0, 3, 3072, 768),
    (1, 3, 3840, 768),
    (0, 3, 4608, 384),
    (1, 3, 4992, 384),
    (0, 2, 0, 512),
    (1, 2, 512, 512),
    (0, 1, 0, 512),
    (1, 1, 512, 512),
    (0, 1, 1024, 512),
    (1, 1, 1536, 512),
    (0, 1, 2048, 512),
    (1, 1, 2560, 512),
)
BACKWARD_ORDER = (
    31, 33, 0, 1, 2, 3, 32, 51, 57, 35, 4, 34, 63, 69, 75, 37, 5, 76, 6, 36, 81, 87, 77, 39, 7, 38,
    41, 8, 40, 52, 58, 42, 10, 64, 70, 11, 78, 93, 99, 12, 13, 14, 53, 59, 15, 82, 88, 54, 65, 71,
    79, 16, 60, 55, 105, 111, 20, 17, 61, 66, 72, 18, 80, 19, 56, 83, 89, 67, 94, 73, 100, 9, 117,
    123, 43, 24, 84, 90, 45, 22, 85, 21, 62, 106, 112, 91, 44, 68, 74, 95, 101, 129, 135, 46, 23,
    102, 96, 86, 103, 25, 97, 118, 124, 92, 141, 147, 47, 26, 107, 104, 113, 49, 108, 27, 114, 48,
    98, 109, 115, 153, 159, 28, 130, 119, 125, 136, 50, 110, 120, 29, 126, 116, 121, 142, 127, 148,
    30, 165, 171, 122, 131, 137, 128, 154, 160, 138, 132, 149, 139, 143, 133, 150, 144, 151, 145,
    140, 134, 166, 172, 161, 152, 155, 146, 162, 156, 173, 163, 167, 157, 174, 168, 175, 169, 164,
    158, 176, 170,
)


def place():
    b = lax.axis_index(BATCH)
    z = lax.axis_index(SEQ)
    return b, z, b // 4, (b // 2) % 2, b % 2


def remote(src, dst, sems, i, device):
    return pltpu.make_async_remote_copy(
        src_ref=src,
        dst_ref=dst,
        send_sem=sems[0].at[i],
        recv_sem=sems[1].at[i],
        device_id=device,
        device_id_type=MESH,
    )


def piece(t, n=32):
    return pl.ds(pl.multiple_of(t * n, n), n)


def enter(direct, n_seq):
    barrier = pltpu.get_barrier_semaphore()
    b, z = lax.axis_index(BATCH), lax.axis_index(SEQ)

    def greet(device):
        pl.semaphore_signal(barrier, inc=1, device_id=device, device_id_type=MESH)

    if direct:
        for bit in (1, 2, 4):
            greet((b ^ bit, z))
    pl.when(z < n_seq - 1)(lambda: greet((b, z + 1)))
    pl.when(z > 0)(lambda: greet((b, z - 1)))
    near = (z < n_seq - 1).astype(jnp.int32) + (z > 0).astype(jnp.int32)
    pl.semaphore_wait(barrier, near + (3 if direct else 0))


class Tasks:
    def __init__(self):
        self.steps, self.finals, self.semaphores = [], [], 0

    def take(self, count=1):
        first = self.semaphores
        self.semaphores += count
        return first

    def add(self, step):
        self.steps.append(step)

    def run(self, order):
        for i in order:
            self.steps[i]()
        for final in self.finals:
            final()


def add_gather(tasks, streams, shards, fulls, sems):
    b, z, y, x, c = place()

    def one(j, order, name, first, count):
        full, cols = fulls[name], pl.ds(first, count)
        whole = set()

        def view(at=None, other=None):
            yy = slice(None) if "y" in whole else (1 - y if other == "y" else y)
            xx = slice(None) if "x" in whole else (1 - x if other == "x" else x)
            zz = piece(z if at is None else at) if "z" not in whole else slice(None)
            return full.at[yy, xx, c, zz, cols]

        pending, sub = None, 0
        for axis in order:
            own = None if whole else shards[name].at[:, cols]
            if axis in "xy":
                i, device = tasks.take(), (b ^ (2 if axis == "x" else 4), z)
                out = remote(view() if own is None else own, view(), sems, i, device)
                into = remote(view(other=axis), view(other=axis), sems, i, device)

                def step(pending=pending, out=out):
                    if pending:
                        pending()
                    out.start()

                tasks.add(step)
                tasks.finals.append(out.wait_send)
                pending, sub = into.wait_recv, sub + 1
            else:
                for hop in range(3):
                    i = tasks.take(2)
                    has_up, has_down = (z >= hop) & (z < 3), (z + hop <= 3) & (z > 0)
                    up_piece, down_piece = jnp.maximum(z - hop, 0), jnp.minimum(z + hop, 3)
                    above, below = (b, jnp.minimum(z + 1, 3)), (b, jnp.maximum(z - 1, 0))
                    start = own if hop == 0 else None
                    up = remote(view(up_piece) if start is None else start, view(up_piece), sems, i, above)
                    down = remote(
                        view(down_piece) if start is None else start, view(down_piece), sems, i + 1, below
                    )
                    from_below, from_above = z - 1 - hop >= 0, z + 1 + hop <= 3
                    low, high = jnp.maximum(z - 1 - hop, 0), jnp.minimum(z + 1 + hop, 3)
                    rise = remote(view(low), view(low), sems, i, above)
                    fall = remote(view(high), view(high), sems, i + 1, below)

                    def step(pending=pending, up=up, down=down, has_up=has_up, has_down=has_down):
                        if pending:
                            pending()
                        pl.when(has_up)(up.start)
                        pl.when(has_down)(down.start)

                    def pending(rise=rise, fall=fall, from_below=from_below, from_above=from_above):
                        pl.when(from_below)(rise.wait_recv)
                        pl.when(from_above)(fall.wait_recv)

                    def final(up=up, down=down, has_up=has_up, has_down=has_down):
                        pl.when(has_up)(up.wait_send)
                        pl.when(has_down)(down.wait_send)

                    tasks.add(step)
                    tasks.finals.append(final)
                    sub += 1
            whole.add(axis)
        i, device = tasks.take(), (b ^ 1, z)
        out = remote(full.at[:, :, c, :, cols], full.at[:, :, c, :, cols], sems, i, device)
        into = remote(full.at[:, :, 1 - c, :, cols], full.at[:, :, 1 - c, :, cols], sems, i, device)

        def step(pending=pending, out=out):
            pending()
            out.start()

        tasks.add(step)
        tasks.add(into.wait_recv)
        tasks.finals.append(out.wait_send)

    for j, (order, which, first, count) in enumerate(streams):
        one(j, ORDERS[order], FULL[which], first, count)


def dot(a, b):
    return jnp.dot(a, b, preferred_element_type=jnp.float32)


def dot_rows(a, b):
    return lax.dot_general(a, b, (((1,), (1,)), ((), ())), preferred_element_type=jnp.float32)


def dot_columns(a, b):
    return lax.dot_general(a, b, (((0,), (0,)), ((), ())), preferred_element_type=jnp.float32)


def tile(j, n):
    return pl.ds(pl.multiple_of(j * n, n), n)


def norm_parts(values):
    center = values - jnp.mean(values, -1, keepdims=True)
    inverse = lax.rsqrt(jnp.mean(center * center, -1, keepdims=True) + NORM_EPS)
    return center * inverse, inverse


def norm_rows(source, gain, target, n=64):
    @pl.loop(0, source.shape[0] // n)
    def _(i):
        unit, _ = norm_parts(source[tile(i, n), :].astype(jnp.float32))
        target[tile(i, n), :] = (unit * gain).astype(jnp.bfloat16)


def lanes(n):
    return lax.broadcasted_iota(jnp.int32, (n, 128), 1)


def rotate(u, cosine, sine):
    partner = jnp.where(lanes(u.shape[0]) % HDIM < HDIM // 2, pltpu.roll(u, 96, 1), pltpu.roll(u, 32, 1))
    return u * cosine + partner * sine


def pair_rows(block):
    zero, first = jnp.zeros_like(block), lanes(block.shape[0]) < HDIM
    return jnp.concatenate([jnp.where(first, block, zero), jnp.where(first, zero, block)], 0)


def weight_tile(full, cols):
    block = full[:, :, :, :, cols]
    return block.reshape(1024, block.shape[-1])


def flip(source, target, c):
    for k in range(8):
        at = (k // 2) + 4 * jnp.where(c == k % 2, 0, 1)
        target[tile(at, 128), :] = source[:, k * 128 : (k + 1) * 128].T


def edge_exchange(tasks, sems, n_seq, up_src, up_dst, down_src, down_dst):
    b, z = lax.axis_index(BATCH), lax.axis_index(SEQ)
    i = tasks.take(2)
    up = remote(up_src, up_dst, sems, i, (b, jnp.minimum(z + 1, n_seq - 1)))
    down = remote(down_src, down_dst, sems, i + 1, (b, jnp.maximum(z - 1, 0)))

    def start():
        pl.when(z < n_seq - 1)(up.start)
        pl.when(z > 0)(down.start)

    def wait():
        pl.when(z > 0)(up.wait_recv)
        pl.when(z < n_seq - 1)(down.wait_recv)

    def final():
        pl.when(z < n_seq - 1)(up.wait_send)
        pl.when(z > 0)(down.wait_send)

    tasks.finals.append(final)
    return start, wait


HELD = ("normed", "queries", "keys", "values", "probs", "attended", "middle", "gains", "flip_normed", "flip_attended")


def forward_kernel(direct, n_seq, *refs):
    refs = list(refs)

    def pop(names):
        return {n: refs.pop(0) for n in names}

    shards = pop(FULL)
    tokens, cotangent, cosine, sine, tag_center, tag_edge, query_tag = pop(range(7)).values()
    saved = Saved(*[refs.pop(0) for _ in Saved._fields])
    fulls = pop(FULL)
    held = pop(HELD)
    normed, queries, keys, values, probs, attended, middle, gains, flip_normed, flip_attended = held.values()
    second, flip_second, flip_cotangent, total, final, active, upstream, bias, tag_prev, tag_next = pop(range(10)).values()
    expanded_ring, narrow_ring, wide_ring = pop(range(3)).values()
    send_sems, recv_sems, local_sems, ring_sems = refs
    sems = (send_sems, recv_sems)
    held.update(fulls)
    b, z, y, x, c = place() if direct else (lax.axis_index(BATCH), lax.axis_index(SEQ), 0, 0, 0)
    rows, span = 2, 256
    tasks = Tasks()
    copies = {}

    def save(name):
        target = getattr(saved, name)
        copies[name] = pltpu.make_async_copy(held[name], target, local_sems.at[Saved._fields.index(name)])
        copies[name].start()

    start_tags, wait_tags = edge_exchange(tasks, sems, n_seq, tag_edge, tag_prev, tag_edge, tag_next)
    tasks.add(start_tags)
    if direct:
        add_gather(tasks, GATHER_STREAMS, shards, fulls, sems)

    def edges(ext):
        return (
            ext.at[:, pl.ds(span, HALF), :],
            ext.at[:, pl.ds(0, HALF), :],
            ext.at[:, pl.ds(HALF, HALF), :],
            ext.at[:, pl.ds(span + HALF, HALF), :],
        )

    def prepare():
        flip(cotangent, flip_cotangent, c)
        for ext in (keys, values):

            @pl.when(z == 0)
            def _():
                ext[:, 0:HALF, :] = jnp.zeros((rows, HALF, 1024), jnp.bfloat16)

            @pl.when(z == n_seq - 1)
            def _():
                ext[:, span + HALF :, :] = jnp.zeros((rows, HALF, 1024), jnp.bfloat16)

        @pl.when(z == 0)
        def _():
            tag_prev[...] = jnp.zeros_like(tag_prev)

        @pl.when(z == n_seq - 1)
        def _():
            tag_next[...] = jnp.zeros_like(tag_next)

    def gain_rows():
        columns = weight_tile(fulls["g"], slice(None)).astype(jnp.float32)
        gains[...] = columns.T[:8]
        save("gains")

    def first_norm():
        norm_rows(tokens, gains[0:1, :], normed)
        flip(normed, flip_normed, c)
        save("flip_normed")

    def project(first, count, put, done=None):
        def run():
            @pl.loop(first, first + count)
            def _(j):
                put(j, dot(normed[...], weight_tile(fulls["q"], tile(j, 256))))

            if done:
                save(done)

        return run

    def put_query(j, out):
        for half in range(2):
            for r in range(rows):
                u = out[r * span : (r + 1) * span, half * 128 : (half + 1) * 128]
                turned = rotate(u, cosine[...], sine[...]) * HDIM**-0.5
                queries[r * span : (r + 1) * span, tile(2 * j + half, 128)] = turned.astype(jnp.bfloat16)

    def put_key(j, out):
        for half in range(2):
            for r in range(rows):
                u = out[r * span : (r + 1) * span, half * 128 : (half + 1) * 128]
                turned = rotate(u, cosine[...], sine[...]).astype(jnp.bfloat16)
                keys[r, HALF : HALF + span, tile(2 * (j - 4) + half, 128)] = turned

    def put_value(j, out):
        for r in range(rows):
            values[r, HALF : HALF + span, tile(j - 8, 256)] = out[r * span : (r + 1) * span].astype(jnp.bfloat16)

    tasks.add(prepare)
    tasks.add(gain_rows)
    tasks.add(first_norm)
    tasks.add(project(0, 4, put_query))
    tasks.add(project(4, 2, put_key))
    tasks.add(project(6, 2, put_key))
    start_keys, wait_keys = edge_exchange(tasks, sems, n_seq, *edges(keys))
    tasks.add(start_keys)
    tasks.add(project(8, 4, put_value, "q"))
    start_values, wait_values = edge_exchange(tasks, sems, n_seq, *edges(values))
    tasks.add(start_values)

    def wait_halo():
        wait_tags()
        wait_keys()
        wait_values()

    tasks.add(wait_halo)

    def masks():
        first = lax.broadcasted_iota(jnp.int32, (8, 128), 1) < HALF
        zero = jnp.zeros((8, 128), jnp.float32)
        low = jnp.where(first, tag_prev[...], zero) + tag_center[:, 0:128]
        high = jnp.where(first, zero, tag_next[...]) + tag_center[:, 256:384]
        ext = jnp.concatenate([low, tag_center[:, 128:256], high], 1)
        offset = lax.broadcasted_iota(jnp.int32, (128, 256), 1) - lax.broadcasted_iota(jnp.int32, (128, 256), 0)
        band, self_pair = (offset >= 0) & (offset <= 2 * HALF), offset == HALF
        for r in range(rows):
            for k in range(2):
                key_tag = ext[r : r + 1, k * 128 : k * 128 + 256]
                same = key_tag == query_tag[r * span + k * 128 : r * span + (k + 1) * 128, :]
                bias[r, k] = jnp.where(band & (same | self_pair), 0.0, MASK_FILL)
        for name in ("queries", "keys", "values"):
            save(name)

    tasks.add(masks)

    def attend(r, k, first):
        def run():
            row, window = slice(r * span + k * 128, r * span + (k + 1) * 128), slice(k * 128, k * 128 + 256)

            @pl.loop(first, first + 4)
            def _(p):
                cols = tile(p, 128)
                scores = dot_rows(queries[row, cols], pair_rows(keys[r, window, cols]))
                parts = []
                for h in range(2):
                    s = scores[:, h * 256 : (h + 1) * 256] + bias[r, k]
                    weights = jnp.exp(s - jnp.max(s, -1, keepdims=True))
                    parts.append((weights * (1.0 / jnp.sum(weights, -1, keepdims=True))).astype(jnp.bfloat16))
                pair = jnp.concatenate(parts, 1)
                probs[r, k, p] = pair
                attended[row, cols] = dot(pair, pair_rows(values[r, window, cols])).astype(jnp.bfloat16)

        return run

    for i in range(8):
        tasks.add(attend(i // 4, (i // 2) % 2, 4 * (i % 2)))

    def project_out():
        @pl.loop(0, 4)
        def _(j):
            cols = tile(j, 256)
            middle[:, cols] = tokens[:, cols].astype(jnp.float32) + dot(attended[...], weight_tile(fulls["o"], cols))

        for name in ("o", "probs", "middle"):
            save(name)

    def second_norm():
        norm_rows(middle, gains[1:2, :], second)
        flip(second, flip_second, c)
        total[...] = middle[...]

    def flip_late():
        flip(attended, flip_attended, c)
        save("flip_attended")

    tasks.add(project_out)
    tasks.add(second_norm)
    tasks.add(flip_late)

    streams = {}

    def stream(name, i, source, target):
        streams[name, i] = pltpu.make_async_copy(source, target, ring_sems.at[name, i % 2])
        streams[name, i].start()

    def free(name, i):
        if (name, i) in streams:
            streams.pop((name, i)).wait()

    def gate(i):
        def run():
            free(0, i - 2)
            upstream[...] = dot(cotangent[...], weight_tile(fulls["n"], pl.ds(i * 384, 384)))

            @pl.loop(0, 3)
            def _(k):
                out = dot(second[...], weight_tile(fulls["w"], tile(3 * i + k, 256)))
                gate_in, gate_up = out[:, :128], out[:, 128:]
                mass = 0.5 * (1.0 + lax.erf(gate_in * 0.5**0.5))
                density = jnp.exp(-0.5 * gate_in * gate_in) * INV_SQRT_2PI
                gelu, above = gate_in * mass, upstream[:, tile(k, 128)]
                slope = gate_up * (mass + gate_in * density)
                expanded_ring[i % 2, :, tile(2 * k, 128)] = (above * slope).astype(jnp.bfloat16)
                expanded_ring[i % 2, :, tile(2 * k + 1, 128)] = (above * gelu).astype(jnp.bfloat16)
                active[i % 2, :, tile(k, 128)] = (gelu * gate_up).astype(jnp.bfloat16)

            stream(0, i, expanded_ring.at[i % 2], saved.grad_expanded.at[:, pl.ds(i * 768, 768)])

        return run

    def add_output(i):
        def run():
            @pl.loop(0, 2)
            def _(j):
                block = fulls["n"][j, :, :, :, pl.ds(i * 384, 384)].reshape(512, 384)
                total[:, tile(j, 512)] += dot_rows(active[i % 2], block)

            if i == 6:
                final[...] = total[...].astype(jnp.bfloat16)
                stream(3, 0, final, saved.outputs)

        return run

    def grad_narrow(i):
        def run():
            free(1, i - 2)

            @pl.loop(0, 2)
            def _(j):
                narrow_ring[i % 2, tile(j, 512), :] = dot(flip_cotangent[tile(j, 512), :], active[i % 2]).astype(jnp.bfloat16)

            stream(1, i, narrow_ring.at[i % 2], saved.grad_narrow.at[:, pl.ds(i * 384, 384)])

        return run

    def grad_wide(i):
        def run():
            free(2, i - 2)

            @pl.loop(0, 3)
            def _(k):
                part = tile(k, 256)
                wide_ring[i % 2, :, part] = dot(flip_second[...], expanded_ring[i % 2, :, part]).astype(jnp.bfloat16)

            stream(2, i, wide_ring.at[i % 2], saved.grad_wide.at[:, pl.ds(i * 768, 768)])
            if i == 6:
                save("w")

        return run

    for i in range(7):
        tasks.add(gate(i))
        tasks.add(add_output(i))
        tasks.add(grad_narrow(i))
        tasks.add(grad_wide(i))

    base = len(Saved._fields)
    if direct:
        local = [
            pltpu.make_async_copy(shards[n], fulls[n].at[y, x, c, piece(z), :], local_sems.at[base + i])
            for i, n in enumerate(FULL)
        ]
    else:
        local = [pltpu.make_async_copy(shards[n], fulls[n], local_sems.at[base + i]) for i, n in enumerate(FULL)]
    for copy in local:
        copy.start()
    enter(direct, n_seq)
    for copy in local:
        copy.wait()
    tasks.run(FORWARD_ORDER if direct else range(len(tasks.steps)))
    for copy in list(copies.values()) + list(streams.values()):
        copy.wait()


BF, F32 = jnp.bfloat16, jnp.float32
SHAPES = {
    "g": ((2, 2, 2, 128, 128), BF),
    "q": ((2, 2, 2, 128, 3072), BF),
    "o": ((2, 2, 2, 128, 1024), BF),
    "w": ((2, 2, 2, 128, 2 * PADDED), BF),
    "n": ((2, 2, 2, 128, PADDED), BF),
    "normed": ((512, 1024), BF),
    "queries": ((512, 1024), BF),
    "keys": ((2, 384, 1024), BF),
    "values": ((2, 384, 1024), BF),
    "probs": ((2, 2, 8, 128, 512), BF),
    "attended": ((512, 1024), BF),
    "middle": ((512, 1024), F32),
    "gains": ((8, 1024), F32),
    "flip_normed": ((1024, 512), BF),
    "flip_attended": ((1024, 512), BF),
    "grad_expanded": ((512, 2 * PADDED), BF),
    "grad_narrow": ((1024, PADDED), BF),
    "grad_wide": ((1024, 2 * PADDED), BF),
    "outputs": ((512, 1024), BF),
}
VMEM, ANY = pl.BlockSpec(memory_space=pltpu.VMEM), pl.BlockSpec(memory_space=pl.ANY)


def forward(direct, n_seq, shards, *inputs):
    results = Saved._fields
    count = 400 if direct else 16
    out = pl.pallas_call(
        functools.partial(forward_kernel, direct, n_seq),
        out_shape=tuple(jax.ShapeDtypeStruct(*SHAPES[n]) for n in results),
        in_specs=[VMEM if direct else ANY] * 5 + [VMEM] * len(inputs),
        out_specs=(ANY,) * len(results),
        scratch_shapes=[pltpu.VMEM(*SHAPES[n]) for n in FULL + HELD]
        + [
            pltpu.VMEM((512, 1024), BF),
            pltpu.VMEM((1024, 512), BF),
            pltpu.VMEM((1024, 512), BF),
            pltpu.VMEM((512, 1024), F32),
            pltpu.VMEM((512, 1024), BF),
            pltpu.VMEM((2, 512, 384), BF),
            pltpu.VMEM((512, 384), F32),
            pltpu.VMEM((2, 2, 128, 256), F32),
            pltpu.VMEM((8, 128), F32),
            pltpu.VMEM((8, 128), F32),
            pltpu.VMEM((2, 512, 768), BF),
            pltpu.VMEM((2, 1024, 384), BF),
            pltpu.VMEM((2, 1024, 768), BF),
            pltpu.SemaphoreType.DMA((count,)),
            pltpu.SemaphoreType.DMA((count,)),
            pltpu.SemaphoreType.DMA((len(results) + len(FULL),)),
            pltpu.SemaphoreType.DMA((4, 2)),
        ],
        compiler_params=pltpu.CompilerParams(collective_id=1, has_side_effects=True, vmem_limit_bytes=62 << 20),
    )(*shards, *inputs)
    return Saved(*out)


def add_into(target, a, b):
    count = target.shape[0]

    def part(i):
        at = pl.ds(pl.multiple_of(i * 32, 32), 32)
        target[at, :] = a[at, :] + b[at, :]

    if count == 32:
        part(0)
    else:
        pl.loop(0, count // 32)(part)


def landing_shapes(streams):
    result = []
    for order, _, _, count in streams:
        shapes, left, depth = {}, ["y", "x"], 128
        for axis in ORDERS[order][::-1]:
            if axis == "z":
                shapes["z"] = (2,) * len(left) + (160, count)
                depth = 32
            else:
                left.remove(axis)
                shapes[axis] = (2,) * len(left) + (depth, count)
        result.append(shapes)
    return result


def add_scatter(tasks, streams, chunks, sources, totals, slots, landed, sums, sems, credit):
    b, z, y, x, c = place()
    for k, (which, first, count) in enumerate(chunks):
        name, cols = FULL[which], pl.ds(first, count)
        slot = slots.at[k % 2, :, :, :, pl.ds(0, count)]
        out = remote(sources[name].at[:, :, :, cols], slot, sems, tasks.take(), (b ^ 1, z))

        def start(k=k, out=out):
            if k >= 2:
                pl.semaphore_wait(credit.at[k % 2], 1)
            out.start()

        def arrive(k=k, out=out, name=name, cols=cols, slot=slot):
            out.wait_recv()
            for yy in range(2):
                for xx in range(2):
                    total = totals[name].at[yy, xx, :, cols]
                    add_into(total, total, slot.at[yy, xx])
            if k + 2 < len(chunks):
                pl.semaphore_signal(credit.at[k % 2], inc=1, device_id=(b ^ 1, z), device_id_type=MESH)

        tasks.add(start)
        tasks.add(arrive)
        tasks.finals.append(out.wait_send)

    def one(j, order, name, first, count):
        cols, land = pl.ds(first, count), landed[j]

        def view(fixed, at=None):
            zz = fixed.get("z", slice(None)) if at is None else piece(at)
            return totals[name].at[fixed.get("y", slice(None)), fixed.get("x", slice(None)), zz, cols]

        def blocks(ref):
            if len(ref.shape) == 2:
                return [ref]
            return [r for i in range(ref.shape[0]) for r in blocks(ref.at[i])]

        def accumulate(target, source):
            for t, s in zip(blocks(target), blocks(source)):
                add_into(t, t, s)

        fixed, pending, sub = {}, None, 0
        for axis in order[::-1]:
            if axis in "xy":
                mine, device = (y if axis == "y" else x), (b ^ (2 if axis == "x" else 4), z)
                keep = dict(fixed)
                keep[axis] = mine
                give = dict(fixed)
                give[axis] = 1 - mine
                out = remote(view(give), land[axis], sems, tasks.take(), device)

                def step(pending=pending, out=out):
                    if pending:
                        pending()
                    out.start()

                def pending(out=out, keep=keep, axis=axis):
                    out.wait_recv()
                    accumulate(view(keep), land[axis])

                tasks.add(step)
                tasks.finals.append(out.wait_send)
                fixed, sub = keep, sub + 1
            else:
                left = [a for a in "yx" if a not in fixed]

                def spot(t, own_from_below):
                    at = jnp.where(own_from_below, 128, t * 32)
                    return land["z"].at[(slice(None),) * len(left) + (pl.ds(pl.multiple_of(at, 32), 32),)]

                for hop in (2, 1, 0):
                    i = tasks.take(2)
                    down_piece, up_piece = jnp.maximum(z - 1 - hop, 0), jnp.minimum(z + 1 + hop, 3)
                    has_down, has_up = z - 1 - hop >= 0, z + 1 + hop <= 3
                    below, above = (b, jnp.maximum(z - 1, 0)), (b, jnp.minimum(z + 1, 3))
                    down = remote(view(fixed, down_piece), spot(down_piece, False), sems, i, below)
                    up = remote(view(fixed, up_piece), spot(up_piece, hop == 0), sems, i + 1, above)
                    from_above, from_below = (z < 3) & (z - hop >= 0), (z > 0) & (z + hop <= 3)
                    low, high = jnp.maximum(z - hop, 0), jnp.minimum(z + hop, 3)
                    fall = remote(view(fixed, low), spot(low, False), sems, i, below)
                    rise = remote(view(fixed, high), spot(high, hop == 0), sems, i + 1, above)

                    def step(pending=pending, up=up, down=down, has_up=has_up, has_down=has_down):
                        if pending:
                            pending()
                        pl.when(has_down)(down.start)
                        pl.when(has_up)(up.start)

                    def pending(
                        fall=fall,
                        rise=rise,
                        from_above=from_above,
                        from_below=from_below,
                        low=low,
                        high=high,
                        hop=hop,
                        fixed=fixed,
                        spot=spot,
                    ):
                        @pl.when(from_above)
                        def _():
                            fall.wait_recv()
                            accumulate(view(fixed, low), spot(low, False))

                        @pl.when(from_below)
                        def _():
                            rise.wait_recv()
                            accumulate(view(fixed, high), spot(high, hop == 0))

                    def final(up=up, down=down, has_up=has_up, has_down=has_down):
                        pl.when(has_down)(down.wait_send)
                        pl.when(has_up)(up.wait_send)

                    tasks.add(step)
                    tasks.finals.append(final)
                    sub += 1
                fixed = dict(fixed)
                fixed["z"] = piece(z)

        def last(pending=pending, fixed=fixed):
            pending()
            sums[name][:, cols] = view(fixed)[...].astype(jnp.float32)

        tasks.add(last)

    for j, (order, which, first, count) in enumerate(streams):
        one(j, ORDERS[order], FULL[which], first, count)


class Scratch(NamedTuple):
    ring: Any
    expanded: Any
    second: Any
    middle: Any
    branch: Any
    flipped: Any
    keys: Any
    values: Any
    probs: Any
    projected: Any
    grad_v: Any
    edge: Any
    edge_landed: Any
    gains: Any


class Saved(NamedTuple):
    q: Any
    o: Any
    w: Any
    queries: Any
    keys: Any
    values: Any
    probs: Any
    middle: Any
    gains: Any
    flip_normed: Any
    flip_attended: Any
    grad_expanded: Any
    grad_narrow: Any
    grad_wide: Any
    outputs: Any


WEIGHTS = ("q", "o", "w", "n")


def backward_kernel(direct, n_seq, shapes, *refs):
    refs = list(refs)

    def pop(names):
        return {n: refs.pop(0) for n in names}

    src = Saved(*[refs.pop(0) for _ in Saved._fields])
    tokens, cotangent, cosine, sine = pop(range(4)).values()
    grad_tokens = refs.pop(0)
    sums = pop(WEIGHTS if direct else range(4))
    totals = pop(WEIGHTS if direct else ("q", "o"))
    others = pop(("q", "o"))
    landed = [pop(s) for s in shapes]
    slots = refs.pop(0) if direct else None
    v = Scratch(*[refs.pop(0) for _ in Scratch._fields])
    send_sems, recv_sems, local_sems, credit = refs
    sems = (send_sems, recv_sems)
    b, z, y, x, c = place() if direct else (lax.axis_index(BATCH), lax.axis_index(SEQ), 0, 0, 0)
    rows, span = 2, 256
    tasks = Tasks()
    local = {}

    def load(name, source, target):
        local[name] = pltpu.make_async_copy(source, target, local_sems.at[name])
        local[name].start()

    def wait(name):
        local.pop(name).wait()

    def load_group(i):
        cols = pl.ds(i * 768, 768)
        load(WIDE + i % 2, src.w.at[:, :, :, :, cols], v.ring.at[i % 2, :, :, :, :, pl.ds(0, 768)])
        load(EXPANDED + i % 2, src.grad_expanded.at[:, cols], v.expanded.at[i % 2])

    def grad_second(i):
        def run():
            wait(WIDE + i % 2)
            wait(EXPANDED + i % 2)

            @pl.loop(0, 2)
            def _(j):
                block = v.ring[i % 2, j, :, :, :, pl.ds(0, 768)].reshape(512, 768)
                part = dot_rows(v.expanded[i % 2], block)
                if i == 0:
                    v.second[:, tile(j, 512)] = part
                else:
                    v.second[:, tile(j, 512)] += part

            if i < 5:
                load_group(i + 2)
            elif i == 5:
                load(WIDE + 1, src.o, v.ring.at[1])
            else:
                load(WIDE, src.q.at[:, :, :, :, pl.ds(0, 1024)], v.ring.at[0])

        return run

    for i in range(7):
        tasks.add(grad_second(i))

    def norm_back(values, upstream, gain):
        unit, inverse = norm_parts(values)
        scaled = upstream * gain
        return inverse * (
            scaled - jnp.mean(scaled, -1, keepdims=True) - unit * jnp.mean(scaled * unit, -1, keepdims=True)
        )

    def second_norm_back():
        wait(MIDDLE)
        wait(GAINS)

        @pl.loop(0, 8)
        def _(i):
            at = tile(i, 64)
            grad = norm_back(v.middle[at, :], v.second[at, :], v.gains[1:2, :])
            grad = grad + cotangent[at, :].astype(jnp.float32)
            v.middle[at, :] = grad
            v.branch[at, :] = grad.astype(jnp.bfloat16)

    tasks.add(second_norm_back)

    def back_out():
        wait(WIDE + 1)

        @pl.loop(0, 4)
        def _(j):
            block = v.ring[1, j // 2, j % 2].reshape(256, 1024)
            v.projected[:, pl.ds(pl.multiple_of(2048 + j * 256, 256), 256)] = dot_rows(
                v.branch[...], block
            ).astype(jnp.bfloat16)

        load(WIDE + 1, src.q.at[:, :, :, :, pl.ds(1024, 1024)], v.ring.at[1])
        for name in (QUERIES, KEYS, VALUES):
            wait(name)

    tasks.add(back_out)

    def grad_weight(name, first, count, source):
        def run():
            if name == "o":
                wait(FLIPPED)

            @pl.loop(first, first + count)
            def _(j):
                cols = tile(j, 256)
                out = dot(v.flipped[...], source(cols)).astype(jnp.bfloat16).reshape(2, 2, 2, 128, 256)
                totals[name][:, :, :, cols], others[name][:, :, :, cols] = out[0], out[1]

            if name == "o":
                load(FLIPPED, src.flip_normed, v.flipped)
            if name == "q" and first == 0:
                pass

        return run

    tasks.add(grad_weight("o", 0, 4, lambda cols: v.branch[:, cols]))

    def attend_back(r, k, first):
        def run():
            if first == 0:
                wait(PROBS + k)
            row, window = slice(r * span + k * 128, r * span + (k + 1) * 128), slice(k * 128, k * 128 + 256)

            @pl.loop(first, first + 4)
            def _(p):
                cols = tile(p, 128)
                upper = pl.ds(pl.multiple_of(2048 + p * 128, 128), 128)
                side = lanes(256) < HDIM
                upstream, pair = v.projected[row, upper], v.probs[k, p]
                key_pair = pair_rows(v.keys[r, window, cols])
                grad_p = dot_rows(upstream, pair_rows(v.values[r, window, cols]))
                parts = []
                for h in range(2):
                    part = slice(h * 256, (h + 1) * 256)
                    weights = pair[:, part].astype(jnp.float32)
                    inner = jnp.sum(grad_p[:, part] * weights, -1, keepdims=True)
                    parts.append((weights * (grad_p[:, part] - inner)).astype(jnp.bfloat16))
                grad_s = jnp.concatenate(parts, 1)
                back_v = dot_columns(pair, upstream)
                back_k = dot_columns(grad_s, v.projected[row, cols])
                at = slice(k * 128, (k + 1) * 128)
                grad_q = rotate(dot(grad_s, key_pair) * HDIM**-0.5, cosine[at, :], -sine[at, :])
                v.projected[row, cols] = grad_q.astype(jnp.bfloat16)
                for which, back in ((0, back_k), (1, back_v)):
                    back = jnp.where(side, back[:256], back[256:])
                    out = v.second if which == 0 else v.grad_v
                    if k == 0:
                        v.edge[r, 0, which, :, cols] = back[:HALF].astype(jnp.bfloat16)
                        out[r * span : r * span + 192, cols] = back[HALF:]
                    else:
                        out[r * span + 64 : r * span + 192, cols] += back[:128]
                        out[r * span + 192 : (r + 1) * span, cols] = back[128:192]
                        v.edge[r, 1, which, :, cols] = back[192:].astype(jnp.bfloat16)

            if first == 4 and r == 0:
                load(PROBS + k, src.probs.at[1, k], v.probs.at[k])

        return run

    waits = []
    for i in range(8):
        tasks.add(attend_back(i // 4, (i // 2) % 2, 4 * (i % 2)))
        if i % 4 == 3:
            edge, land = v.edge.at[i // 4], v.edge_landed.at[i // 4]
            start, finish = edge_exchange(tasks, sems, n_seq, edge.at[1], land.at[0], edge.at[0], land.at[1])
            tasks.add(start)
            waits.append(finish)
    for r in range(rows):
        tasks.add(waits[r])

    def turn_back(r):
        def run():
            for part, out in ((0, v.second), (1, v.grad_v)):

                @pl.when(z > 0)
                def _():
                    out[r * span : r * span + HALF, :] += v.edge_landed[r, 0, part].astype(jnp.float32)

                @pl.when(z < n_seq - 1)
                def _():
                    at = slice((r + 1) * span - HALF, (r + 1) * span)
                    out[at, :] += v.edge_landed[r, 1, part].astype(jnp.float32)

            @pl.loop(0, 8)
            def _(p):
                at, cols = slice(r * span, (r + 1) * span), tile(p, 128)
                turned = rotate(v.second[at, cols], cosine[...], -sine[...])
                v.projected[at, pl.ds(pl.multiple_of(1024 + p * 128, 128), 128)] = turned.astype(jnp.bfloat16)
                v.projected[at, pl.ds(pl.multiple_of(2048 + p * 128, 128), 128)] = v.grad_v[at, cols].astype(
                    jnp.bfloat16
                )

        return run

    for r in range(rows):
        tasks.add(turn_back(r))

    def grad_qkv(first):
        inner = grad_weight("q", first, 4, lambda cols: v.projected[:, cols])

        def run():
            if first == 0:
                wait(FLIPPED)
            inner()

        return run

    for i, letter in enumerate("abc"):
        tasks.add(grad_qkv(4 * i))

    def grad_normed(i):
        def run():
            wait(WIDE + i % 2)

            @pl.loop(0, 2)
            def _(j):
                block = v.ring[i % 2, j].reshape(512, 1024)
                part = dot_rows(v.projected[:, i * 1024 : (i + 1) * 1024], block)
                if i == 0:
                    v.grad_v[:, tile(j, 512)] = part
                else:
                    v.grad_v[:, tile(j, 512)] += part

            if i == 0:
                load(WIDE, src.q.at[:, :, :, :, pl.ds(2048, 1024)], v.ring.at[0])

        return run

    for i in range(3):
        tasks.add(grad_normed(i))

    def first_norm_back():
        @pl.loop(0, 8)
        def _(i):
            at = tile(i, 64)
            grad = norm_back(tokens[at, :].astype(jnp.float32), v.grad_v[at, :], v.gains[0:1, :])
            v.branch[at, :] = (v.middle[at, :] + grad).astype(jnp.bfloat16)

        load(RESULT, v.branch, grad_tokens)

    tasks.add(first_norm_back)
    if direct:
        sources = dict(others)
        sources.update({n: g.at[1] for n, g in (("n", src.grad_narrow), ("w", src.grad_wide))})
        add_scatter(tasks, SCATTER_STREAMS, SCATTER_CHUNKS, sources, totals, slots, landed, sums, sems, credit)
        load(TOTAL, src.grad_narrow.at[0], totals["n"])
        load(TOTAL + 1, src.grad_wide.at[0], totals["w"])
    load_group(0)
    load_group(1)
    load(MIDDLE, src.middle, v.middle)
    load(GAINS, src.gains, v.gains)
    load(QUERIES, src.queries, v.projected.at[:, pl.ds(0, 1024)])
    load(KEYS, src.keys, v.keys)
    load(VALUES, src.values, v.values)
    load(FLIPPED, src.flip_attended, v.flipped)
    for k in range(2):
        load(PROBS + k, src.probs.at[0, k], v.probs.at[k])
    enter(direct, n_seq)
    if direct:
        wait(TOTAL)
        wait(TOTAL + 1)
    tasks.run(BACKWARD_ORDER if direct else range(len(tasks.steps)))
    if not direct:
        for i, name in enumerate("qo"):
            load(OWN + i, totals[name], sums[i])
            load(OTHER + i, others[name], sums[2 + i])
    for copy in local.values():
        copy.wait()


WIDE, EXPANDED, PROBS, TOTAL, OWN, OTHER = 0, 2, 4, 6, 8, 10
MIDDLE, GAINS, QUERIES, KEYS, VALUES, FLIPPED, RESULT, LOADS = range(12, 20)


def backward(direct, n_seq, saved, *inputs):
    split = lambda a: a.reshape(2, 2, 2, 128, -1)
    saved = saved._replace(grad_narrow=split(saved.grad_narrow), grad_wide=split(saved.grad_wide))
    shapes = landing_shapes(SCATTER_STREAMS) if direct else []
    widths = {"q": 3072, "o": 1024, "w": 2 * PADDED, "n": PADDED}
    held = WEIGHTS if direct else ("q", "o")
    half = lambda n: (2, 2, 128, widths[n])
    if direct:
        sums = [jax.ShapeDtypeStruct((32, widths[n]), F32) for n in WEIGHTS]
    else:
        sums = [jax.ShapeDtypeStruct(half(n), BF) for n in ("q", "o", "q", "o")]
    largest = max(count for _, _, count in SCATTER_CHUNKS)
    count = 400 if direct else 16
    out = pl.pallas_call(
        functools.partial(backward_kernel, direct, n_seq, shapes),
        out_shape=(jax.ShapeDtypeStruct((512, 1024), BF), *sums),
        in_specs=[ANY] * len(saved) + [VMEM] * len(inputs),
        out_specs=(ANY, *([VMEM if direct else ANY] * 4)),
        scratch_shapes=[pltpu.VMEM(half(n), BF) for n in held]
        + [pltpu.VMEM(half(n), BF) for n in ("q", "o")]
        + [pltpu.VMEM(s, BF) for stream in shapes for s in stream.values()]
        + ([pltpu.VMEM((2, 2, 2, 128, largest), BF)] if direct else [])
        + [
            pltpu.VMEM((2, 2, 2, 2, 128, 1024), BF),
            pltpu.VMEM((2, 512, 768), BF),
            pltpu.VMEM((512, 1024), F32),
            pltpu.VMEM((512, 1024), F32),
            pltpu.VMEM((512, 1024), BF),
            pltpu.VMEM((1024, 512), BF),
            pltpu.VMEM((2, 384, 1024), BF),
            pltpu.VMEM((2, 384, 1024), BF),
            pltpu.VMEM((2, 8, 128, 512), BF),
            pltpu.VMEM((512, 3072), BF),
            pltpu.VMEM((512, 1024), F32),
            pltpu.VMEM((2, 2, 2, HALF, 1024), BF),
            pltpu.VMEM((2, 2, 2, HALF, 1024), BF),
            pltpu.VMEM((8, 1024), F32),
            pltpu.SemaphoreType.DMA((count,)),
            pltpu.SemaphoreType.DMA((count,)),
            pltpu.SemaphoreType.DMA((LOADS,)),
            pltpu.SemaphoreType.REGULAR((2,)),
        ],
        compiler_params=pltpu.CompilerParams(collective_id=2, has_side_effects=True, vmem_limit_bytes=63 << 20),
    )(*saved, *inputs)
    return out


def tables(span):
    frequency = ROPE_BASE ** (-(2.0 * jnp.arange(HDIM // 2, dtype=jnp.float32)) / HDIM)
    positions = (lax.axis_index(SEQ) * span + jnp.arange(span, dtype=jnp.int32)).astype(jnp.float32)
    angles = positions[:, None] * frequency[None, :]
    cosine, sine = jnp.cos(angles), jnp.sin(angles)
    return jnp.concatenate([cosine] * 4, 1), jnp.concatenate([-sine, sine, -sine, sine], 1)


def interleave(wide):
    lead = wide.shape[0]
    wide = jnp.pad(wide.reshape(lead, 2, FF), ((0, 0), (0, 0), (0, PADDED - FF)))
    return wide.reshape(lead, 2, PADDED // 128, 128).swapaxes(1, 2).reshape(lead, 2 * PADDED)


def separate(wide):
    lead = wide.shape[0]
    wide = wide.reshape(lead, PADDED // 128, 2, 128).swapaxes(1, 2).reshape(lead, 2, PADDED)
    return wide[:, :, :FF].reshape(lead, 2 * FF)


def body(
    tokens,
    segment_ids,
    padding_mask,
    qkv_weight,
    out_weight,
    wide_weight,
    narrow_weight,
    first_gain,
    second_gain,
    cotangent,
):
    row_count, span, width = tokens.shape
    count = row_count * span
    n_seq = lax.axis_size(SEQ)
    direct = (lax.axis_size(BATCH), n_seq) == (8, 4)
    gains = jnp.stack([first_gain, second_gain], axis=1)
    shards = (
        jnp.pad(gains, ((0, 0), (0, 126))),
        qkv_weight,
        out_weight,
        interleave(wide_weight),
        jnp.pad(narrow_weight, ((0, 0), (0, PADDED - FF))),
    )
    if not direct:
        shards = [
            lax.all_gather(s, (BATCH, SEQ), axis=0, tiled=True).reshape(2, 2, 2, 128, s.shape[-1]) for s in shards
        ]
    tags = jnp.where(padding_mask == 1, segment_ids + 1, 0).astype(jnp.float32)
    tag_center = jnp.pad(tags, ((0, 8 - row_count), (HALF, HALF)))
    tag_edge = jnp.pad(
        jnp.concatenate([tags[:, span - HALF :], tags[:, :HALF]], 1), ((0, 8 - row_count), (0, 0))
    )
    query_tag = (segment_ids + 1).astype(jnp.float32).reshape(count, 1)
    cosine, sine = tables(span)
    hidden, upstream = tokens.reshape(count, width), cotangent.reshape(count, width)
    saved = forward(direct, n_seq, shards, hidden, upstream, cosine, sine, tag_center, tag_edge, query_tag)
    grad_tokens, *sums = backward(direct, n_seq, saved, hidden, upstream, cosine, sine)
    if not direct:
        own_q, own_o, other_q, other_o = sums
        grads = [jnp.stack([own, other]) for own, other in ((own_q, other_q), (own_o, other_o))]
        grads += [saved.grad_wide, saved.grad_narrow]
        sums = []
        for g in grads:
            g = jnp.moveaxis(g.reshape(2, 4, 128, -1), 0, 1).reshape(width, -1)
            sums.append(lax.psum_scatter(g, (BATCH, SEQ), scatter_dimension=0, tiled=True).astype(jnp.float32))
    sum_qkv, sum_out, sum_wide, sum_narrow = sums
    wide_shard = interleave(wide_weight)

    def gain_grad(weight, grad, gain):
        return jnp.sum(weight.astype(jnp.float32) * grad, 1) / gain.astype(jnp.float32)

    return (
        saved.outputs.reshape(tokens.shape),
        grad_tokens.reshape(tokens.shape),
        sum_qkv,
        sum_out,
        separate(sum_wide),
        sum_narrow[:, :FF],
        gain_grad(qkv_weight, sum_qkv, first_gain),
        gain_grad(wide_shard, sum_wide, second_gain),
    )


def solution(mesh):
    placed = (
        P(BATCH, SEQ, None),
        P(BATCH, SEQ),
        P(BATCH, SEQ),
        P((BATCH, SEQ), None),
        P((BATCH, SEQ), None),
        P((BATCH, SEQ), None),
        P((BATCH, SEQ), None),
        P((BATCH, SEQ)),
        P((BATCH, SEQ)),
        P(BATCH, SEQ, None),
    )
    return jax.shard_map(
        body,
        mesh=mesh,
        in_specs=placed,
        out_specs=(
            P(BATCH, SEQ, None),
            P(BATCH, SEQ, None),
            P((BATCH, SEQ), None),
            P((BATCH, SEQ), None),
            P((BATCH, SEQ), None),
            P((BATCH, SEQ), None),
            P((BATCH, SEQ)),
            P((BATCH, SEQ)),
        ),
        check_vma=False,
    )
```

```python
import functools
from typing import Any, NamedTuple

import jax
import jax.numpy as jnp
import numpy as np
from jax import lax
from jax.experimental import pallas as pl
from jax.experimental.pallas import tpu as pltpu
from jax.sharding import PartitionSpec as P

MESH = pl.DeviceIdType.MESH
HDIM = 64
FF = 2624
PADDED = 2688
HALF = 64
BATCH, SEQ = "batch", "seq"
ORDERS = ("zxy", "zyx", "xyz", "yxz", "xzy", "yzx")
FULL = ("g", "q", "o", "w", "n")
NORM_EPS = 1e-05
MASK_FILL = -1e30
ROPE_BASE = 10000.0
INV_SQRT_2PI = 0.3989422804014327
BF, F32 = jnp.bfloat16, jnp.float32

GATHER_STREAMS = (
    (5, 0, 0, 128),
    (0, 1, 0, 256),
    (1, 1, 256, 640),
    (4, 1, 896, 128),
    (0, 1, 1024, 256),
    (1, 1, 1280, 512),
    (2, 1, 1792, 128),
    (5, 1, 1920, 128),
    (0, 1, 2048, 640),
    (1, 1, 2688, 256),
    (4, 1, 2944, 128),
    (0, 2, 0, 384),
    (1, 2, 384, 512),
    (3, 2, 896, 128),
    (0, 4, 0, 1664),
    (1, 4, 1664, 896),
    (2, 4, 2560, 128),
    (1, 3, 0, 256),
    (4, 3, 256, 384),
    (5, 3, 640, 896),
    (0, 3, 1536, 128),
    (1, 3, 1664, 512),
    (2, 3, 2176, 128),
    (3, 3, 2304, 256),
    (4, 3, 2560, 512),
    (0, 3, 3072, 256),
    (1, 3, 3328, 256),
    (3, 3, 3584, 640),
    (5, 3, 4224, 384),
    (0, 3, 4608, 512),
    (5, 3, 5120, 256),
)
FORWARD_ORDER = (
    0, 1, 8, 15, 22, 29, 36, 43, 50, 57, 71, 92, 113, 127, 134, 155, 162, 169, 190, 218, 64, 78, 2,
    85, 197, 211, 44, 9, 93, 114, 16, 156, 23, 30, 163, 37, 191, 51, 58, 3, 45, 10, 17, 24, 31, 38,
    52, 65, 72, 4, 59, 11, 46, 18, 25, 32, 79, 39, 53, 66, 86, 73, 5, 94, 60, 12, 47, 99, 74, 19,
    80, 6, 87, 26, 95, 48, 33, 106, 7, 219, 115, 220, 13, 49, 67, 100, 27, 40, 61, 96, 107, 14, 116,
    28, 34, 20, 101, 97, 54, 35, 108, 120, 117, 68, 75, 128, 21, 221, 135, 41, 81, 88, 98, 118, 55,
    62, 109, 121, 102, 129, 76, 69, 42, 222, 56, 119, 223, 224, 63, 70, 77, 82, 225, 226, 89, 122,
    136, 83, 103, 130, 110, 141, 148, 170, 84, 227, 90, 228, 137, 229, 142, 149, 157, 164, 230, 91,
    171, 176, 231, 138, 143, 150, 158, 232, 165, 111, 123, 172, 183, 177, 233, 131, 159, 234, 166,
    112, 104, 198, 235, 184, 144, 178, 192, 124, 151, 160, 167, 185, 173, 179, 139, 199, 204, 132,
    212, 105, 161, 168, 125, 152, 193, 140, 145, 133, 200, 126, 186, 236, 205, 213, 180, 237, 174,
    238, 194, 239, 146, 153, 201, 240, 206, 175, 214, 187, 241, 147, 181, 242, 154, 195, 243, 207,
    244, 202, 182, 245, 196, 215, 246, 188, 247, 203, 248, 189, 208, 249, 250, 216, 251, 252, 217,
    253, 254, 255, 209, 256, 257, 258, 210, 259, 260, 261, 262, 263,
)
SCATTER_CHUNKS = (
    (4, 0, 1536),
    (4, 1536, 1152),
    (3, 0, 1536),
    (3, 1536, 1536),
    (3, 3072, 1536),
    (3, 4608, 768),
    (2, 0, 1024),
    (1, 0, 1024),
    (1, 1024, 1024),
    (1, 2048, 1024),
)
SCATTER_STREAMS = (
    (0, 4, 0, 512),
    (1, 4, 512, 640),
    (3, 4, 1152, 256),
    (4, 4, 1408, 128),
    (0, 4, 1536, 128),
    (1, 4, 1664, 128),
    (2, 4, 1792, 256),
    (3, 4, 2048, 384),
    (4, 4, 2432, 256),
    (0, 3, 0, 640),
    (1, 3, 640, 768),
    (3, 3, 1408, 128),
    (0, 3, 1536, 1024),
    (1, 3, 2560, 512),
    (0, 3, 3072, 256),
    (1, 3, 3328, 1280),
    (0, 3, 4608, 256),
    (2, 3, 4864, 384),
    (3, 3, 5248, 128),
    (1, 2, 0, 768),
    (2, 2, 768, 128),
    (5, 2, 896, 128),
    (0, 1, 0, 768),
    (1, 1, 768, 128),
    (5, 1, 896, 128),
    (0, 1, 1024, 896),
    (2, 1, 1920, 128),
    (0, 1, 2048, 256),
    (1, 1, 2304, 256),
    (3, 1, 2560, 256),
    (5, 1, 2816, 256),
)
BACKWARD_ORDER = (
    27, 0, 1, 29, 2, 3, 4, 28, 47, 53, 59, 31, 5, 6, 30, 83, 33, 7, 60, 65, 89, 8, 71, 77, 95, 32,
    107, 35, 10, 61, 54, 84, 66, 34, 37, 11, 12, 78, 101, 36, 13, 67, 48, 38, 90, 14, 62, 15, 72,
    108, 125, 9, 16, 39, 20, 41, 18, 49, 55, 63, 119, 68, 85, 102, 40, 64, 50, 96, 137, 17, 19, 73,
    79, 56, 91, 42, 21, 43, 22, 51, 97, 74, 80, 57, 113, 45, 23, 86, 103, 109, 126, 24, 52, 98, 75,
    81, 114, 58, 131, 44, 25, 104, 46, 26, 76, 82, 115, 110, 69, 92, 127, 143, 149, 105, 87, 99,
    120, 179, 155, 128, 111, 70, 106, 88, 100, 129, 150, 116, 112, 132, 156, 144, 167, 130, 93, 161,
    138, 121, 151, 157, 168, 94, 133, 122, 145, 117, 152, 169, 203, 197, 158, 173, 221, 134, 123,
    185, 146, 118, 191, 204, 139, 135, 153, 180, 124, 147, 222, 205, 136, 148, 174, 154, 215, 140,
    159, 162, 192, 223, 227, 181, 175, 141, 160, 170, 193, 186, 198, 206, 209, 176, 182, 142, 163,
    194, 216, 177, 187, 171, 207, 228, 224, 183, 195, 164, 210, 217, 199, 188, 172, 178, 196, 184,
    208, 225, 229, 165, 211, 189, 218, 226, 200, 230, 166, 190, 212, 219, 201, 231, 213, 220, 232,
    202, 214,
)


def place():
    b = lax.axis_index(BATCH)
    z = lax.axis_index(SEQ)
    return b, z, b // 4, (b // 2) % 2, b % 2


def remote(src, dst, sems, i, device):
    return pltpu.make_async_remote_copy(
        src_ref=src,
        dst_ref=dst,
        send_sem=sems[0].at[i],
        recv_sem=sems[1].at[i],
        device_id=device,
        device_id_type=MESH,
    )


def piece(t, n=32):
    return pl.ds(pl.multiple_of(t * n, n), n)


def greet(direct, n_seq):
    barrier = pltpu.get_barrier_semaphore()
    b, z = lax.axis_index(BATCH), lax.axis_index(SEQ)

    def signal(device):
        pl.semaphore_signal(barrier, inc=1, device_id=device, device_id_type=MESH)

    if direct:
        for bit in (1, 2, 4):
            signal((b ^ bit, z))
    pl.when(z < n_seq - 1)(lambda: signal((b, z + 1)))
    pl.when(z > 0)(lambda: signal((b, z - 1)))
    near = (z < n_seq - 1).astype(jnp.int32) + (z > 0).astype(jnp.int32)
    return lambda: pl.semaphore_wait(barrier, near + (3 if direct else 0))


class Tasks:
    def __init__(self):
        self.steps, self.finals, self.semaphores = [], [], 0

    def take(self, count=1):
        first = self.semaphores
        self.semaphores += count
        return first

    def add(self, step):
        self.steps.append(step)

    def run(self, order):
        for i in order:
            self.steps[i]()
        for final in self.finals:
            final()


def add_gather(tasks, streams, shards, fulls, sems):
    b, z, y, x, c = place()

    def one(j, order, name, first, count):
        full, cols = fulls[name], pl.ds(first, count)
        whole = set()

        def view(at=None, other=None):
            yy = slice(None) if "y" in whole else (1 - y if other == "y" else y)
            xx = slice(None) if "x" in whole else (1 - x if other == "x" else x)
            zz = piece(z if at is None else at) if "z" not in whole else slice(None)
            return full.at[yy, xx, c, zz, cols]

        pending, sub = None, 0
        for axis in order:
            own = None if whole else shards[name].at[:, cols]
            if axis in "xy":
                i, device = tasks.take(), (b ^ (2 if axis == "x" else 4), z)
                out = remote(view() if own is None else own, view(), sems, i, device)
                into = remote(view(other=axis), view(other=axis), sems, i, device)

                def step(pending=pending, out=out):
                    if pending:
                        pending()
                    out.start()

                tasks.add(step)
                tasks.finals.append(out.wait_send)
                pending, sub = into.wait_recv, sub + 1
            else:
                for hop in range(3):
                    i = tasks.take(2)
                    has_up, has_down = (z >= hop) & (z < 3), (z + hop <= 3) & (z > 0)
                    up_piece, down_piece = jnp.maximum(z - hop, 0), jnp.minimum(z + hop, 3)
                    above, below = (b, jnp.minimum(z + 1, 3)), (b, jnp.maximum(z - 1, 0))
                    start = own if hop == 0 else None
                    up = remote(view(up_piece) if start is None else start, view(up_piece), sems, i, above)
                    down = remote(
                        view(down_piece) if start is None else start, view(down_piece), sems, i + 1, below
                    )
                    from_below, from_above = z - 1 - hop >= 0, z + 1 + hop <= 3
                    low, high = jnp.maximum(z - 1 - hop, 0), jnp.minimum(z + 1 + hop, 3)
                    rise = remote(view(low), view(low), sems, i, above)
                    fall = remote(view(high), view(high), sems, i + 1, below)

                    def step(pending=pending, up=up, down=down, has_up=has_up, has_down=has_down):
                        if pending:
                            pending()
                        pl.when(has_up)(up.start)
                        pl.when(has_down)(down.start)

                    def pending(rise=rise, fall=fall, from_below=from_below, from_above=from_above):
                        pl.when(from_below)(rise.wait_recv)
                        pl.when(from_above)(fall.wait_recv)

                    def final(up=up, down=down, has_up=has_up, has_down=has_down):
                        pl.when(has_up)(up.wait_send)
                        pl.when(has_down)(down.wait_send)

                    tasks.add(step)
                    tasks.finals.append(final)
                    sub += 1
            whole.add(axis)
        i, device = tasks.take(), (b ^ 1, z)
        out = remote(full.at[:, :, c, :, cols], full.at[:, :, c, :, cols], sems, i, device)
        into = remote(full.at[:, :, 1 - c, :, cols], full.at[:, :, 1 - c, :, cols], sems, i, device)

        def step(pending=pending, out=out):
            pending()
            out.start()

        tasks.add(step)
        tasks.add(into.wait_recv)
        tasks.finals.append(out.wait_send)

    for j, (order, which, first, count) in enumerate(streams):
        one(j, ORDERS[order], FULL[which], first, count)


def dot(a, b):
    return jnp.dot(a, b, preferred_element_type=F32)


def dot_rows(a, b):
    return lax.dot_general(a, b, (((1,), (1,)), ((), ())), preferred_element_type=F32)


def dot_columns(a, b):
    return lax.dot_general(a, b, (((0,), (0,)), ((), ())), preferred_element_type=F32)


def tile(j, n):
    return pl.ds(pl.multiple_of(j * n, n), n)


def norm_parts(values):
    center = values - jnp.mean(values, -1, keepdims=True)
    inverse = lax.rsqrt(jnp.mean(center * center, -1, keepdims=True) + NORM_EPS)
    return center * inverse, inverse


def norm_rows(source, gain, target, n=256):
    @pl.loop(0, source.shape[0] // n)
    def _(i):
        unit, _ = norm_parts(source[tile(i, n), :].astype(F32))
        target[tile(i, n), :] = (unit * gain).astype(BF)


def lanes(n):
    return lax.broadcasted_iota(jnp.int32, (n, 128), 1)


def rotate(u, cosine, sine):
    partner = jnp.where(lanes(u.shape[0]) % HDIM < HDIM // 2, pltpu.roll(u, 96, 1), pltpu.roll(u, 32, 1))
    return u * cosine + partner * sine


def pair_rows(block):
    zero, first = jnp.zeros_like(block), lanes(block.shape[0]) < HDIM
    return jnp.concatenate([jnp.where(first, block, zero), jnp.where(first, zero, block)], 0)


def weight_tile(full, cols):
    block = full[:, :, :, :, cols]
    return block.reshape(1024, block.shape[-1])


def lay_out_gains(given, square, target):
    square[...] = jnp.zeros_like(square)
    square[0:2, 0:32] = given[...].astype(F32)
    target[...] = square[...].T[:32].astype(BF)


def shifted(ref, t):
    return pltpu.roll(ref[:, t * 128 : (t + 1) * 128].astype(F32), HALF, 1)


def lay_out_wide(given, target):
    first, count = lanes(32) < HALF, FF // 128
    for t in range(count + 1):
        into = given[:, t * 128 : (t + 1) * 128].astype(F32)
        gate = jnp.where(first, shifted(given, count + t), 0.0 if t == count else shifted(given, min(count + 1 + t, 2 * count)))
        if t == count:
            into = jnp.where(first, into, 0.0)
        target[:, t * 256 : t * 256 + 128] = into.astype(BF)
        target[:, t * 256 + 128 : (t + 1) * 256] = gate.astype(BF)


def lay_out_narrow(given, target):
    even = FF // 128 * 128
    target[:, :even] = given[:, :even]
    target[:, even:] = jnp.zeros((32, PADDED - even), BF)
    target[:, even:FF] = given[:, even:]


def flip(source, target, c):
    for k in range(8):
        at = (k // 2) + 4 * jnp.where(c == k % 2, 0, 1)
        target[tile(at, 128), :] = source[:, k * 128 : (k + 1) * 128].T


def edge_exchange(tasks, sems, n_seq, up_src, up_dst, down_src, down_dst):
    b, z = lax.axis_index(BATCH), lax.axis_index(SEQ)
    i = tasks.take(2)
    up = remote(up_src, up_dst, sems, i, (b, jnp.minimum(z + 1, n_seq - 1)))
    down = remote(down_src, down_dst, sems, i + 1, (b, jnp.maximum(z - 1, 0)))

    def start():
        pl.when(z < n_seq - 1)(up.start)
        pl.when(z > 0)(down.start)

    def wait():
        pl.when(z > 0)(up.wait_recv)
        pl.when(z < n_seq - 1)(down.wait_recv)

    def final():
        pl.when(z < n_seq - 1)(up.wait_send)
        pl.when(z > 0)(down.wait_send)

    tasks.finals.append(final)
    return start, wait


HELD = ("normed", "queries", "keys", "values", "probs", "attended", "middle", "gains", "flip_normed", "flip_attended")


def forward_kernel(direct, n_seq, *refs):
    refs = list(refs)

    def pop(names):
        return {n: refs.pop(0) for n in names}

    given = pop(FULL)
    given_tokens, given_cotangent, all_cosine, all_sine, given_segments, given_padding = pop(range(6)).values()
    saved = Saved(*[refs.pop(0) for _ in Saved._fields])
    fulls = pop(FULL)
    held = pop(HELD)
    normed, queries, keys, values, probs, attended, middle, gains, flip_normed, flip_attended = held.values()
    second, flip_second, flip_cotangent, total, final, active, upstream, bias = pop(range(8)).values()
    tag_rows, tag_edge, tag_prev, tag_next, cosine, sine = pop(range(6)).values()
    tokens, cotangent, segments, padding = pop(range(4)).values()
    expanded_ring, narrow_ring, wide_ring = pop(range(3)).values()
    shards = dict(given)
    if direct:
        square, raw_gains, raw_wide, raw_narrow = pop(range(4)).values()
        shards.update(pop("gqown"))
    send_sems, recv_sems, local_sems, ring_sems = refs
    sems = (send_sems, recv_sems)
    held.update(fulls)
    b, z, y, x, c = place() if direct else (lax.axis_index(BATCH), lax.axis_index(SEQ), 0, 0, 0)
    rows, span = 2, 256
    tasks = Tasks()
    copies = {}

    def save(name):
        target = getattr(saved, name)
        copies[name] = pltpu.make_async_copy(held[name], target, local_sems.at[Saved._fields.index(name)])
        copies[name].start()

    start_tags, wait_tags = edge_exchange(tasks, sems, n_seq, tag_edge, tag_prev, tag_edge, tag_next)
    tasks.add(start_tags)
    if direct:
        add_gather(tasks, GATHER_STREAMS, shards, fulls, sems)

    def edges(ext):
        return (
            ext.at[:, pl.ds(span, HALF), :],
            ext.at[:, pl.ds(0, HALF), :],
            ext.at[:, pl.ds(HALF, HALF), :],
            ext.at[:, pl.ds(span + HALF, HALF), :],
        )

    def prepare():
        flip(cotangent, flip_cotangent, c)
        for ext in (keys, values):

            @pl.when(z == 0)
            def _():
                ext[:, 0:HALF, :] = jnp.zeros((rows, HALF, 1024), BF)

            @pl.when(z == n_seq - 1)
            def _():
                ext[:, span + HALF :, :] = jnp.zeros((rows, HALF, 1024), BF)

        @pl.when(z == 0)
        def _():
            tag_prev[...] = jnp.zeros_like(tag_prev)

        @pl.when(z == n_seq - 1)
        def _():
            tag_next[...] = jnp.zeros_like(tag_next)

    def gain_rows():
        columns = weight_tile(fulls["g"], slice(None)).astype(F32)
        gains[...] = columns.T[:8]
        save("gains")

    def first_norm():
        norm_rows(tokens, gains[0:1, :], normed)
        flip(normed, flip_normed, c)
        save("flip_normed")

    def project(first, count, put, done=None):
        def run():
            @pl.loop(first, first + count)
            def _(j):
                put(j, dot(normed[...], weight_tile(fulls["q"], tile(j, 512))))

            if done:
                save(done)

        return run

    def turned(out, r, part):
        u = out[r * span : (r + 1) * span, part * 128 : (part + 1) * 128]
        return rotate(u, cosine[...], sine[...])

    def put_query(j, out):
        for part in range(4):
            for r in range(rows):
                u = (turned(out, r, part) * HDIM**-0.5).astype(BF)
                queries[r * span : (r + 1) * span, tile(4 * j + part, 128)] = u

    def put_key(j, out):
        for part in range(4):
            for r in range(rows):
                keys[r, HALF : HALF + span, tile(4 * (j - 2) + part, 128)] = turned(out, r, part).astype(BF)

    def put_value(j, out):
        for r in range(rows):
            values[r, HALF : HALF + span, tile(j - 4, 512)] = out[r * span : (r + 1) * span].astype(BF)

    tasks.add(prepare)
    tasks.add(gain_rows)
    tasks.add(first_norm)
    tasks.add(project(0, 2, put_query))
    tasks.add(project(2, 1, put_key))
    tasks.add(project(3, 1, put_key))
    start_keys, wait_keys = edge_exchange(tasks, sems, n_seq, *edges(keys))
    tasks.add(start_keys)
    tasks.add(project(4, 2, put_value, "q"))
    start_values, wait_values = edge_exchange(tasks, sems, n_seq, *edges(values))
    tasks.add(start_values)

    def wait_halo():
        wait_tags()
        wait_keys()
        wait_values()

    tasks.add(wait_halo)

    def masks():
        first = lanes(8) < HALF
        low, high = (pltpu.roll(tag_rows[:, t * 128 : (t + 1) * 128], HALF, 1) for t in range(2))
        ext = (jnp.where(first, tag_prev[...], low), jnp.where(first, low, high), jnp.where(first, high, tag_next[...]))
        ext = jnp.concatenate([jnp.concatenate([t, jnp.zeros((120, 128), F32)], 0).T for t in ext], 0)
        offset = lax.broadcasted_iota(jnp.int32, (256, 128), 0) - lax.broadcasted_iota(jnp.int32, (256, 128), 1)
        band, self_pair = (offset >= 0) & (offset <= 2 * HALF), offset == HALF
        for r in range(rows):
            for k in range(2):
                query_tag = (segments[r : r + 1, k * 128 : (k + 1) * 128] + 1).astype(F32)
                same = ext[k * 128 : k * 128 + 256, r : r + 1] == query_tag
                bias[r, k] = jnp.where(band & (same | self_pair), 0.0, MASK_FILL)
        for name in ("queries", "keys", "values"):
            save(name)

    tasks.add(masks)

    def attend_block(r, k, p):
        row, window = slice(r * span + k * 128, r * span + (k + 1) * 128), slice(k * 128, k * 128 + 256)
        cols = tile(p, 128)
        scores = dot_rows(pair_rows(keys[r, window, cols]), queries[row, cols])
        parts = []
        for h in range(2):
            s = scores[h * 256 : (h + 1) * 256] + bias[r, k]
            weights = jnp.exp(s - jnp.max(s, 0, keepdims=True))
            parts.append((weights * (1.0 / jnp.sum(weights, 0, keepdims=True))).astype(BF))
        pair = jnp.concatenate(parts, 0)
        probs[r, k, p] = pair
        attended[row, cols] = dot_columns(pair, pair_rows(values[r, window, cols])).astype(BF)

    def attend(first):
        def run():
            @pl.loop(first, first + 2)
            def _(p):
                for r in range(rows):
                    for k in range(2):
                        attend_block(r, k, p)

        return run

    for i in range(4):
        tasks.add(attend(2 * i))

    def project_out():
        @pl.loop(0, 2)
        def _(j):
            cols = tile(j, 512)
            middle[:, cols] = tokens[:, cols].astype(F32) + dot(attended[...], weight_tile(fulls["o"], cols))

        for name in ("o", "probs", "middle"):
            save(name)

    def second_norm():
        norm_rows(middle, gains[1:2, :], second)
        flip(second, flip_second, c)
        total[...] = middle[...]

    def flip_late():
        flip(attended, flip_attended, c)
        save("flip_attended")

    tasks.add(project_out)
    tasks.add(second_norm)
    tasks.add(flip_late)

    streams = {}

    def stream(name, i, source, target):
        streams[name, i] = pltpu.make_async_copy(source, target, ring_sems.at[name, i % 2])
        streams[name, i].start()

    def free(name, i):
        if (name, i) in streams:
            streams.pop((name, i)).wait()

    def gate(i):
        def run():
            free(0, i - 2)
            upstream[...] = dot(cotangent[...], weight_tile(fulls["n"], pl.ds(i * 384, 384)))

            @pl.loop(0, 3)
            def _(k):
                out = dot(second[...], weight_tile(fulls["w"], tile(3 * i + k, 256)))
                gate_in, gate_up = out[:, :128], out[:, 128:]
                mass = 0.5 * (1.0 + lax.erf(gate_in * 0.5**0.5))
                density = jnp.exp(-0.5 * gate_in * gate_in) * INV_SQRT_2PI
                gelu, above = gate_in * mass, upstream[:, tile(k, 128)]
                slope = gate_up * (mass + gate_in * density)
                expanded_ring[i % 2, :, tile(2 * k, 128)] = (above * slope).astype(BF)
                expanded_ring[i % 2, :, tile(2 * k + 1, 128)] = (above * gelu).astype(BF)
                active[i % 2, :, tile(k, 128)] = (gelu * gate_up).astype(BF)

            cols = pl.ds(i * 768, 768)
            stream(0, i, expanded_ring.at[i % 2], saved.grad_expanded.at[:, cols])
            free(4, i - 2)
            stream(4, i, fulls["w"].at[:, :, :, :, cols], saved.w.at[:, :, :, :, cols])

        return run

    def add_output(i):
        def run():
            @pl.loop(0, 2)
            def _(j):
                block = fulls["n"][j, :, :, :, pl.ds(i * 384, 384)].reshape(512, 384)
                total[:, tile(j, 512)] += dot_rows(active[i % 2], block)

            if i == 6:
                final[...] = total[...].astype(BF)
                stream(3, 0, final, saved.outputs)

        return run

    def grad_narrow(i):
        def run():
            free(1, i - 2)

            @pl.loop(0, 2)
            def _(j):
                narrow_ring[i % 2, tile(j, 512), :] = dot(flip_cotangent[tile(j, 512), :], active[i % 2]).astype(BF)

            stream(1, i, narrow_ring.at[i % 2], saved.grad_narrow.at[:, pl.ds(i * 384, 384)])

        return run

    def grad_wide(i):
        def run():
            free(2, i - 2)

            @pl.loop(0, 3)
            def _(k):
                part = tile(k, 256)
                wide_ring[i % 2, :, part] = dot(flip_second[...], expanded_ring[i % 2, :, part]).astype(BF)

            stream(2, i, wide_ring.at[i % 2], saved.grad_wide.at[:, pl.ds(i * 768, 768)])

        return run

    for i in range(7):
        tasks.add(gate(i))
        tasks.add(add_output(i))
        tasks.add(grad_narrow(i))
        tasks.add(grad_wide(i))

    base = len(Saved._fields)
    moves = [(given_segments, segments), (given_padding, padding)]
    if direct:
        moves += [(given["g"], raw_gains), (given["w"], raw_wide), (given["n"], raw_narrow)]
        moves += [(given[n], shards[n]) for n in "qo"]
    else:
        moves += [(given[n], fulls[n]) for n in FULL]
    moves += [(all_cosine.at[tile(z, span), :], cosine), (all_sine.at[tile(z, span), :], sine)]
    moves += [(given_tokens, tokens), (given_cotangent, cotangent)]
    moves = [pltpu.make_async_copy(*move, local_sems.at[base + i]) for i, move in enumerate(moves)]
    for move in moves:
        move.start()
    arrived = greet(direct, n_seq)
    for move in moves[:-4]:
        move.wait()
    tag_rows[...] = jnp.zeros_like(tag_rows)
    tag_rows[0:rows, :] = jnp.where(padding[...] == 1, segments[...] + 1, 0).astype(F32)
    low, high = (pltpu.roll(tag_rows[:, t * 128 : (t + 1) * 128], HALF, 1) for t in range(2))
    tag_edge[...] = jnp.where(lanes(8) < HALF, high, low)
    if direct:
        lay_out_gains(raw_gains, square, shards["g"])
        lay_out_wide(raw_wide, shards["w"])
        lay_out_narrow(raw_narrow, shards["n"])
        own = [
            pltpu.make_async_copy(shards[n], fulls[n].at[y, x, c, piece(z), :], local_sems.at[base + i])
            for i, n in enumerate(FULL)
        ]
        for copy in own:
            copy.start()
        for copy in own:
            copy.wait()
    for move in moves[-4:]:
        move.wait()
    arrived()
    tasks.run(FORWARD_ORDER if direct else range(len(tasks.steps)))
    for copy in list(copies.values()) + list(streams.values()):
        copy.wait()


SHAPES = {
    "g": ((2, 2, 2, 128, 128), BF),
    "q": ((2, 2, 2, 128, 3072), BF),
    "o": ((2, 2, 2, 128, 1024), BF),
    "w": ((2, 2, 2, 128, 2 * PADDED), BF),
    "n": ((2, 2, 2, 128, PADDED), BF),
    "normed": ((512, 1024), BF),
    "queries": ((512, 1024), BF),
    "keys": ((2, 384, 1024), BF),
    "values": ((2, 384, 1024), BF),
    "probs": ((2, 2, 8, 512, 128), BF),
    "attended": ((512, 1024), BF),
    "middle": ((512, 1024), F32),
    "gains": ((8, 1024), F32),
    "flip_normed": ((1024, 512), BF),
    "flip_attended": ((1024, 512), BF),
    "grad_expanded": ((512, 2 * PADDED), BF),
    "grad_narrow": ((1024, PADDED), BF),
    "grad_wide": ((1024, 2 * PADDED), BF),
    "outputs": ((512, 1024), BF),
}
VMEM, ANY = pl.BlockSpec(memory_space=pltpu.VMEM), pl.BlockSpec(memory_space=pl.ANY)


def forward(direct, n_seq, shards, *inputs):
    results = Saved._fields
    count = 400 if direct else 16
    out = pl.pallas_call(
        functools.partial(forward_kernel, direct, n_seq),
        out_shape=tuple(jax.ShapeDtypeStruct(*SHAPES[n]) for n in results),
        in_specs=[ANY] * 11,
        out_specs=(ANY,) * len(results),
        scratch_shapes=[pltpu.VMEM(*SHAPES[n]) for n in FULL + HELD]
        + [
            pltpu.VMEM((512, 1024), BF),
            pltpu.VMEM((1024, 512), BF),
            pltpu.VMEM((1024, 512), BF),
            pltpu.VMEM((512, 1024), F32),
            pltpu.VMEM((512, 1024), BF),
            pltpu.VMEM((2, 512, 384), BF),
            pltpu.VMEM((512, 384), F32),
            pltpu.VMEM((2, 2, 256, 128), F32),
            pltpu.VMEM((8, 256), F32),
            pltpu.VMEM((8, 128), F32),
            pltpu.VMEM((8, 128), F32),
            pltpu.VMEM((8, 128), F32),
            pltpu.VMEM((256, 128), F32),
            pltpu.VMEM((256, 128), F32),
            pltpu.VMEM((512, 1024), BF),
            pltpu.VMEM((512, 1024), BF),
            pltpu.VMEM((2, 256), jnp.int32),
            pltpu.VMEM((2, 256), jnp.int32),
            pltpu.VMEM((2, 512, 768), BF),
            pltpu.VMEM((2, 1024, 384), BF),
            pltpu.VMEM((2, 1024, 768), BF),
            *([pltpu.VMEM((128, 128), F32), pltpu.VMEM((2, 32), BF)] if direct else []),
            *([pltpu.VMEM((32, n), BF) for n in (2 * FF, FF, 128, 3072, 1024, 2 * PADDED, PADDED)] if direct else []),
            pltpu.SemaphoreType.DMA((count,)),
            pltpu.SemaphoreType.DMA((count,)),
            pltpu.SemaphoreType.DMA((len(results) + 11,)),
            pltpu.SemaphoreType.DMA((5, 2)),
        ],
        compiler_params=pltpu.CompilerParams(collective_id=1, has_side_effects=True, vmem_limit_bytes=62 << 20),
    )(*shards, *inputs)
    return Saved(*out)


def add_into(target, a, b):
    count = target.shape[0]

    def part(i):
        at = pl.ds(pl.multiple_of(i * 32, 32), 32)
        target[at, :] = a[at, :] + b[at, :]

    if count == 32:
        part(0)
    else:
        pl.loop(0, count // 32)(part)


def landing_shapes(streams):
    result = []
    for order, _, _, count in streams:
        shapes, left, depth = {}, ["y", "x"], 128
        for axis in ORDERS[order][::-1]:
            if axis == "z":
                shapes["z"] = (2,) * len(left) + (160, count)
                depth = 32
            else:
                left.remove(axis)
                shapes[axis] = (2,) * len(left) + (depth, count)
        result.append(shapes)
    return result


def add_scatter(tasks, streams, chunks, sources, totals, slots, landed, sums, sems, credit, ready):
    b, z, y, x, c = place()
    for k, (which, first, count) in enumerate(chunks):
        name, cols = FULL[which], pl.ds(first, count)
        slot = slots.at[k % 2, :, :, :, pl.ds(0, count)]
        out = remote(sources[name].at[:, :, :, cols], slot, sems, tasks.take(), (b ^ 1, z))

        def start(k=k, out=out):
            if k >= 2:
                pl.semaphore_wait(credit.at[k % 2], 1)
            out.start()

        def arrive(k=k, out=out, name=name, cols=cols, slot=slot):
            ready(k)
            out.wait_recv()
            for yy in range(2):
                for xx in range(2):
                    total = totals[name].at[yy, xx, :, cols]
                    add_into(total, total, slot.at[yy, xx])
            if k + 2 < len(chunks):
                pl.semaphore_signal(credit.at[k % 2], inc=1, device_id=(b ^ 1, z), device_id_type=MESH)

        tasks.add(start)
        tasks.add(arrive)
        tasks.finals.append(out.wait_send)

    def one(j, order, name, first, count):
        cols, land = pl.ds(first, count), landed[j]

        def view(fixed, at=None):
            zz = fixed.get("z", slice(None)) if at is None else piece(at)
            return totals[name].at[fixed.get("y", slice(None)), fixed.get("x", slice(None)), zz, cols]

        def blocks(ref):
            if len(ref.shape) == 2:
                return [ref]
            return [r for i in range(ref.shape[0]) for r in blocks(ref.at[i])]

        def accumulate(target, source):
            for t, s in zip(blocks(target), blocks(source)):
                add_into(t, t, s)

        fixed, pending, sub = {}, None, 0
        for axis in order[::-1]:
            if axis in "xy":
                mine, device = (y if axis == "y" else x), (b ^ (2 if axis == "x" else 4), z)
                keep = dict(fixed)
                keep[axis] = mine
                give = dict(fixed)
                give[axis] = 1 - mine
                out = remote(view(give), land[axis], sems, tasks.take(), device)

                def step(pending=pending, out=out):
                    if pending:
                        pending()
                    out.start()

                def pending(out=out, keep=keep, axis=axis):
                    out.wait_recv()
                    accumulate(view(keep), land[axis])

                tasks.add(step)
                tasks.finals.append(out.wait_send)
                fixed, sub = keep, sub + 1
            else:
                left = [a for a in "yx" if a not in fixed]

                def spot(t, own_from_below):
                    at = jnp.where(own_from_below, 128, t * 32)
                    return land["z"].at[(slice(None),) * len(left) + (pl.ds(pl.multiple_of(at, 32), 32),)]

                for hop in (2, 1, 0):
                    i = tasks.take(2)
                    down_piece, up_piece = jnp.maximum(z - 1 - hop, 0), jnp.minimum(z + 1 + hop, 3)
                    has_down, has_up = z - 1 - hop >= 0, z + 1 + hop <= 3
                    below, above = (b, jnp.maximum(z - 1, 0)), (b, jnp.minimum(z + 1, 3))
                    down = remote(view(fixed, down_piece), spot(down_piece, False), sems, i, below)
                    up = remote(view(fixed, up_piece), spot(up_piece, hop == 0), sems, i + 1, above)
                    from_above, from_below = (z < 3) & (z - hop >= 0), (z > 0) & (z + hop <= 3)
                    low, high = jnp.maximum(z - hop, 0), jnp.minimum(z + hop, 3)
                    fall = remote(view(fixed, low), spot(low, False), sems, i, below)
                    rise = remote(view(fixed, high), spot(high, hop == 0), sems, i + 1, above)

                    def step(pending=pending, up=up, down=down, has_up=has_up, has_down=has_down):
                        if pending:
                            pending()
                        pl.when(has_down)(down.start)
                        pl.when(has_up)(up.start)

                    def pending(
                        fall=fall,
                        rise=rise,
                        from_above=from_above,
                        from_below=from_below,
                        low=low,
                        high=high,
                        hop=hop,
                        fixed=fixed,
                        spot=spot,
                    ):
                        @pl.when(from_above)
                        def _():
                            fall.wait_recv()
                            accumulate(view(fixed, low), spot(low, False))

                        @pl.when(from_below)
                        def _():
                            rise.wait_recv()
                            accumulate(view(fixed, high), spot(high, hop == 0))

                    def final(up=up, down=down, has_up=has_up, has_down=has_down):
                        pl.when(has_down)(down.wait_send)
                        pl.when(has_up)(up.wait_send)

                    tasks.add(step)
                    tasks.finals.append(final)
                    sub += 1
                fixed = dict(fixed)
                fixed["z"] = piece(z)

        def last(pending=pending, fixed=fixed):
            pending()
            sums[name][:, cols] = view(fixed)[...].astype(F32)

        tasks.add(last)

    for j, (order, which, first, count) in enumerate(streams):
        one(j, ORDERS[order], FULL[which], first, count)


class Scratch(NamedTuple):
    ring: Any
    expanded: Any
    second: Any
    middle: Any
    branch: Any
    flipped: Any
    keys: Any
    values: Any
    probs: Any
    projected: Any
    grad_v: Any
    edge: Any
    edge_landed: Any
    gains: Any
    cosine: Any
    sine: Any
    tokens: Any
    cotangent: Any


class Saved(NamedTuple):
    q: Any
    o: Any
    w: Any
    queries: Any
    keys: Any
    values: Any
    probs: Any
    middle: Any
    gains: Any
    flip_normed: Any
    flip_attended: Any
    grad_expanded: Any
    grad_narrow: Any
    grad_wide: Any
    outputs: Any


WEIGHTS = ("q", "o", "w", "n")


def lay_out_sums(sums, wide, narrow):
    even, first, count = FF // 128 * 128, lanes(32) < HALF, FF // 128
    narrow[:, :even], narrow[:, even:] = sums["n"][:, :even], sums["n"][:, even:FF]

    def gate(t):
        return pltpu.roll(sums["w"][:, t * 256 + 128 : (t + 1) * 256], HALF, 1)

    for t in range(count):
        wide[:, t * 128 : (t + 1) * 128] = sums["w"][:, t * 256 : t * 256 + 128]
    wide[:, even : even + 128] = jnp.where(first, sums["w"][:, count * 256 : count * 256 + 128], gate(0))
    for t in range(count):
        wide[:, even + 128 + t * 128 : even + 256 + t * 128] = jnp.where(first, gate(t), gate(t + 1))


def grad_gains(sum_qkv, sum_wide, gain_pair, qkv_shard, wide_shard, square, target):
    square[...] = jnp.zeros_like(square)
    square[0:32, 0:1] = jnp.sum(qkv_shard[...].astype(F32) * sum_qkv[...], -1, keepdims=True)
    square[0:32, 1:2] = jnp.sum(wide_shard[...].astype(F32) * sum_wide[...], -1, keepdims=True)
    target[...] = square[...].T[0:2, 0:32] / gain_pair[...].astype(F32)


def backward_kernel(direct, n_seq, shapes, *refs):
    refs = list(refs)

    def pop(names):
        return {n: refs.pop(0) for n in names}

    src = Saved(*[refs.pop(0) for _ in Saved._fields])
    given_tokens, given_cotangent, all_cosine, all_sine = pop(range(4)).values()
    if direct:
        given_shards = pop(range(3)).values()
    grad_tokens = refs.pop(0)
    if direct:
        targets = pop(range(5)).values()
        sums = pop(WEIGHTS)
        square = refs.pop(0)
        laid_wide, laid_narrow, laid_gains, gain_pair, qkv_shard, wide_shard = pop(range(6)).values()
    else:
        sums = pop(range(4))
    totals = pop(WEIGHTS if direct else ("q", "o"))
    others = pop(("q", "o"))
    landed = [pop(s) for s in shapes]
    slots = refs.pop(0) if direct else None
    v = Scratch(*[refs.pop(0) for _ in Scratch._fields])
    cosine, sine, tokens, cotangent = v.cosine, v.sine, v.tokens, v.cotangent
    send_sems, recv_sems, local_sems, credit = refs
    sems = (send_sems, recv_sems)
    b, z, y, x, c = place() if direct else (lax.axis_index(BATCH), lax.axis_index(SEQ), 0, 0, 0)
    rows, span = 2, 256
    tasks = Tasks()
    local = {}

    def load(name, source, target):
        local[name] = pltpu.make_async_copy(source, target, local_sems.at[name])
        local[name].start()

    def wait(name):
        local.pop(name).wait()

    def load_group(i):
        cols = pl.ds(i * 768, 768)
        load(WIDE + i % 2, src.w.at[:, :, :, :, cols], v.ring.at[i % 2, :, :, :, :, pl.ds(0, 768)])
        load(EXPANDED + i % 2, src.grad_expanded.at[:, cols], v.expanded.at[i % 2])

    def grad_second(i):
        def run():
            wait(WIDE + i % 2)
            wait(EXPANDED + i % 2)

            @pl.loop(0, 2)
            def _(j):
                block = v.ring[i % 2, j, :, :, :, pl.ds(0, 768)].reshape(512, 768)
                part = dot_rows(v.expanded[i % 2], block)
                if i == 0:
                    v.second[:, tile(j, 512)] = part
                else:
                    v.second[:, tile(j, 512)] += part

            if i < 5:
                load_group(i + 2)
            elif i == 5:
                load(WIDE + 1, src.o, v.ring.at[1])
            else:
                load(WIDE, src.q.at[:, :, :, :, pl.ds(0, 1024)], v.ring.at[0])

        return run

    for i in range(7):
        tasks.add(grad_second(i))

    def norm_back(values, upstream, gain):
        unit, inverse = norm_parts(values)
        scaled = upstream * gain
        return inverse * (
            scaled - jnp.mean(scaled, -1, keepdims=True) - unit * jnp.mean(scaled * unit, -1, keepdims=True)
        )

    def second_norm_back():
        for name in (MIDDLE, GAINS, COTANGENT):
            wait(name)

        @pl.loop(0, 4)
        def _(i):
            at = tile(i, 128)
            grad = norm_back(v.middle[at, :], v.second[at, :], v.gains[1:2, :])
            grad = grad + cotangent[at, :].astype(F32)
            v.middle[at, :] = grad
            v.branch[at, :] = grad.astype(BF)

    tasks.add(second_norm_back)

    def back_out():
        wait(WIDE + 1)

        @pl.loop(0, 2)
        def _(j):
            cols = pl.ds(pl.multiple_of(2048 + j * 512, 512), 512)
            v.projected[:, cols] = dot_rows(v.branch[...], v.ring[1, j].reshape(512, 1024)).astype(BF)

        load(WIDE + 1, src.q.at[:, :, :, :, pl.ds(1024, 1024)], v.ring.at[1])
        for name in (QUERIES, KEYS, VALUES, COSINE, SINE):
            wait(name)

    tasks.add(back_out)

    def grad_weight(name, first, count, source):
        def run():
            if name == "o":
                wait(FLIPPED)

            @pl.loop(first, first + count)
            def _(j):
                cols = tile(j, 512)
                out = dot(v.flipped[...], source(cols)).astype(BF).reshape(2, 2, 2, 128, 512)
                totals[name][:, :, :, cols], others[name][:, :, :, cols] = out[0], out[1]

            if name == "o":
                load(FLIPPED, src.flip_normed, v.flipped)
            if name == "q" and first == 0:
                pass

        return run

    tasks.add(grad_weight("o", 0, 2, lambda cols: v.branch[:, cols]))

    def attend_back_block(r, k, p, i):
        row, window = slice(r * span + k * 128, r * span + (k + 1) * 128), slice(k * 128, k * 128 + 256)
        cols, upper = tile(p, 128), pl.ds(pl.multiple_of(2048 + p * 128, 128), 128)
        half, local_cols = i // 2, tile(p - 4 * (i // 2), 128)
        side = lanes(256) < HDIM
        upstream, pair = v.projected[row, upper], v.probs[i % 2, r, k, p - 2 * i]
        key_pair = pair_rows(v.keys[r, window, cols])
        grad_p = dot_rows(pair_rows(v.values[r, window, cols]), upstream)
        parts = []
        for h in range(2):
            part = slice(h * 256, (h + 1) * 256)
            weights = pair[part].astype(F32)
            inner = jnp.sum(grad_p[part] * weights, 0, keepdims=True)
            parts.append((weights * (grad_p[part] - inner)).astype(BF))
        grad_s = jnp.concatenate(parts, 0)
        back_v = dot(pair, upstream)
        back_k = dot(grad_s, v.projected[row, cols])
        at = slice(k * 128, (k + 1) * 128)
        grad_q = rotate(dot_columns(grad_s, key_pair) * HDIM**-0.5, cosine[at, :], -sine[at, :])
        v.projected[row, cols] = grad_q.astype(BF)
        for which, back, out in ((0, back_k, v.second), (1, back_v, v.grad_v)):
            back = jnp.where(side, back[:256], back[256:])
            if k == 0:
                v.edge[half, 0, which, r, :, local_cols] = back[:HALF].astype(BF)
                out[r * span : r * span + 192, cols] = back[HALF:]
            else:
                out[r * span + 64 : r * span + 192, cols] += back[:128]
                out[r * span + 192 : (r + 1) * span, cols] = back[128:192]
                v.edge[half, 1, which, r, :, local_cols] = back[192:].astype(BF)

    def load_probs(i):
        load(PROBS + i % 2, src.probs.at[:, :, pl.ds(2 * i, 2)], v.probs.at[i % 2])

    def attend_back(i):
        def run():
            wait(PROBS + i % 2)

            @pl.loop(2 * i, 2 * i + 2)
            def _(p):
                for k in range(2):
                    for r in range(rows):
                        attend_back_block(r, k, p, i)

            if i < 2:
                load_probs(i + 2)

        return run

    waits = []
    for i in range(4):
        tasks.add(attend_back(i))
        if i % 2:
            edge, land = v.edge.at[i // 2], v.edge_landed.at[i // 2]
            start, finish = edge_exchange(tasks, sems, n_seq, edge.at[1], land.at[0], edge.at[0], land.at[1])
            tasks.add(start)
            waits.append(finish)
    for half in range(2):
        tasks.add(waits[half])

    def turn_back(half):
        def run():
            here = slice(half * 512, (half + 1) * 512)
            for part, out in ((0, v.second), (1, v.grad_v)):
                for r in range(rows):

                    @pl.when(z > 0)
                    def _():
                        out[r * span : r * span + HALF, here] += v.edge_landed[half, 0, part, r].astype(F32)

                    @pl.when(z < n_seq - 1)
                    def _():
                        at = slice((r + 1) * span - HALF, (r + 1) * span)
                        out[at, here] += v.edge_landed[half, 1, part, r].astype(F32)

            @pl.loop(4 * half, 4 * half + 4)
            def _(p):
                cols, middle_cols, upper = (pl.ds(pl.multiple_of(f + p * 128, 128), 128) for f in (0, 1024, 2048))
                for r in range(rows):
                    at = slice(r * span, (r + 1) * span)
                    turned = rotate(v.second[at, cols], cosine[...], -sine[...])
                    v.projected[at, middle_cols] = turned.astype(BF)
                    v.projected[at, upper] = v.grad_v[at, cols].astype(BF)

        return run

    for half in range(2):
        tasks.add(turn_back(half))

    def grad_qkv(first):
        inner = grad_weight("q", first, 2, lambda cols: v.projected[:, cols])

        def run():
            if first == 0:
                wait(FLIPPED)
            inner()

        return run

    for i, letter in enumerate("abc"):
        tasks.add(grad_qkv(2 * i))

    def grad_normed(i):
        def run():
            wait(WIDE + i % 2)

            @pl.loop(0, 2)
            def _(j):
                block = v.ring[i % 2, j].reshape(512, 1024)
                part = dot_rows(v.projected[:, i * 1024 : (i + 1) * 1024], block)
                if i == 0:
                    v.grad_v[:, tile(j, 512)] = part
                else:
                    v.grad_v[:, tile(j, 512)] += part

            if i == 0:
                load(WIDE, src.q.at[:, :, :, :, pl.ds(2048, 1024)], v.ring.at[0])

        return run

    for i in range(3):
        tasks.add(grad_normed(i))

    def first_norm_back():
        wait(TOKENS)

        @pl.loop(0, 4)
        def _(i):
            at = tile(i, 128)
            grad = norm_back(tokens[at, :].astype(F32), v.grad_v[at, :], v.gains[0:1, :])
            v.branch[at, :] = (v.middle[at, :] + grad).astype(BF)

        load(RESULT, v.branch, grad_tokens)

    tasks.add(first_norm_back)
    if direct:
        sources = dict(others)
        sources.update({n: g.at[1] for n, g in (("n", src.grad_narrow), ("w", src.grad_wide))})

        def load_total(k):
            which, first, count = SCATTER_CHUNKS[k]
            if FULL[which] in sources and FULL[which] not in others:
                cols = pl.ds(first, count)
                source = (src.grad_narrow if FULL[which] == "n" else src.grad_wide).at[0, :, :, :, cols]
                load(LOADS + k, source, totals[FULL[which]].at[:, :, :, cols])

        def ready(k):
            if LOADS + k in local:
                wait(LOADS + k)

        add_scatter(tasks, SCATTER_STREAMS, SCATTER_CHUNKS, sources, totals, slots, landed, sums, sems, credit, ready)
        load_total(0)
    load_group(0)
    load_group(1)
    if direct:
        for k in range(1, len(SCATTER_CHUNKS)):
            load_total(k)
    load(COTANGENT, given_cotangent, cotangent)
    load(MIDDLE, src.middle, v.middle)
    load(GAINS, src.gains, v.gains)
    load(QUERIES, src.queries, v.projected.at[:, pl.ds(0, 1024)])
    load(KEYS, src.keys, v.keys)
    load(VALUES, src.values, v.values)
    load(FLIPPED, src.flip_attended, v.flipped)
    for i in range(2):
        load_probs(i)
    load(COSINE, all_cosine.at[tile(z, span), :], v.cosine)
    load(SINE, all_sine.at[tile(z, span), :], v.sine)
    load(TOKENS, given_tokens, tokens)
    if direct:
        for i, (given, held_here) in enumerate(zip(given_shards, (gain_pair, qkv_shard, wide_shard))):
            load(SHARD + i, given, held_here)
    greet(direct, n_seq)()
    tasks.run(BACKWARD_ORDER if direct else range(len(tasks.steps)))
    if direct:
        lay_out_sums(sums, laid_wide, laid_narrow)
        for i in range(3):
            wait(SHARD + i)
        grad_gains(sums["q"], laid_wide, gain_pair, qkv_shard, wide_shard, square, laid_gains)
        for i, (done, target) in enumerate(zip((sums["q"], sums["o"], laid_wide, laid_narrow, laid_gains), targets)):
            load(OWN + i, done, target)
    else:
        for i, name in enumerate("qo"):
            load(OWN + i, totals[name], sums[i])
            load(OTHER + i, others[name], sums[2 + i])
    for copy in local.values():
        copy.wait()


WIDE, EXPANDED, PROBS, OWN, OTHER = 0, 2, 4, 6, 8
MIDDLE, GAINS, QUERIES, KEYS, VALUES, FLIPPED, RESULT, COSINE, SINE, TOKENS, COTANGENT, SHARD, _, _, LOADS = range(12, 27)


def backward(direct, n_seq, saved, *inputs):
    split = lambda a: a.reshape(2, 2, 2, 128, -1)
    saved = saved._replace(grad_narrow=split(saved.grad_narrow), grad_wide=split(saved.grad_wide))
    shapes = landing_shapes(SCATTER_STREAMS) if direct else []
    widths = {"q": 3072, "o": 1024, "w": 2 * PADDED, "n": PADDED}
    held = WEIGHTS if direct else ("q", "o")
    half = lambda n: (2, 2, 128, widths[n])
    if direct:
        sums = [jax.ShapeDtypeStruct(s, F32) for s in ((32, 3072), (32, 1024), (32, 2 * FF), (32, FF), (2, 32))]
    else:
        sums = [jax.ShapeDtypeStruct(half(n), BF) for n in ("q", "o", "q", "o")]
    largest = max(count for _, _, count in SCATTER_CHUNKS)
    count = 400 if direct else 16
    out = pl.pallas_call(
        functools.partial(backward_kernel, direct, n_seq, shapes),
        out_shape=(jax.ShapeDtypeStruct((512, 1024), BF), *sums),
        in_specs=[ANY] * (len(saved) + len(inputs)),
        out_specs=(ANY,) * (1 + len(sums)),
        scratch_shapes=([pltpu.VMEM((32, widths[n]), F32) for n in WEIGHTS] if direct else [])
        + ([pltpu.VMEM((128, 128), F32)] if direct else [])
        + ([pltpu.VMEM((32, n), F32) for n in (2 * FF, FF)] + [pltpu.VMEM((2, 32), F32)] if direct else [])
        + ([pltpu.VMEM((2, 32), BF)] + [pltpu.VMEM((32, n), BF) for n in (3072, 2 * FF)] if direct else [])
        + [pltpu.VMEM(half(n), BF) for n in held]
        + [pltpu.VMEM(half(n), BF) for n in ("q", "o")]
        + [pltpu.VMEM(s, BF) for stream in shapes for s in stream.values()]
        + ([pltpu.VMEM((2, 2, 2, 128, largest), BF)] if direct else [])
        + [
            pltpu.VMEM((2, 2, 2, 2, 128, 1024), BF),
            pltpu.VMEM((2, 512, 768), BF),
            pltpu.VMEM((512, 1024), F32),
            pltpu.VMEM((512, 1024), F32),
            pltpu.VMEM((512, 1024), BF),
            pltpu.VMEM((1024, 512), BF),
            pltpu.VMEM((2, 384, 1024), BF),
            pltpu.VMEM((2, 384, 1024), BF),
            pltpu.VMEM((2, 2, 2, 2, 512, 128), BF),
            pltpu.VMEM((512, 3072), BF),
            pltpu.VMEM((512, 1024), F32),
            pltpu.VMEM((2, 2, 2, 2, HALF, 512), BF),
            pltpu.VMEM((2, 2, 2, 2, HALF, 512), BF),
            pltpu.VMEM((8, 1024), F32),
            pltpu.VMEM((256, 128), F32),
            pltpu.VMEM((256, 128), F32),
            pltpu.VMEM((512, 1024), BF),
            pltpu.VMEM((512, 1024), BF),
            pltpu.SemaphoreType.DMA((count,)),
            pltpu.SemaphoreType.DMA((count,)),
            pltpu.SemaphoreType.DMA((LOADS + len(SCATTER_CHUNKS),)),
            pltpu.SemaphoreType.REGULAR((2,)),
        ],
        compiler_params=pltpu.CompilerParams(collective_id=2, has_side_effects=True, vmem_limit_bytes=63 << 20),
    )(*saved, *inputs)
    return out


def tables(length):
    frequency = np.float32(ROPE_BASE) ** (-(2.0 * np.arange(HDIM // 2, dtype=np.float32)) / np.float32(HDIM))
    angles = np.arange(length, dtype=np.float32)[:, None] * frequency[None, :].astype(np.float32)
    cosine, sine = np.cos(angles), np.sin(angles)
    return np.concatenate([cosine] * 4, 1), np.concatenate([-sine, sine, -sine, sine], 1)


def interleave(wide):
    lead = wide.shape[0]
    wide = jnp.pad(wide.reshape(lead, 2, FF), ((0, 0), (0, 0), (0, PADDED - FF)))
    return wide.reshape(lead, 2, PADDED // 128, 128).swapaxes(1, 2).reshape(lead, 2 * PADDED)


def separate(wide):
    lead = wide.shape[0]
    wide = wide.reshape(lead, PADDED // 128, 2, 128).swapaxes(1, 2).reshape(lead, 2, PADDED)
    return wide[:, :, :FF].reshape(lead, 2 * FF)


def hand_over_kernel(*refs):
    count = (len(refs) - 2) // 3
    sources, targets, held = refs[:count], refs[count : 2 * count], refs[2 * count : 3 * count]
    arrive, leave = refs[3 * count :]
    moves = [pltpu.make_async_copy(s, h, arrive.at[i]) for i, (s, h) in enumerate(zip(sources, held))]
    for move in moves:
        move.start()
    backs = []
    for i, (h, t) in enumerate(zip(held, targets)):
        moves[i].wait()
        backs.append(pltpu.make_async_copy(h, t, leave.at[i]))
        backs[i].start()
    for back in backs:
        back.wait()


def hand_over(*arrays):
    count = len(arrays)
    return pl.pallas_call(
        hand_over_kernel,
        out_shape=tuple(jax.ShapeDtypeStruct(a.shape, a.dtype) for a in arrays),
        in_specs=[ANY] * count,
        out_specs=(ANY,) * count,
        scratch_shapes=[pltpu.VMEM(a.shape, a.dtype) for a in arrays] + [pltpu.SemaphoreType.DMA((count,))] * 2,
        compiler_params=pltpu.CompilerParams(vmem_limit_bytes=62 << 20),
    )(*arrays)


def body(
    tokens,
    segment_ids,
    padding_mask,
    qkv_weight,
    out_weight,
    wide_weight,
    narrow_weight,
    first_gain,
    second_gain,
    cotangent,
):
    row_count, span, width = tokens.shape
    count = row_count * span
    n_seq = lax.axis_size(SEQ)
    direct = (lax.axis_size(BATCH), n_seq) == (8, 4)
    gains = jnp.stack([first_gain, second_gain])
    if direct:
        shards = (gains, qkv_weight, out_weight, wide_weight, narrow_weight)
    else:
        shards = (
            jnp.pad(gains.T, ((0, 0), (0, 126))),
            qkv_weight,
            out_weight,
            interleave(wide_weight),
            jnp.pad(narrow_weight, ((0, 0), (0, PADDED - FF))),
        )
        shards = [lax.all_gather(s, (BATCH, SEQ), axis=0, tiled=True).reshape(2, 2, 2, 128, s.shape[-1]) for s in shards]
    cosine, sine = (jnp.asarray(t) for t in tables(n_seq * span))
    hidden, upstream = tokens.reshape(count, width), cotangent.reshape(count, width)
    saved = forward(direct, n_seq, shards, hidden, upstream, cosine, sine, segment_ids, padding_mask)
    if direct:
        grad_tokens, grad_qkv, grad_out, grad_wide, grad_narrow, grad_gains = backward(
            direct, n_seq, saved, hidden, upstream, cosine, sine, gains, qkv_weight, wide_weight
        )
        outputs, grad_tokens, grad_qkv, grad_out, grad_wide, grad_narrow, grad_gains = hand_over(
            saved.outputs, grad_tokens, grad_qkv, grad_out, grad_wide, grad_narrow, grad_gains
        )
        grad_first, grad_second = grad_gains[0], grad_gains[1]
    else:
        outputs = saved.outputs
        grad_tokens, own_q, own_o, other_q, other_o = backward(direct, n_seq, saved, hidden, upstream, cosine, sine)
        grads = [jnp.stack([own, other]) for own, other in ((own_q, other_q), (own_o, other_o))]
        sums = []
        for g in grads + [saved.grad_wide, saved.grad_narrow]:
            g = jnp.moveaxis(g.reshape(2, 4, 128, -1), 0, 1).reshape(width, -1)
            sums.append(lax.psum_scatter(g, (BATCH, SEQ), scatter_dimension=0, tiled=True).astype(F32))
        grad_qkv, grad_out, grad_wide, grad_narrow = sums
        grad_wide, grad_narrow = separate(grad_wide), grad_narrow[:, :FF]

        def gain_grad(weight, grad, gain):
            return jnp.sum(weight.astype(F32) * grad, 1) / gain.astype(F32)

        grad_first = gain_grad(qkv_weight, grad_qkv, first_gain)
        grad_second = gain_grad(wide_weight, grad_wide, second_gain)
    return (
        outputs.reshape(tokens.shape),
        grad_tokens.reshape(tokens.shape),
        grad_qkv,
        grad_out,
        grad_wide,
        grad_narrow,
        grad_first,
        grad_second,
    )


def solution(mesh):
    placed = (
        P(BATCH, SEQ, None),
        P(BATCH, SEQ),
        P(BATCH, SEQ),
        P((BATCH, SEQ), None),
        P((BATCH, SEQ), None),
        P((BATCH, SEQ), None),
        P((BATCH, SEQ), None),
        P((BATCH, SEQ)),
        P((BATCH, SEQ)),
        P(BATCH, SEQ, None),
    )
    return jax.shard_map(
        body,
        mesh=mesh,
        in_specs=placed,
        out_specs=(
            P(BATCH, SEQ, None),
            P(BATCH, SEQ, None),
            P((BATCH, SEQ), None),
            P((BATCH, SEQ), None),
            P((BATCH, SEQ), None),
            P((BATCH, SEQ), None),
            P((BATCH, SEQ)),
            P((BATCH, SEQ)),
        ),
        check_vma=False,
    )
```

```python
import functools
from typing import Any, NamedTuple

import jax
import jax.numpy as jnp
import numpy as np
from jax import lax
from jax.experimental import pallas as pl
from jax.experimental.pallas import tpu as pltpu
from jax.sharding import PartitionSpec as P

MESH = pl.DeviceIdType.MESH
HDIM = 64
FF = 2624
PADDED = 2688
HALF = 64
BATCH, SEQ = "batch", "seq"
ORDERS = ("zxy", "zyx", "xyz", "yxz", "xzy", "yzx")
FULL = ("g", "q", "o", "w", "n")
NORM_EPS = 1e-05
MASK_FILL = -1e30
ROPE_BASE = 10000.0
INV_SQRT_2PI = 0.3989422804014327
BF, F32 = jnp.bfloat16, jnp.float32

GATHER_STREAMS = (
    (1, 0, 0, 128),
    (0, 1, 0, 384),
    (1, 1, 384, 512),
    (5, 1, 896, 128),
    (0, 1, 1024, 128),
    (1, 1, 1152, 384),
    (2, 1, 1536, 128),
    (4, 1, 1664, 384),
    (0, 1, 2048, 256),
    (1, 1, 2304, 768),
    (0, 2, 0, 384),
    (1, 2, 384, 384),
    (5, 2, 768, 256),
    (0, 4, 0, 768),
    (1, 4, 768, 640),
    (2, 4, 1408, 128),
    (4, 4, 1536, 768),
    (5, 4, 2304, 384),
    (0, 3, 0, 128),
    (1, 3, 128, 128),
    (2, 3, 256, 128),
    (4, 3, 384, 768),
    (5, 3, 1152, 384),
    (0, 3, 1536, 512),
    (1, 3, 2048, 128),
    (2, 3, 2176, 384),
    (5, 3, 2560, 512),
    (0, 3, 3072, 384),
    (1, 3, 3456, 128),
    (2, 3, 3584, 256),
    (3, 3, 3840, 384),
    (5, 3, 4224, 384),
    (3, 3, 4608, 384),
    (5, 3, 4992, 384),
)
FORWARD_ORDER = (
    1, 0, 22, 43, 50, 85, 106, 113, 120, 141, 148, 155, 183, 211, 239, 176, 218, 225, 204, 232, 44,
    107, 2, 8, 15, 142, 23, 212, 29, 36, 177, 51, 226, 205, 45, 242, 3, 57, 248, 9, 16, 24, 30, 64,
    37, 52, 4, 10, 46, 17, 25, 31, 5, 58, 38, 65, 53, 11, 47, 18, 6, 26, 32, 59, 39, 71, 78, 66, 86,
    7, 12, 240, 92, 241, 19, 27, 48, 243, 99, 72, 79, 33, 87, 28, 49, 93, 54, 73, 40, 80, 88, 100,
    13, 114, 121, 34, 67, 60, 20, 94, 74, 14, 101, 21, 89, 55, 81, 244, 35, 108, 115, 41, 61, 95,
    122, 127, 56, 246, 134, 149, 75, 42, 245, 109, 68, 90, 116, 123, 62, 102, 128, 135, 156, 91,
    110, 143, 150, 63, 76, 96, 129, 136, 157, 82, 111, 144, 162, 77, 112, 151, 69, 103, 158, 117,
    145, 169, 163, 184, 70, 83, 247, 178, 97, 146, 124, 249, 170, 164, 84, 185, 250, 104, 98, 130,
    137, 152, 147, 179, 159, 251, 171, 190, 197, 219, 186, 252, 118, 125, 105, 138, 180, 253, 206,
    165, 191, 198, 254, 213, 131, 255, 119, 160, 172, 187, 181, 192, 199, 220, 126, 139, 207, 153,
    161, 166, 132, 214, 182, 140, 173, 221, 154, 193, 133, 256, 208, 233, 200, 257, 188, 215, 222,
    258, 227, 167, 174, 209, 259, 194, 201, 260, 234, 189, 216, 261, 168, 175, 262, 223, 210, 228,
    235, 217, 263, 202, 264, 195, 224, 265, 229, 203, 236, 266, 267, 196, 268, 269, 230, 270, 237,
    271, 272, 231, 273, 238, 274, 275, 276, 277,
)
SCATTER_CHUNKS = (
    (4, 0, 896),
    (4, 896, 896),
    (4, 1792, 896),
    (3, 0, 1792),
    (3, 1792, 1792),
    (3, 3584, 1792),
    (2, 0, 1024),
    (1, 0, 1024),
    (1, 1024, 1024),
    (1, 2048, 1024),
)
SCATTER_STREAMS = (
    (1, 4, 0, 128),
    (2, 4, 128, 256),
    (4, 4, 384, 384),
    (5, 4, 768, 128),
    (1, 4, 896, 128),
    (2, 4, 1024, 128),
    (3, 4, 1152, 128),
    (4, 4, 1280, 128),
    (5, 4, 1408, 384),
    (0, 4, 1792, 384),
    (1, 4, 2176, 384),
    (4, 4, 2560, 128),
    (0, 3, 0, 1152),
    (1, 3, 1152, 512),
    (3, 3, 1664, 128),
    (0, 3, 1792, 1408),
    (3, 3, 3200, 384),
    (1, 3, 3584, 1152),
    (4, 3, 4736, 128),
    (5, 3, 4864, 512),
    (0, 2, 0, 128),
    (1, 2, 128, 640),
    (4, 2, 768, 256),
    (1, 1, 0, 640),
    (3, 1, 640, 256),
    (5, 1, 896, 128),
    (0, 1, 1024, 128),
    (1, 1, 1152, 512),
    (2, 1, 1664, 128),
    (5, 1, 1792, 256),
    (0, 1, 2048, 640),
    (2, 1, 2688, 128),
    (4, 1, 2816, 256),
)
BACKWARD_ORDER = (
    31, 33, 32, 51, 57, 63, 69, 35, 34, 75, 81, 87, 93, 99, 37, 52, 58, 36, 70, 105, 111, 39, 0, 1,
    117, 64, 76, 2, 59, 82, 88, 94, 53, 38, 123, 129, 135, 3, 41, 100, 4, 71, 65, 5, 83, 89, 106,
    40, 6, 54, 72, 95, 118, 77, 147, 7, 66, 136, 8, 55, 101, 90, 96, 42, 153, 9, 60, 119, 137, 73,
    56, 84, 112, 11, 78, 102, 107, 120, 91, 148, 130, 12, 13, 61, 67, 74, 103, 141, 14, 79, 85, 97,
    92, 113, 108, 121, 124, 149, 15, 16, 62, 104, 138, 10, 17, 68, 80, 86, 131, 98, 114, 122, 109,
    165, 43, 21, 45, 19, 150, 159, 125, 44, 177, 132, 139, 154, 18, 20, 115, 110, 46, 195, 22, 126,
    133, 47, 23, 116, 142, 166, 49, 24, 151, 140, 127, 160, 171, 183, 196, 25, 134, 48, 219, 26,
    167, 128, 207, 50, 231, 237, 27, 152, 161, 155, 197, 189, 28, 168, 220, 162, 184, 238, 178, 143,
    172, 221, 156, 239, 201, 163, 169, 198, 213, 222, 243, 185, 157, 190, 173, 186, 144, 225, 164,
    202, 179, 158, 240, 170, 199, 187, 174, 208, 223, 232, 203, 145, 244, 180, 175, 214, 204, 245,
    191, 200, 241, 146, 30, 181, 176, 188, 226, 205, 209, 224, 192, 246, 215, 206, 182, 29, 227,
    233, 193, 242, 247, 210, 216, 228, 194, 248, 211, 234, 217, 229, 212, 235, 218, 230, 236,
)


def place():
    b = lax.axis_index(BATCH)
    z = lax.axis_index(SEQ)
    return b, z, b // 4, (b // 2) % 2, b % 2


def remote(src, dst, sems, i, device):
    return pltpu.make_async_remote_copy(
        src_ref=src,
        dst_ref=dst,
        send_sem=sems[0].at[i],
        recv_sem=sems[1].at[i],
        device_id=device,
        device_id_type=MESH,
    )


def piece(t, n=32):
    return pl.ds(pl.multiple_of(t * n, n), n)


def greet(direct, n_seq):
    barrier = pltpu.get_barrier_semaphore()
    b, z = lax.axis_index(BATCH), lax.axis_index(SEQ)

    def signal(device):
        pl.semaphore_signal(barrier, inc=1, device_id=device, device_id_type=MESH)

    if direct:
        for bit in (1, 2, 4):
            signal((b ^ bit, z))
    pl.when(z < n_seq - 1)(lambda: signal((b, z + 1)))
    pl.when(z > 0)(lambda: signal((b, z - 1)))
    near = (z < n_seq - 1).astype(jnp.int32) + (z > 0).astype(jnp.int32)
    return lambda: pl.semaphore_wait(barrier, near + (3 if direct else 0))


class Tasks:
    def __init__(self):
        self.steps, self.finals, self.semaphores = [], [], 0

    def take(self, count=1):
        first = self.semaphores
        self.semaphores += count
        return first

    def add(self, step):
        self.steps.append(step)

    def run(self, order):
        for i in order:
            self.steps[i]()
        for final in self.finals:
            final()


def add_gather(tasks, streams, shards, fulls, sems):
    b, z, y, x, c = place()

    def one(j, order, name, first, count):
        full, cols = fulls[name], pl.ds(first, count)
        whole = set()

        def view(at=None, other=None):
            yy = slice(None) if "y" in whole else (1 - y if other == "y" else y)
            xx = slice(None) if "x" in whole else (1 - x if other == "x" else x)
            zz = piece(z if at is None else at) if "z" not in whole else slice(None)
            return full.at[yy, xx, c, zz, cols]

        pending, sub = None, 0
        for axis in order:
            own = None if whole else shards[name].at[:, cols]
            if axis in "xy":
                i, device = tasks.take(), (b ^ (2 if axis == "x" else 4), z)
                out = remote(view() if own is None else own, view(), sems, i, device)
                into = remote(view(other=axis), view(other=axis), sems, i, device)

                def step(pending=pending, out=out):
                    if pending:
                        pending()
                    out.start()

                tasks.add(step)
                tasks.finals.append(out.wait_send)
                pending, sub = into.wait_recv, sub + 1
            else:
                for hop in range(3):
                    i = tasks.take(2)
                    has_up, has_down = (z >= hop) & (z < 3), (z + hop <= 3) & (z > 0)
                    up_piece, down_piece = jnp.maximum(z - hop, 0), jnp.minimum(z + hop, 3)
                    above, below = (b, jnp.minimum(z + 1, 3)), (b, jnp.maximum(z - 1, 0))
                    start = own if hop == 0 else None
                    up = remote(view(up_piece) if start is None else start, view(up_piece), sems, i, above)
                    down = remote(
                        view(down_piece) if start is None else start, view(down_piece), sems, i + 1, below
                    )
                    from_below, from_above = z - 1 - hop >= 0, z + 1 + hop <= 3
                    low, high = jnp.maximum(z - 1 - hop, 0), jnp.minimum(z + 1 + hop, 3)
                    rise = remote(view(low), view(low), sems, i, above)
                    fall = remote(view(high), view(high), sems, i + 1, below)

                    def step(pending=pending, up=up, down=down, has_up=has_up, has_down=has_down):
                        if pending:
                            pending()
                        pl.when(has_up)(up.start)
                        pl.when(has_down)(down.start)

                    def pending(rise=rise, fall=fall, from_below=from_below, from_above=from_above):
                        pl.when(from_below)(rise.wait_recv)
                        pl.when(from_above)(fall.wait_recv)

                    def final(up=up, down=down, has_up=has_up, has_down=has_down):
                        pl.when(has_up)(up.wait_send)
                        pl.when(has_down)(down.wait_send)

                    tasks.add(step)
                    tasks.finals.append(final)
                    sub += 1
            whole.add(axis)
        i, device = tasks.take(), (b ^ 1, z)
        out = remote(full.at[:, :, c, :, cols], full.at[:, :, c, :, cols], sems, i, device)
        into = remote(full.at[:, :, 1 - c, :, cols], full.at[:, :, 1 - c, :, cols], sems, i, device)

        def step(pending=pending, out=out):
            pending()
            out.start()

        tasks.add(step)
        tasks.add(into.wait_recv)
        tasks.finals.append(out.wait_send)

    for j, (order, which, first, count) in enumerate(streams):
        one(j, ORDERS[order], FULL[which], first, count)


def dot(a, b):
    return jnp.dot(a, b, preferred_element_type=F32)


def dot_rows(a, b):
    return lax.dot_general(a, b, (((1,), (1,)), ((), ())), preferred_element_type=F32)


def dot_columns(a, b):
    return lax.dot_general(a, b, (((0,), (0,)), ((), ())), preferred_element_type=F32)


def tile(j, n):
    return pl.ds(pl.multiple_of(j * n, n), n)


def norm_parts(values):
    center = values - jnp.mean(values, -1, keepdims=True)
    inverse = lax.rsqrt(jnp.mean(center * center, -1, keepdims=True) + NORM_EPS)
    return center * inverse, inverse


def norm_rows(source, gain, target, n=256):
    @pl.loop(0, source.shape[0] // n)
    def _(i):
        unit, _ = norm_parts(source[tile(i, n), :].astype(F32))
        target[tile(i, n), :] = (unit * gain).astype(BF)


def lanes(n):
    return lax.broadcasted_iota(jnp.int32, (n, 128), 1)


def rotate(u, cosine, sine):
    partner = jnp.where(lanes(u.shape[0]) % HDIM < HDIM // 2, pltpu.roll(u, 96, 1), pltpu.roll(u, 32, 1))
    return u * cosine + partner * sine


def pair_rows(block):
    zero, first = jnp.zeros_like(block), lanes(block.shape[0]) < HDIM
    return jnp.concatenate([jnp.where(first, block, zero), jnp.where(first, zero, block)], 0)


def weight_tile(full, cols):
    block = full[:, :, :, :, cols]
    return block.reshape(1024, block.shape[-1])


def lay_out_gains(given, square, target):
    square[...] = jnp.zeros_like(square)
    square[0:2, 0:32] = given[...].astype(F32)
    target[...] = square[...].T[:32].astype(BF)


def shifted(ref, t):
    return pltpu.roll(ref[:, t * 128 : (t + 1) * 128].astype(F32), HALF, 1)


def lay_out_wide(given, target):
    first, count = lanes(32) < HALF, FF // 128
    for t in range(count + 1):
        into = given[:, t * 128 : (t + 1) * 128].astype(F32)
        gate = jnp.where(first, shifted(given, count + t), 0.0 if t == count else shifted(given, min(count + 1 + t, 2 * count)))
        if t == count:
            into = jnp.where(first, into, 0.0)
        target[:, t * 256 : t * 256 + 128] = into.astype(BF)
        target[:, t * 256 + 128 : (t + 1) * 256] = gate.astype(BF)


def lay_out_narrow(given, target):
    even = FF // 128 * 128
    target[:, :even] = given[:, :even]
    target[:, even:] = jnp.zeros((32, PADDED - even), BF)
    target[:, even:FF] = given[:, even:]


def flip(source, target, c):
    for k in range(8):
        at = (k // 2) + 4 * jnp.where(c == k % 2, 0, 1)
        target[tile(at, 128), :] = source[:, k * 128 : (k + 1) * 128].T


def edge_exchange(tasks, sems, n_seq, up_src, up_dst, down_src, down_dst):
    b, z = lax.axis_index(BATCH), lax.axis_index(SEQ)
    i = tasks.take(2)
    up = remote(up_src, up_dst, sems, i, (b, jnp.minimum(z + 1, n_seq - 1)))
    down = remote(down_src, down_dst, sems, i + 1, (b, jnp.maximum(z - 1, 0)))

    def start():
        pl.when(z < n_seq - 1)(up.start)
        pl.when(z > 0)(down.start)

    def wait():
        pl.when(z > 0)(up.wait_recv)
        pl.when(z < n_seq - 1)(down.wait_recv)

    def final():
        pl.when(z < n_seq - 1)(up.wait_send)
        pl.when(z > 0)(down.wait_send)

    tasks.finals.append(final)
    return start, wait


HELD = ("normed", "queries", "keys", "values", "probs", "attended", "middle", "gains", "flip_normed", "flip_attended")


def forward_kernel(direct, n_seq, *refs):
    refs = list(refs)

    def pop(names):
        return {n: refs.pop(0) for n in names}

    given = pop(FULL)
    given_tokens, given_cotangent, all_cosine, all_sine, given_segments, given_padding = pop(range(6)).values()
    saved = Saved(*[refs.pop(0) for _ in Saved._fields])
    fulls = pop(FULL)
    held = pop(HELD)
    normed, queries, keys, values, probs, attended, middle, gains, flip_normed, flip_attended = held.values()
    second, flip_second, flip_cotangent, total, final, active, bias = pop(range(7)).values()
    tag_rows, tag_edge, tag_prev, tag_next, cosine, sine = pop(range(6)).values()
    tokens, cotangent, segments, padding, halo, halo_normed = pop(range(6)).values()
    expanded_ring, narrow_ring, wide_ring = pop(range(3)).values()
    shards = dict(given)
    if direct:
        square, raw_gains, raw_wide, raw_narrow = pop(range(4)).values()
        shards.update(pop("gqown"))
    send_sems, recv_sems, local_sems, ring_sems = refs
    sems = (send_sems, recv_sems)
    held.update(fulls)
    b, z, y, x, c = place() if direct else (lax.axis_index(BATCH), lax.axis_index(SEQ), 0, 0, 0)
    rows, span = 2, 256
    tasks = Tasks()
    copies = {}
    pending_moves = []

    def save(name):
        target = getattr(saved, name)
        copies[name] = pltpu.make_async_copy(held[name], target, local_sems.at[Saved._fields.index(name)])
        copies[name].start()

    exchanges = [edge_exchange(tasks, sems, n_seq, tag_edge, tag_prev, tag_edge, tag_next)]
    for r in range(rows):
        ends = (pl.ds((r + 1) * span - HALF, HALF), pl.ds(r * HALF, HALF), pl.ds(r * span, HALF))
        ends += (pl.ds((rows + r) * HALF, HALF),)
        parts = (ref.at[end] for ref, end in zip((tokens, halo, tokens, halo), ends))
        exchanges.append(edge_exchange(tasks, sems, n_seq, *parts))

    def start_edges():
        for start, _ in exchanges:
            start()

    def wait_edges():
        for _, finish in exchanges:
            finish()

    tasks.add(start_edges)
    if direct:
        add_gather(tasks, GATHER_STREAMS, shards, fulls, sems)

    def prepare():
        pending_moves.pop().wait()
        flip(cotangent, flip_cotangent, c)
        @pl.when(z == 0)
        def _():
            tag_prev[...] = jnp.zeros_like(tag_prev)
            halo[0 : rows * HALF, :] = jnp.zeros((rows * HALF, 1024), BF)

        @pl.when(z == n_seq - 1)
        def _():
            tag_next[...] = jnp.zeros_like(tag_next)
            halo[rows * HALF :, :] = jnp.zeros((rows * HALF, 1024), BF)

    def gain_rows():
        columns = weight_tile(fulls["g"], slice(None)).astype(F32)
        gains[...] = columns.T[:8]
        save("gains")

    def halo_norm():
        norm_rows(halo, gains[0:1, :], halo_normed)

    def first_norm():
        norm_rows(tokens, gains[0:1, :], normed)
        flip(normed, flip_normed, c)
        save("flip_normed")

    def project(first, count, put, done=None):
        def run():
            @pl.loop(first, first + count)
            def _(j):
                weight = weight_tile(fulls["q"], tile(j, 512))
                put(j, dot(normed[...], weight))
                if put is not put_query:
                    put(j, dot(halo_normed[...], weight), True)

            if done:
                save(done)

        return run

    def put_query(j, out):
        for part in range(4):
            for r in range(rows):
                u = out[r * span : (r + 1) * span, part * 128 : (part + 1) * 128]
                u = rotate(u, cosine[HALF : HALF + span, :], sine[HALF : HALF + span, :]) * HDIM**-0.5
                queries[r * span : (r + 1) * span, tile(4 * j + part, 128)] = u.astype(BF)

    def places(outside):
        if outside:
            ends = ((0, 0), (1, HALF + span))
            return [(r, slice((e * rows + r) * HALF, (e * rows + r + 1) * HALF), slice(at, at + HALF)) for e, at in ends for r in range(rows)]
        return [(r, slice(r * span, (r + 1) * span), slice(HALF, HALF + span)) for r in range(rows)]

    def put_key(j, out, outside=False):
        for r, here, there in places(outside):
            for part in range(4):
                u = rotate(out[here, part * 128 : (part + 1) * 128], cosine[there, :], sine[there, :])
                keys[r, there, tile(4 * (j - 2) + part, 128)] = u.astype(BF)

    def put_value(j, out, outside=False):
        for r, here, there in places(outside):
            values[r, there, tile(j - 4, 512)] = out[here].astype(BF)

    tasks.add(prepare)
    tasks.add(gain_rows)
    tasks.add(first_norm)
    tasks.add(wait_edges)
    tasks.add(halo_norm)
    tasks.add(project(0, 2, put_query))
    tasks.add(project(2, 1, put_key))
    tasks.add(project(3, 1, put_key))
    tasks.add(project(4, 2, put_value, "q"))

    def masks():
        first = lanes(8) < HALF
        low, high = (pltpu.roll(tag_rows[:, t * 128 : (t + 1) * 128], HALF, 1) for t in range(2))
        ext = (jnp.where(first, tag_prev[...], low), jnp.where(first, low, high), jnp.where(first, high, tag_next[...]))
        ext = jnp.concatenate([jnp.concatenate([t, jnp.zeros((120, 128), F32)], 0).T for t in ext], 0)
        offset = lax.broadcasted_iota(jnp.int32, (256, 128), 0) - lax.broadcasted_iota(jnp.int32, (256, 128), 1)
        band, self_pair = (offset >= 0) & (offset <= 2 * HALF), offset == HALF
        for r in range(rows):
            for k in range(2):
                query_tag = (segments[r : r + 1, k * 128 : (k + 1) * 128] + 1).astype(F32)
                same = ext[k * 128 : k * 128 + 256, r : r + 1] == query_tag
                bias[r, k] = jnp.where(band & (same | self_pair), 0.0, MASK_FILL)
    tasks.add(masks)

    def attend_block(r, k, p):
        row, window = slice(r * span + k * 128, r * span + (k + 1) * 128), slice(k * 128, k * 128 + 256)
        cols = tile(p, 128)
        scores = dot_rows(pair_rows(keys[r, window, cols]), queries[row, cols])
        parts = []
        for h in range(2):
            s = scores[h * 256 : (h + 1) * 256] + bias[r, k]
            weights = jnp.exp(s - jnp.max(s, 0, keepdims=True))
            parts.append((weights * (1.0 / jnp.sum(weights, 0, keepdims=True))).astype(BF))
        pair = jnp.concatenate(parts, 0)
        probs[r, k, p] = pair
        attended[row, cols] = dot_columns(pair, pair_rows(values[r, window, cols])).astype(BF)

    def attend(first):
        def run():
            if first == 0:
                for name in ("queries", "keys", "values"):
                    save(name)

            @pl.loop(first, first + 2)
            def _(p):
                for r in range(rows):
                    for k in range(2):
                        attend_block(r, k, p)

        return run

    for i in range(4):
        tasks.add(attend(2 * i))

    def project_out():
        @pl.loop(0, 2)
        def _(j):
            cols = tile(j, 512)
            middle[:, cols] = tokens[:, cols].astype(F32) + dot(attended[...], weight_tile(fulls["o"], cols))

        for name in ("o", "probs", "middle"):
            save(name)

    def second_norm():
        norm_rows(middle, gains[1:2, :], second)
        flip(second, flip_second, c)
        total[...] = middle[...]

    def flip_late():
        flip(attended, flip_attended, c)
        save("flip_attended")

    tasks.add(project_out)
    tasks.add(second_norm)
    tasks.add(flip_late)

    streams = {}

    def stream(name, i, source, target):
        streams[name, i] = pltpu.make_async_copy(source, target, ring_sems.at[name, i % 2])
        streams[name, i].start()

    def free(name, i):
        if (name, i) in streams:
            streams.pop((name, i)).wait()

    def gate(i):
        def run():
            free(0, i - 2)
            above = dot(cotangent[...], weight_tile(fulls["n"], pl.ds(i * 384, 384)))
            out = dot(second[...], weight_tile(fulls["w"], pl.ds(i * 768, 768)))
            for k in range(3):
                gate_in, gate_up = out[:, k * 256 : k * 256 + 128], out[:, k * 256 + 128 : (k + 1) * 256]
                mass = 0.5 * (1.0 + lax.erf(gate_in * 0.5**0.5))
                density = jnp.exp(-0.5 * gate_in * gate_in) * INV_SQRT_2PI
                gelu, up = gate_in * mass, above[:, k * 128 : (k + 1) * 128]
                slope = gate_up * (mass + gate_in * density)
                expanded_ring[i % 2, :, k * 256 : k * 256 + 128] = (up * slope).astype(BF)
                expanded_ring[i % 2, :, k * 256 + 128 : (k + 1) * 256] = (up * gelu).astype(BF)
                at = (i % 2) * 384 + k * 128
                active[:, at : at + 128] = (gelu * gate_up).astype(BF)
            cols = pl.ds(i * 768, 768)
            stream(0, i, expanded_ring.at[i % 2], saved.grad_expanded.at[:, cols])
            free(4, i - 2)
            stream(4, i, fulls["w"].at[:, :, :, :, cols], saved.w.at[:, :, :, :, cols])

        return run

    def add_output(i):
        width = 768 if i % 2 else 384
        first = (i + 1) * 384 - width

        def run():
            @pl.loop(0, 2)
            def _(j):
                block = fulls["n"][j, :, :, :, pl.ds(first, width)].reshape(512, width)
                total[:, tile(j, 512)] += dot_rows(active[:, :width], block)

            if i == 6:
                final[...] = total[...].astype(BF)
                stream(3, 0, final, saved.outputs)

        return run

    def grad_narrow(i):
        width = 768 if i % 2 else 384
        first = (i + 1) * 384 - width

        def run():
            free(1, i - 2 if i % 2 else i - 1)

            @pl.loop(0, 2)
            def _(j):
                narrow_ring[tile(j, 512), :width] = dot(flip_cotangent[tile(j, 512), :], active[:, :width]).astype(BF)

            stream(1, i, narrow_ring.at[:, pl.ds(0, width)], saved.grad_narrow.at[:, pl.ds(first, width)])

        return run

    def grad_wide(i):
        def run():
            free(2, i - 2)

            @pl.loop(0, 2)
            def _(j):
                wide_ring[i % 2, tile(j, 512), :] = dot(flip_second[tile(j, 512), :], expanded_ring[i % 2]).astype(BF)

            stream(2, i, wide_ring.at[i % 2], saved.grad_wide.at[:, pl.ds(i * 768, 768)])

        return run

    for i in range(7):
        tasks.add(gate(i))
        tasks.add(grad_wide(i))
        if i % 2 or i == 6:
            tasks.add(add_output(i))
            tasks.add(grad_narrow(i))

    base = len(Saved._fields)
    moves = [(given_segments, segments), (given_padding, padding)]
    if direct:
        moves += [(given["g"], raw_gains), (given["w"], raw_wide), (given["n"], raw_narrow)]
        moves += [(given[n], shards[n]) for n in "qo"]
    else:
        moves += [(given[n], fulls[n]) for n in FULL]
    here = pl.ds(pl.multiple_of(z * span, span), span + 2 * HALF)
    moves += [(given_tokens, tokens), (all_cosine.at[here, :], cosine), (all_sine.at[here, :], sine)]
    moves += [(given_cotangent, cotangent)]
    moves = [pltpu.make_async_copy(*move, local_sems.at[base + i]) for i, move in enumerate(moves)]
    for move in moves:
        move.start()
    arrived = greet(direct, n_seq)
    for move in moves[:-4]:
        move.wait()
    pending_moves.append(moves[-1])
    tag_rows[...] = jnp.zeros_like(tag_rows)
    tag_rows[0:rows, :] = jnp.where(padding[...] == 1, segments[...] + 1, 0).astype(F32)
    low, high = (pltpu.roll(tag_rows[:, t * 128 : (t + 1) * 128], HALF, 1) for t in range(2))
    tag_edge[...] = jnp.where(lanes(8) < HALF, high, low)
    if direct:
        lay_out_gains(raw_gains, square, shards["g"])
        lay_out_wide(raw_wide, shards["w"])
        lay_out_narrow(raw_narrow, shards["n"])
        own = [
            pltpu.make_async_copy(shards[n], fulls[n].at[y, x, c, piece(z), :], local_sems.at[base + i])
            for i, n in enumerate(FULL)
        ]
        for copy in own:
            copy.start()
        for copy in own:
            copy.wait()
    for move in moves[-4:-1]:
        move.wait()
    arrived()
    tasks.run(FORWARD_ORDER if direct else range(len(tasks.steps)))
    for copy in list(copies.values()) + list(streams.values()):
        copy.wait()


SHAPES = {
    "g": ((2, 2, 2, 128, 128), BF),
    "q": ((2, 2, 2, 128, 3072), BF),
    "o": ((2, 2, 2, 128, 1024), BF),
    "w": ((2, 2, 2, 128, 2 * PADDED), BF),
    "n": ((2, 2, 2, 128, PADDED), BF),
    "normed": ((512, 1024), BF),
    "queries": ((512, 1024), BF),
    "keys": ((2, 384, 1024), BF),
    "values": ((2, 384, 1024), BF),
    "probs": ((2, 2, 8, 512, 128), BF),
    "attended": ((512, 1024), BF),
    "middle": ((512, 1024), F32),
    "gains": ((8, 1024), F32),
    "flip_normed": ((1024, 512), BF),
    "flip_attended": ((1024, 512), BF),
    "grad_expanded": ((512, 2 * PADDED), BF),
    "grad_narrow": ((1024, PADDED), BF),
    "grad_wide": ((1024, 2 * PADDED), BF),
    "outputs": ((512, 1024), BF),
}
VMEM, ANY = pl.BlockSpec(memory_space=pltpu.VMEM), pl.BlockSpec(memory_space=pl.ANY)


def forward(direct, n_seq, shards, *inputs):
    results = Saved._fields
    count = 400 if direct else 16
    out = pl.pallas_call(
        functools.partial(forward_kernel, direct, n_seq),
        out_shape=tuple(jax.ShapeDtypeStruct(*SHAPES[n]) for n in results),
        in_specs=[ANY] * 11,
        out_specs=(ANY,) * len(results),
        scratch_shapes=[pltpu.VMEM(*SHAPES[n]) for n in FULL + HELD]
        + [
            pltpu.VMEM((512, 1024), BF),
            pltpu.VMEM((1024, 512), BF),
            pltpu.VMEM((1024, 512), BF),
            pltpu.VMEM((512, 1024), F32),
            pltpu.VMEM((512, 1024), BF),
            pltpu.VMEM((512, 768), BF),
            pltpu.VMEM((2, 2, 256, 128), F32),
            pltpu.VMEM((8, 256), F32),
            pltpu.VMEM((8, 128), F32),
            pltpu.VMEM((8, 128), F32),
            pltpu.VMEM((8, 128), F32),
            pltpu.VMEM((256 + 2 * HALF, 128), F32),
            pltpu.VMEM((256 + 2 * HALF, 128), F32),
            pltpu.VMEM((512, 1024), BF),
            pltpu.VMEM((512, 1024), BF),
            pltpu.VMEM((2, 256), jnp.int32),
            pltpu.VMEM((2, 256), jnp.int32),
            pltpu.VMEM((4 * HALF, 1024), BF),
            pltpu.VMEM((4 * HALF, 1024), BF),
            pltpu.VMEM((2, 512, 768), BF),
            pltpu.VMEM((1024, 768), BF),
            pltpu.VMEM((2, 1024, 768), BF),
            *([pltpu.VMEM((128, 128), F32), pltpu.VMEM((2, 32), BF)] if direct else []),
            *([pltpu.VMEM((32, n), BF) for n in (2 * FF, FF, 128, 3072, 1024, 2 * PADDED, PADDED)] if direct else []),
            pltpu.SemaphoreType.DMA((count,)),
            pltpu.SemaphoreType.DMA((count,)),
            pltpu.SemaphoreType.DMA((len(results) + 11,)),
            pltpu.SemaphoreType.DMA((5, 2)),
        ],
        compiler_params=pltpu.CompilerParams(collective_id=1, has_side_effects=True, vmem_limit_bytes=62 << 20),
    )(*shards, *inputs)
    return Saved(*out)


def add_into(target, a, b):
    count = target.shape[0]

    def part(i):
        at = pl.ds(pl.multiple_of(i * 32, 32), 32)
        target[at, :] = a[at, :] + b[at, :]

    if count == 32:
        part(0)
    else:
        pl.loop(0, count // 32)(part)


def landing_shapes(streams):
    result = []
    for order, _, _, count in streams:
        shapes, left, depth = {}, ["y", "x"], 128
        for axis in ORDERS[order][::-1]:
            if axis == "z":
                shapes["z"] = (2,) * len(left) + (160, count)
                depth = 32
            else:
                left.remove(axis)
                shapes[axis] = (2,) * len(left) + (depth, count)
        result.append(shapes)
    return result


def add_scatter(tasks, streams, chunks, sources, totals, slots, landed, sums, sems, credit, ready):
    b, z, y, x, c = place()
    for k, (which, first, count) in enumerate(chunks):
        name, cols = FULL[which], pl.ds(first, count)
        slot = slots.at[k % 2, :, :, :, pl.ds(0, count)]
        out = remote(sources[name].at[:, :, :, cols], slot, sems, tasks.take(), (b ^ 1, z))

        def start(k=k, out=out):
            if k >= 2:
                pl.semaphore_wait(credit.at[k % 2], 1)
            out.start()

        def arrive(k=k, out=out, name=name, cols=cols, slot=slot):
            ready(k)
            out.wait_recv()
            for yy in range(2):
                for xx in range(2):
                    total = totals[name].at[yy, xx, :, cols]
                    add_into(total, total, slot.at[yy, xx])
            if k + 2 < len(chunks):
                pl.semaphore_signal(credit.at[k % 2], inc=1, device_id=(b ^ 1, z), device_id_type=MESH)

        tasks.add(start)
        tasks.add(arrive)
        tasks.finals.append(out.wait_send)

    def one(j, order, name, first, count):
        cols, land = pl.ds(first, count), landed[j]

        def view(fixed, at=None):
            zz = fixed.get("z", slice(None)) if at is None else piece(at)
            return totals[name].at[fixed.get("y", slice(None)), fixed.get("x", slice(None)), zz, cols]

        def blocks(ref):
            if len(ref.shape) == 2:
                return [ref]
            return [r for i in range(ref.shape[0]) for r in blocks(ref.at[i])]

        def accumulate(target, source):
            for t, s in zip(blocks(target), blocks(source)):
                add_into(t, t, s)

        fixed, pending, sub = {}, None, 0
        for axis in order[::-1]:
            if axis in "xy":
                mine, device = (y if axis == "y" else x), (b ^ (2 if axis == "x" else 4), z)
                keep = dict(fixed)
                keep[axis] = mine
                give = dict(fixed)
                give[axis] = 1 - mine
                out = remote(view(give), land[axis], sems, tasks.take(), device)

                def step(pending=pending, out=out):
                    if pending:
                        pending()
                    out.start()

                def pending(out=out, keep=keep, axis=axis):
                    out.wait_recv()
                    accumulate(view(keep), land[axis])

                tasks.add(step)
                tasks.finals.append(out.wait_send)
                fixed, sub = keep, sub + 1
            else:
                left = [a for a in "yx" if a not in fixed]

                def spot(t, own_from_below):
                    at = jnp.where(own_from_below, 128, t * 32)
                    return land["z"].at[(slice(None),) * len(left) + (pl.ds(pl.multiple_of(at, 32), 32),)]

                for hop in (2, 1, 0):
                    i = tasks.take(2)
                    down_piece, up_piece = jnp.maximum(z - 1 - hop, 0), jnp.minimum(z + 1 + hop, 3)
                    has_down, has_up = z - 1 - hop >= 0, z + 1 + hop <= 3
                    below, above = (b, jnp.maximum(z - 1, 0)), (b, jnp.minimum(z + 1, 3))
                    down = remote(view(fixed, down_piece), spot(down_piece, False), sems, i, below)
                    up = remote(view(fixed, up_piece), spot(up_piece, hop == 0), sems, i + 1, above)
                    from_above, from_below = (z < 3) & (z - hop >= 0), (z > 0) & (z + hop <= 3)
                    low, high = jnp.maximum(z - hop, 0), jnp.minimum(z + hop, 3)
                    fall = remote(view(fixed, low), spot(low, False), sems, i, below)
                    rise = remote(view(fixed, high), spot(high, hop == 0), sems, i + 1, above)

                    def step(pending=pending, up=up, down=down, has_up=has_up, has_down=has_down):
                        if pending:
                            pending()
                        pl.when(has_down)(down.start)
                        pl.when(has_up)(up.start)

                    def pending(
                        fall=fall,
                        rise=rise,
                        from_above=from_above,
                        from_below=from_below,
                        low=low,
                        high=high,
                        hop=hop,
                        fixed=fixed,
                        spot=spot,
                    ):
                        @pl.when(from_above)
                        def _():
                            fall.wait_recv()
                            accumulate(view(fixed, low), spot(low, False))

                        @pl.when(from_below)
                        def _():
                            rise.wait_recv()
                            accumulate(view(fixed, high), spot(high, hop == 0))

                    def final(up=up, down=down, has_up=has_up, has_down=has_down):
                        pl.when(has_down)(down.wait_send)
                        pl.when(has_up)(up.wait_send)

                    tasks.add(step)
                    tasks.finals.append(final)
                    sub += 1
                fixed = dict(fixed)
                fixed["z"] = piece(z)

        def last(pending=pending, fixed=fixed):
            pending()
            sums[name][:, cols] = view(fixed)[...].astype(F32)

        tasks.add(last)

    for j, (order, which, first, count) in enumerate(streams):
        one(j, ORDERS[order], FULL[which], first, count)


class Scratch(NamedTuple):
    ring: Any
    expanded: Any
    second: Any
    middle: Any
    branch: Any
    flipped: Any
    keys: Any
    values: Any
    probs: Any
    projected: Any
    grad_v: Any
    edge: Any
    edge_landed: Any
    gains: Any
    cosine: Any
    sine: Any
    tokens: Any
    cotangent: Any


class Saved(NamedTuple):
    q: Any
    o: Any
    w: Any
    queries: Any
    keys: Any
    values: Any
    probs: Any
    middle: Any
    gains: Any
    flip_normed: Any
    flip_attended: Any
    grad_expanded: Any
    grad_narrow: Any
    grad_wide: Any
    outputs: Any


WEIGHTS = ("q", "o", "w", "n")


def lay_out_narrow_sum(held, narrow):
    even = FF // 128 * 128
    narrow[:, :even], narrow[:, even:] = held[:, :even], held[:, even:FF]


def lay_out_wide_sum(held, wide):
    even, first, count = FF // 128 * 128, lanes(32) < HALF, FF // 128

    def gate(t):
        return pltpu.roll(held[:, t * 256 + 128 : (t + 1) * 256], HALF, 1)

    for t in range(count):
        wide[:, t * 128 : (t + 1) * 128] = held[:, t * 256 : t * 256 + 128]
    wide[:, even : even + 128] = jnp.where(first, held[:, count * 256 : count * 256 + 128], gate(0))
    for t in range(count):
        wide[:, even + 128 + t * 128 : even + 256 + t * 128] = jnp.where(first, gate(t), gate(t + 1))


def grad_gain(weight, total, square, column):
    square[0:32, column : column + 1] = jnp.sum(weight[...].astype(F32) * total[...], -1, keepdims=True)


def backward_kernel(direct, n_seq, shapes, *refs):
    refs = list(refs)

    def pop(names):
        return {n: refs.pop(0) for n in names}

    src = Saved(*[refs.pop(0) for _ in Saved._fields])
    given_tokens, given_cotangent, all_cosine, all_sine = pop(range(4)).values()
    if direct:
        given_shards = pop(range(3)).values()
    grad_tokens = refs.pop(0)
    if direct:
        targets = list(pop(range(5)).values())
        sums = pop(WEIGHTS)
        square = refs.pop(0)
        laid_wide, laid_narrow, laid_gains, gain_pair, qkv_shard, wide_shard = pop(range(6)).values()
    else:
        sums = pop(range(4))
    totals = pop(WEIGHTS if direct else ("q", "o"))
    others = pop(("q", "o"))
    landed = [pop(s) for s in shapes]
    slots = refs.pop(0) if direct else None
    v = Scratch(*[refs.pop(0) for _ in Scratch._fields])
    cosine, sine, tokens, cotangent = v.cosine, v.sine, v.tokens, v.cotangent
    send_sems, recv_sems, local_sems, credit = refs
    sems = (send_sems, recv_sems)
    b, z, y, x, c = place() if direct else (lax.axis_index(BATCH), lax.axis_index(SEQ), 0, 0, 0)
    rows, span = 2, 256
    tasks = Tasks()
    local = {}

    def load(name, source, target):
        local[name] = pltpu.make_async_copy(source, target, local_sems.at[name])
        local[name].start()

    def wait(name):
        local.pop(name).wait()

    def load_group(i):
        cols = pl.ds(i * 768, 768)
        load(WIDE + i % 2, src.w.at[:, :, :, :, cols], v.ring.at[i % 2, :, :, :, :, pl.ds(0, 768)])
        load(EXPANDED + i % 2, src.grad_expanded.at[:, cols], v.expanded.at[i % 2])

    def grad_second(i):
        def run():
            wait(WIDE + i % 2)
            wait(EXPANDED + i % 2)

            @pl.loop(0, 2)
            def _(j):
                block = v.ring[i % 2, j, :, :, :, pl.ds(0, 768)].reshape(512, 768)
                part = dot_rows(v.expanded[i % 2], block)
                if i == 0:
                    v.second[:, tile(j, 512)] = part
                else:
                    v.second[:, tile(j, 512)] += part

            if i < 5:
                load_group(i + 2)
            elif i == 5:
                load(WIDE + 1, src.o, v.ring.at[1])
            else:
                load(WIDE, src.q.at[:, :, :, :, pl.ds(0, 1024)], v.ring.at[0])

        return run

    def load_rest():
        load_group(0)
        load_group(1)
        load(COTANGENT, given_cotangent, cotangent)
        load(MIDDLE, src.middle, v.middle)
        load(GAINS, src.gains, v.gains)
        load(QUERIES, src.queries, v.projected.at[:, pl.ds(0, 1024)])
        load(KEYS, src.keys, v.keys)
        load(VALUES, src.values, v.values)
        load(FLIPPED, src.flip_attended, v.flipped)
        for i in range(2):
            load_probs(i)
        here = pl.ds(pl.multiple_of(z * span + HALF, HALF), span)
        load(COSINE, all_cosine.at[here, :], v.cosine)
        load(SINE, all_sine.at[here, :], v.sine)
        load(TOKENS, given_tokens, tokens)
        if direct:
            for i, (given, held_here) in enumerate(zip(given_shards, (gain_pair, qkv_shard, wide_shard))):
                load(SHARD + i, given, held_here)

    tasks.add(load_rest)
    for i in range(7):
        tasks.add(grad_second(i))

    def norm_back(values, upstream, gain):
        unit, inverse = norm_parts(values)
        scaled = upstream * gain
        return inverse * (
            scaled - jnp.mean(scaled, -1, keepdims=True) - unit * jnp.mean(scaled * unit, -1, keepdims=True)
        )

    def second_norm_back():
        for name in (MIDDLE, GAINS, COTANGENT):
            wait(name)

        @pl.loop(0, 4)
        def _(i):
            at = tile(i, 128)
            grad = norm_back(v.middle[at, :], v.second[at, :], v.gains[1:2, :])
            grad = grad + cotangent[at, :].astype(F32)
            v.middle[at, :] = grad
            v.branch[at, :] = grad.astype(BF)

    tasks.add(second_norm_back)

    def back_out():
        wait(WIDE + 1)

        @pl.loop(0, 2)
        def _(j):
            cols = pl.ds(pl.multiple_of(2048 + j * 512, 512), 512)
            v.projected[:, cols] = dot_rows(v.branch[...], v.ring[1, j].reshape(512, 1024)).astype(BF)

        load(WIDE + 1, src.q.at[:, :, :, :, pl.ds(1024, 1024)], v.ring.at[1])
        for name in (QUERIES, KEYS, VALUES, COSINE, SINE):
            wait(name)

    tasks.add(back_out)

    def grad_weight(name, first, count, source):
        def run():
            if name == "o":
                wait(FLIPPED)

            @pl.loop(first, first + count)
            def _(j):
                cols = tile(j, 512)
                out = dot(v.flipped[...], source(cols)).astype(BF).reshape(2, 2, 2, 128, 512)
                totals[name][:, :, :, cols], others[name][:, :, :, cols] = out[0], out[1]

            if name == "o":
                load(FLIPPED, src.flip_normed, v.flipped)
            if name == "q" and first == 0:
                pass

        return run

    tasks.add(grad_weight("o", 0, 2, lambda cols: v.branch[:, cols]))

    def attend_back_block(r, k, p, i):
        row, window = slice(r * span + k * 128, r * span + (k + 1) * 128), slice(k * 128, k * 128 + 256)
        cols, upper = tile(p, 128), pl.ds(pl.multiple_of(2048 + p * 128, 128), 128)
        half, local_cols = i // 2, tile(p - 4 * (i // 2), 128)
        side = lanes(256) < HDIM
        upstream, pair = v.projected[row, upper], v.probs[i % 2, r, k, p - 2 * i]
        key_pair = pair_rows(v.keys[r, window, cols])
        grad_p = dot_rows(pair_rows(v.values[r, window, cols]), upstream)
        parts = []
        for h in range(2):
            part = slice(h * 256, (h + 1) * 256)
            weights = pair[part].astype(F32)
            inner = jnp.sum(grad_p[part] * weights, 0, keepdims=True)
            parts.append((weights * (grad_p[part] - inner)).astype(BF))
        grad_s = jnp.concatenate(parts, 0)
        back_v = dot(pair, upstream)
        back_k = dot(grad_s, v.projected[row, cols])
        at = slice(k * 128, (k + 1) * 128)
        grad_q = rotate(dot_columns(grad_s, key_pair) * HDIM**-0.5, cosine[at, :], -sine[at, :])
        v.projected[row, cols] = grad_q.astype(BF)
        for which, back, out in ((0, back_k, v.second), (1, back_v, v.grad_v)):
            back = jnp.where(side, back[:256], back[256:])
            if k == 0:
                v.edge[half, 0, which, r, :, local_cols] = back[:HALF].astype(BF)
                out[r * span : r * span + 192, cols] = back[HALF:]
            else:
                out[r * span + 64 : r * span + 192, cols] += back[:128]
                out[r * span + 192 : (r + 1) * span, cols] = back[128:192]
                v.edge[half, 1, which, r, :, local_cols] = back[192:].astype(BF)

    def load_probs(i):
        load(PROBS + i % 2, src.probs.at[:, :, pl.ds(2 * i, 2)], v.probs.at[i % 2])

    def attend_back(i):
        def run():
            wait(PROBS + i % 2)

            @pl.loop(2 * i, 2 * i + 2)
            def _(p):
                for k in range(2):
                    for r in range(rows):
                        attend_back_block(r, k, p, i)

            if i < 2:
                load_probs(i + 2)

        return run

    waits = []
    for i in range(4):
        tasks.add(attend_back(i))
        if i % 2:
            edge, land = v.edge.at[i // 2], v.edge_landed.at[i // 2]
            start, finish = edge_exchange(tasks, sems, n_seq, edge.at[1], land.at[0], edge.at[0], land.at[1])
            tasks.add(start)
            waits.append(finish)
    for half in range(2):
        tasks.add(waits[half])

    def turn_back(half):
        def run():
            here = slice(half * 512, (half + 1) * 512)
            for part, out in ((0, v.second), (1, v.grad_v)):
                for r in range(rows):

                    @pl.when(z > 0)
                    def _():
                        out[r * span : r * span + HALF, here] += v.edge_landed[half, 0, part, r].astype(F32)

                    @pl.when(z < n_seq - 1)
                    def _():
                        at = slice((r + 1) * span - HALF, (r + 1) * span)
                        out[at, here] += v.edge_landed[half, 1, part, r].astype(F32)

            @pl.loop(4 * half, 4 * half + 4)
            def _(p):
                cols, middle_cols, upper = (pl.ds(pl.multiple_of(f + p * 128, 128), 128) for f in (0, 1024, 2048))
                for r in range(rows):
                    at = slice(r * span, (r + 1) * span)
                    turned = rotate(v.second[at, cols], cosine[...], -sine[...])
                    v.projected[at, middle_cols] = turned.astype(BF)
                    v.projected[at, upper] = v.grad_v[at, cols].astype(BF)

        return run

    for half in range(2):
        tasks.add(turn_back(half))

    def grad_qkv(first):
        inner = grad_weight("q", first, 2, lambda cols: v.projected[:, cols])

        def run():
            if first == 0:
                wait(FLIPPED)
            inner()

        return run

    for i, letter in enumerate("abc"):
        tasks.add(grad_qkv(2 * i))

    def grad_normed(i):
        def run():
            wait(WIDE + i % 2)

            @pl.loop(0, 2)
            def _(j):
                block = v.ring[i % 2, j].reshape(512, 1024)
                part = dot_rows(v.projected[:, i * 1024 : (i + 1) * 1024], block)
                if i == 0:
                    v.grad_v[:, tile(j, 512)] = part
                else:
                    v.grad_v[:, tile(j, 512)] += part

            if i == 0:
                load(WIDE, src.q.at[:, :, :, :, pl.ds(2048, 1024)], v.ring.at[0])

        return run

    for i in range(3):
        tasks.add(grad_normed(i))

    def first_norm_back():
        wait(TOKENS)

        @pl.loop(0, 4)
        def _(i):
            at = tile(i, 128)
            grad = norm_back(tokens[at, :].astype(F32), v.grad_v[at, :], v.gains[0:1, :])
            v.branch[at, :] = (v.middle[at, :] + grad).astype(BF)

        load(RESULT, v.branch, grad_tokens)

    tasks.add(first_norm_back)
    if direct:

        def finish(name):
            if name == "o":
                load(OWN + 1, sums["o"], targets[1])
            elif name == "n":
                lay_out_narrow_sum(sums["n"], laid_narrow)
                load(OWN + 3, laid_narrow, targets[3])
            else:
                for i in range(3):
                    wait(SHARD + i)
                square[...] = jnp.zeros_like(square)
                lay_out_wide_sum(sums["w"], laid_wide)
                grad_gain(wide_shard, laid_wide, square, 1)
                load(OWN + 2, laid_wide, targets[2])

        for name in "now":
            tasks.add(functools.partial(finish, name))

        sources = dict(others)
        sources.update({n: g.at[1] for n, g in (("n", src.grad_narrow), ("w", src.grad_wide))})

        def load_total(k):
            which, first, count = SCATTER_CHUNKS[k]
            if FULL[which] in sources and FULL[which] not in others:
                cols = pl.ds(first, count)
                source = (src.grad_narrow if FULL[which] == "n" else src.grad_wide).at[0, :, :, :, cols]
                load(LOADS + k, source, totals[FULL[which]].at[:, :, :, cols])

        def ready(k):
            if LOADS + k in local:
                wait(LOADS + k)

        add_scatter(tasks, SCATTER_STREAMS, SCATTER_CHUNKS, sources, totals, slots, landed, sums, sems, credit, ready)
        load_total(0)
    if direct:
        for k in range(1, len(SCATTER_CHUNKS)):
            load_total(k)
    greet(direct, n_seq)()
    tasks.run(BACKWARD_ORDER if direct else range(len(tasks.steps)))
    if direct:
        grad_gain(qkv_shard, sums["q"], square, 0)
        laid_gains[...] = square[...].T[0:2, 0:32] / gain_pair[...].astype(F32)
        load(OWN, sums["q"], targets[0])
        load(OWN + 4, laid_gains, targets[4])
    else:
        for i, name in enumerate("qo"):
            load(OWN + i, totals[name], sums[i])
            load(OTHER + i, others[name], sums[2 + i])
    for copy in local.values():
        copy.wait()


WIDE, EXPANDED, PROBS, OWN, OTHER = 0, 2, 4, 6, 8
MIDDLE, GAINS, QUERIES, KEYS, VALUES, FLIPPED, RESULT, COSINE, SINE, TOKENS, COTANGENT, SHARD, _, _, LOADS = range(12, 27)


def backward(direct, n_seq, saved, *inputs):
    split = lambda a: a.reshape(2, 2, 2, 128, -1)
    saved = saved._replace(grad_narrow=split(saved.grad_narrow), grad_wide=split(saved.grad_wide))
    shapes = landing_shapes(SCATTER_STREAMS) if direct else []
    widths = {"q": 3072, "o": 1024, "w": 2 * PADDED, "n": PADDED}
    held = WEIGHTS if direct else ("q", "o")
    half = lambda n: (2, 2, 128, widths[n])
    if direct:
        sums = [jax.ShapeDtypeStruct(s, F32) for s in ((32, 3072), (32, 1024), (32, 2 * FF), (32, FF), (2, 32))]
    else:
        sums = [jax.ShapeDtypeStruct(half(n), BF) for n in ("q", "o", "q", "o")]
    largest = max(count for _, _, count in SCATTER_CHUNKS)
    count = 400 if direct else 16
    out = pl.pallas_call(
        functools.partial(backward_kernel, direct, n_seq, shapes),
        out_shape=(jax.ShapeDtypeStruct((512, 1024), BF), *sums),
        in_specs=[ANY] * (len(saved) + len(inputs)),
        out_specs=(ANY,) * (1 + len(sums)),
        scratch_shapes=([pltpu.VMEM((32, widths[n]), F32) for n in WEIGHTS] if direct else [])
        + ([pltpu.VMEM((128, 128), F32)] if direct else [])
        + ([pltpu.VMEM((32, n), F32) for n in (2 * FF, FF)] + [pltpu.VMEM((2, 32), F32)] if direct else [])
        + ([pltpu.VMEM((2, 32), BF)] + [pltpu.VMEM((32, n), BF) for n in (3072, 2 * FF)] if direct else [])
        + [pltpu.VMEM(half(n), BF) for n in held]
        + [pltpu.VMEM(half(n), BF) for n in ("q", "o")]
        + [pltpu.VMEM(s, BF) for stream in shapes for s in stream.values()]
        + ([pltpu.VMEM((2, 2, 2, 128, largest), BF)] if direct else [])
        + [
            pltpu.VMEM((2, 2, 2, 2, 128, 1024), BF),
            pltpu.VMEM((2, 512, 768), BF),
            pltpu.VMEM((512, 1024), F32),
            pltpu.VMEM((512, 1024), F32),
            pltpu.VMEM((512, 1024), BF),
            pltpu.VMEM((1024, 512), BF),
            pltpu.VMEM((2, 384, 1024), BF),
            pltpu.VMEM((2, 384, 1024), BF),
            pltpu.VMEM((2, 2, 2, 2, 512, 128), BF),
            pltpu.VMEM((512, 3072), BF),
            pltpu.VMEM((512, 1024), F32),
            pltpu.VMEM((2, 2, 2, 2, HALF, 512), BF),
            pltpu.VMEM((2, 2, 2, 2, HALF, 512), BF),
            pltpu.VMEM((8, 1024), F32),
            pltpu.VMEM((256, 128), F32),
            pltpu.VMEM((256, 128), F32),
            pltpu.VMEM((512, 1024), BF),
            pltpu.VMEM((512, 1024), BF),
            pltpu.SemaphoreType.DMA((count,)),
            pltpu.SemaphoreType.DMA((count,)),
            pltpu.SemaphoreType.DMA((LOADS + len(SCATTER_CHUNKS),)),
            pltpu.SemaphoreType.REGULAR((2,)),
        ],
        compiler_params=pltpu.CompilerParams(collective_id=2, has_side_effects=True, vmem_limit_bytes=63 << 20),
    )(*saved, *inputs)
    return out


def tables(length):
    frequency = np.float32(ROPE_BASE) ** (-(2.0 * np.arange(HDIM // 2, dtype=np.float32)) / np.float32(HDIM))
    angles = np.arange(-HALF, length + HALF, dtype=np.float32)[:, None] * frequency[None, :].astype(np.float32)
    cosine, sine = np.cos(angles), np.sin(angles)
    return np.concatenate([cosine] * 4, 1), np.concatenate([-sine, sine, -sine, sine], 1)


def interleave(wide):
    lead = wide.shape[0]
    wide = jnp.pad(wide.reshape(lead, 2, FF), ((0, 0), (0, 0), (0, PADDED - FF)))
    return wide.reshape(lead, 2, PADDED // 128, 128).swapaxes(1, 2).reshape(lead, 2 * PADDED)


def separate(wide):
    lead = wide.shape[0]
    wide = wide.reshape(lead, PADDED // 128, 2, 128).swapaxes(1, 2).reshape(lead, 2, PADDED)
    return wide[:, :, :FF].reshape(lead, 2 * FF)


def hand_over_kernel(*refs):
    count = (len(refs) - 2) // 3
    sources, targets, held = refs[:count], refs[count : 2 * count], refs[2 * count : 3 * count]
    arrive, leave = refs[3 * count :]
    moves = [pltpu.make_async_copy(s, h, arrive.at[i]) for i, (s, h) in enumerate(zip(sources, held))]
    for move in moves:
        move.start()
    backs = []
    for i, (h, t) in enumerate(zip(held, targets)):
        moves[i].wait()
        backs.append(pltpu.make_async_copy(h, t, leave.at[i]))
        backs[i].start()
    for back in backs:
        back.wait()


def hand_over(*arrays):
    count = len(arrays)
    return pl.pallas_call(
        hand_over_kernel,
        out_shape=tuple(jax.ShapeDtypeStruct(a.shape, a.dtype) for a in arrays),
        in_specs=[ANY] * count,
        out_specs=(ANY,) * count,
        scratch_shapes=[pltpu.VMEM(a.shape, a.dtype) for a in arrays] + [pltpu.SemaphoreType.DMA((count,))] * 2,
        compiler_params=pltpu.CompilerParams(vmem_limit_bytes=62 << 20),
    )(*arrays)


def body(
    tokens,
    segment_ids,
    padding_mask,
    qkv_weight,
    out_weight,
    wide_weight,
    narrow_weight,
    first_gain,
    second_gain,
    cotangent,
):
    row_count, span, width = tokens.shape
    count = row_count * span
    n_seq = lax.axis_size(SEQ)
    direct = (lax.axis_size(BATCH), n_seq) == (8, 4)
    gains = jnp.stack([first_gain, second_gain])
    if direct:
        shards = (gains, qkv_weight, out_weight, wide_weight, narrow_weight)
    else:
        shards = (
            jnp.pad(gains.T, ((0, 0), (0, 126))),
            qkv_weight,
            out_weight,
            interleave(wide_weight),
            jnp.pad(narrow_weight, ((0, 0), (0, PADDED - FF))),
        )
        shards = [lax.all_gather(s, (BATCH, SEQ), axis=0, tiled=True).reshape(2, 2, 2, 128, s.shape[-1]) for s in shards]
    cosine, sine = (jnp.asarray(t) for t in tables(n_seq * span))
    hidden, upstream = tokens.reshape(count, width), cotangent.reshape(count, width)
    saved = forward(direct, n_seq, shards, hidden, upstream, cosine, sine, segment_ids, padding_mask)
    if direct:
        grad_tokens, grad_qkv, grad_out, grad_wide, grad_narrow, grad_gains = backward(
            direct, n_seq, saved, hidden, upstream, cosine, sine, gains, qkv_weight, wide_weight
        )
        outputs, grad_tokens, grad_qkv, grad_out, grad_wide, grad_narrow, grad_gains = hand_over(
            saved.outputs, grad_tokens, grad_qkv, grad_out, grad_wide, grad_narrow, grad_gains
        )
        grad_first, grad_second = grad_gains[0], grad_gains[1]
    else:
        outputs = saved.outputs
        grad_tokens, own_q, own_o, other_q, other_o = backward(direct, n_seq, saved, hidden, upstream, cosine, sine)
        grads = [jnp.stack([own, other]) for own, other in ((own_q, other_q), (own_o, other_o))]
        sums = []
        for g in grads + [saved.grad_wide, saved.grad_narrow]:
            g = jnp.moveaxis(g.reshape(2, 4, 128, -1), 0, 1).reshape(width, -1)
            sums.append(lax.psum_scatter(g, (BATCH, SEQ), scatter_dimension=0, tiled=True).astype(F32))
        grad_qkv, grad_out, grad_wide, grad_narrow = sums
        grad_wide, grad_narrow = separate(grad_wide), grad_narrow[:, :FF]

        def gain_grad(weight, grad, gain):
            return jnp.sum(weight.astype(F32) * grad, 1) / gain.astype(F32)

        grad_first = gain_grad(qkv_weight, grad_qkv, first_gain)
        grad_second = gain_grad(wide_weight, grad_wide, second_gain)
    return (
        outputs.reshape(tokens.shape),
        grad_tokens.reshape(tokens.shape),
        grad_qkv,
        grad_out,
        grad_wide,
        grad_narrow,
        grad_first,
        grad_second,
    )


def solution(mesh):
    placed = (
        P(BATCH, SEQ, None),
        P(BATCH, SEQ),
        P(BATCH, SEQ),
        P((BATCH, SEQ), None),
        P((BATCH, SEQ), None),
        P((BATCH, SEQ), None),
        P((BATCH, SEQ), None),
        P((BATCH, SEQ)),
        P((BATCH, SEQ)),
        P(BATCH, SEQ, None),
    )
    return jax.shard_map(
        body,
        mesh=mesh,
        in_specs=placed,
        out_specs=(
            P(BATCH, SEQ, None),
            P(BATCH, SEQ, None),
            P((BATCH, SEQ), None),
            P((BATCH, SEQ), None),
            P((BATCH, SEQ), None),
            P((BATCH, SEQ), None),
            P((BATCH, SEQ)),
            P((BATCH, SEQ)),
        ),
        check_vma=False,
    )
```

```python
import functools
from typing import Any, NamedTuple

import jax
import jax.numpy as jnp
import numpy as np
from jax import lax
from jax.experimental import pallas as pl
from jax.experimental.pallas import tpu as pltpu
from jax.sharding import PartitionSpec as P

MESH = pl.DeviceIdType.MESH
HDIM = 64
FF = 2624
PADDED = 2688
HALF = 64
BATCH, SEQ = "batch", "seq"
ORDERS = ("zxy", "zyx", "xyz", "yxz", "xzy", "yzx")
FULL = ("g", "q", "o", "w", "n")
NORM_EPS = 1e-05
MASK_FILL = -1e30
ROPE_BASE = 10000.0
INV_SQRT_2PI = 0.3989422804014327
BF, F32 = jnp.bfloat16, jnp.float32

GATHER_STREAMS = (
    (4, 0, 0, 128),
    (0, 1, 0, 640),
    (1, 1, 640, 384),
    (0, 1, 1024, 896),
    (5, 1, 1920, 128),
    (0, 1, 2048, 256),
    (1, 1, 2304, 640),
    (2, 1, 2944, 128),
    (0, 2, 0, 128),
    (1, 2, 128, 384),
    (3, 2, 512, 128),
    (4, 2, 640, 128),
    (5, 2, 768, 256),
    (0, 4, 0, 128),
    (4, 4, 128, 512),
    (5, 4, 640, 128),
    (0, 3, 0, 128),
    (1, 3, 128, 512),
    (4, 3, 640, 640),
    (5, 3, 1280, 256),
    (1, 4, 768, 128),
    (5, 4, 896, 640),
    (0, 3, 1536, 512),
    (1, 3, 2048, 128),
    (2, 3, 2176, 512),
    (4, 3, 2688, 384),
    (0, 4, 1536, 384),
    (1, 4, 1920, 512),
    (5, 4, 2432, 256),
    (3, 3, 3072, 512),
    (4, 3, 3584, 384),
    (5, 3, 3968, 640),
    (1, 3, 4608, 128),
    (2, 3, 4736, 640),
)
FORWARD_ORDER = (
    1, 0, 239, 29, 50, 71, 78, 85, 99, 106, 127, 134, 148, 169, 197, 204, 176, 211, 218, 232, 51,
    72, 2, 8, 15, 170, 205, 22, 30, 233, 36, 43, 242, 248, 3, 9, 16, 52, 23, 31, 37, 44, 4, 10, 17,
    53, 24, 32, 38, 45, 5, 11, 18, 57, 64, 54, 79, 86, 73, 25, 6, 46, 92, 100, 55, 58, 65, 7, 240,
    241, 12, 80, 19, 87, 107, 56, 59, 243, 66, 74, 81, 113, 93, 120, 101, 88, 33, 75, 39, 26, 94,
    108, 114, 47, 128, 121, 20, 102, 34, 76, 13, 21, 109, 135, 115, 122, 35, 77, 129, 141, 149, 14,
    244, 60, 155, 40, 89, 136, 95, 130, 48, 110, 67, 142, 116, 150, 27, 61, 137, 90, 49, 162, 156,
    82, 41, 143, 96, 111, 177, 28, 245, 246, 42, 68, 62, 91, 103, 112, 151, 247, 163, 157, 171, 83,
    138, 97, 63, 249, 123, 84, 152, 164, 178, 98, 250, 183, 190, 198, 212, 69, 117, 251, 172, 104,
    131, 139, 252, 179, 184, 70, 124, 191, 118, 199, 253, 219, 105, 140, 173, 144, 254, 119, 153,
    165, 180, 255, 185, 192, 200, 158, 206, 132, 145, 154, 174, 125, 166, 193, 213, 133, 186, 220,
    159, 175, 181, 201, 207, 126, 256, 146, 257, 167, 258, 214, 147, 182, 194, 221, 259, 225, 234,
    168, 187, 260, 202, 261, 160, 215, 208, 222, 203, 161, 262, 263, 226, 188, 195, 235, 264, 265,
    209, 216, 227, 189, 266, 196, 267, 223, 228, 236, 210, 217, 268, 269, 229, 224, 270, 271, 237,
    272, 230, 273, 238, 231, 274, 275, 276, 277, 278, 279,
)
SCATTER_CHUNKS = (
    (4, 0, 896),
    (4, 896, 896),
    (4, 1792, 896),
    (3, 0, 1792),
    (3, 1792, 1792),
    (3, 3584, 1792),
    (2, 0, 1024),
    (1, 0, 1024),
    (1, 1024, 1024),
    (1, 2048, 1024),
)
SCATTER_STREAMS = (
    (1, 4, 0, 128),
    (2, 4, 128, 256),
    (4, 4, 384, 384),
    (5, 4, 768, 128),
    (1, 4, 896, 128),
    (2, 4, 1024, 128),
    (3, 4, 1152, 128),
    (4, 4, 1280, 128),
    (5, 4, 1408, 384),
    (0, 4, 1792, 384),
    (1, 4, 2176, 384),
    (4, 4, 2560, 128),
    (0, 3, 0, 1152),
    (1, 3, 1152, 512),
    (3, 3, 1664, 128),
    (0, 3, 1792, 1408),
    (3, 3, 3200, 384),
    (1, 3, 3584, 1152),
    (4, 3, 4736, 128),
    (5, 3, 4864, 512),
    (0, 2, 0, 128),
    (1, 2, 128, 640),
    (4, 2, 768, 256),
    (1, 1, 0, 640),
    (3, 1, 640, 256),
    (5, 1, 896, 128),
    (0, 1, 1024, 128),
    (1, 1, 1152, 512),
    (2, 1, 1664, 128),
    (5, 1, 1792, 256),
    (0, 1, 2048, 640),
    (2, 1, 2688, 128),
    (4, 1, 2816, 256),
)
BACKWARD_ORDER = (
    31, 33, 32, 51, 57, 63, 69, 35, 34, 75, 81, 87, 93, 99, 37, 52, 58, 36, 70, 105, 111, 39, 0, 1,
    117, 64, 76, 2, 59, 82, 88, 94, 53, 38, 123, 129, 135, 3, 41, 100, 4, 71, 65, 5, 83, 89, 106,
    40, 6, 54, 72, 95, 118, 77, 147, 7, 66, 136, 8, 55, 101, 90, 96, 42, 153, 9, 60, 119, 137, 73,
    56, 84, 112, 11, 78, 102, 107, 120, 91, 148, 130, 12, 13, 61, 67, 74, 103, 141, 14, 79, 85, 97,
    92, 113, 108, 121, 124, 149, 15, 16, 62, 104, 138, 10, 17, 68, 80, 86, 131, 98, 114, 122, 109,
    165, 43, 21, 45, 19, 150, 159, 125, 44, 177, 132, 139, 154, 18, 20, 115, 110, 46, 195, 22, 126,
    133, 47, 23, 116, 142, 166, 49, 24, 151, 140, 127, 160, 171, 183, 196, 25, 134, 48, 219, 26,
    167, 128, 207, 50, 231, 237, 27, 152, 161, 155, 197, 189, 28, 168, 220, 162, 184, 238, 178, 143,
    172, 221, 156, 239, 201, 163, 169, 198, 213, 222, 243, 185, 157, 190, 173, 186, 144, 225, 164,
    202, 179, 158, 240, 170, 199, 187, 174, 208, 223, 232, 203, 145, 244, 180, 175, 214, 204, 245,
    191, 200, 241, 146, 30, 181, 176, 188, 226, 205, 209, 224, 192, 246, 215, 206, 182, 29, 227,
    233, 193, 242, 247, 210, 216, 228, 194, 248, 211, 234, 217, 229, 212, 235, 218, 230, 236,
)


def place():
    b = lax.axis_index(BATCH)
    z = lax.axis_index(SEQ)
    return b, z, b // 4, (b // 2) % 2, b % 2


def remote(src, dst, sems, i, device):
    return pltpu.make_async_remote_copy(
        src_ref=src,
        dst_ref=dst,
        send_sem=sems[0].at[i],
        recv_sem=sems[1].at[i],
        device_id=device,
        device_id_type=MESH,
    )


def piece(t, n=32):
    return pl.ds(pl.multiple_of(t * n, n), n)


def greet(direct, n_seq):
    barrier = pltpu.get_barrier_semaphore()
    b, z = lax.axis_index(BATCH), lax.axis_index(SEQ)

    def signal(device):
        pl.semaphore_signal(barrier, inc=1, device_id=device, device_id_type=MESH)

    if direct:
        for bit in (1, 2, 4):
            signal((b ^ bit, z))
    pl.when(z < n_seq - 1)(lambda: signal((b, z + 1)))
    pl.when(z > 0)(lambda: signal((b, z - 1)))
    near = (z < n_seq - 1).astype(jnp.int32) + (z > 0).astype(jnp.int32)
    return lambda: pl.semaphore_wait(barrier, near + (3 if direct else 0))


class Tasks:
    def __init__(self):
        self.steps, self.finals, self.semaphores = [], [], 0

    def take(self, count=1):
        first = self.semaphores
        self.semaphores += count
        return first

    def add(self, step):
        self.steps.append(step)

    def run(self, order):
        for i in order:
            self.steps[i]()
        for final in self.finals:
            final()


def add_gather(tasks, streams, shards, fulls, sems):
    b, z, y, x, c = place()

    def one(j, order, name, first, count):
        full, cols = fulls[name], pl.ds(first, count)
        whole = set()

        def view(at=None, other=None):
            yy = slice(None) if "y" in whole else (1 - y if other == "y" else y)
            xx = slice(None) if "x" in whole else (1 - x if other == "x" else x)
            zz = piece(z if at is None else at) if "z" not in whole else slice(None)
            return full.at[yy, xx, c, zz, cols]

        pending, sub = None, 0
        for axis in order:
            own = None if whole else shards[name].at[:, cols]
            if axis in "xy":
                i, device = tasks.take(), (b ^ (2 if axis == "x" else 4), z)
                out = remote(view() if own is None else own, view(), sems, i, device)
                into = remote(view(other=axis), view(other=axis), sems, i, device)

                def step(pending=pending, out=out):
                    if pending:
                        pending()
                    out.start()

                tasks.add(step)
                tasks.finals.append(out.wait_send)
                pending, sub = into.wait_recv, sub + 1
            else:
                for hop in range(3):
                    i = tasks.take(2)
                    has_up, has_down = (z >= hop) & (z < 3), (z + hop <= 3) & (z > 0)
                    up_piece, down_piece = jnp.maximum(z - hop, 0), jnp.minimum(z + hop, 3)
                    above, below = (b, jnp.minimum(z + 1, 3)), (b, jnp.maximum(z - 1, 0))
                    start = own if hop == 0 else None
                    up = remote(view(up_piece) if start is None else start, view(up_piece), sems, i, above)
                    down = remote(
                        view(down_piece) if start is None else start, view(down_piece), sems, i + 1, below
                    )
                    from_below, from_above = z - 1 - hop >= 0, z + 1 + hop <= 3
                    low, high = jnp.maximum(z - 1 - hop, 0), jnp.minimum(z + 1 + hop, 3)
                    rise = remote(view(low), view(low), sems, i, above)
                    fall = remote(view(high), view(high), sems, i + 1, below)

                    def step(pending=pending, up=up, down=down, has_up=has_up, has_down=has_down):
                        if pending:
                            pending()
                        pl.when(has_up)(up.start)
                        pl.when(has_down)(down.start)

                    def pending(rise=rise, fall=fall, from_below=from_below, from_above=from_above):
                        pl.when(from_below)(rise.wait_recv)
                        pl.when(from_above)(fall.wait_recv)

                    def final(up=up, down=down, has_up=has_up, has_down=has_down):
                        pl.when(has_up)(up.wait_send)
                        pl.when(has_down)(down.wait_send)

                    tasks.add(step)
                    tasks.finals.append(final)
                    sub += 1
            whole.add(axis)
        i, device = tasks.take(), (b ^ 1, z)
        out = remote(full.at[:, :, c, :, cols], full.at[:, :, c, :, cols], sems, i, device)
        into = remote(full.at[:, :, 1 - c, :, cols], full.at[:, :, 1 - c, :, cols], sems, i, device)

        def step(pending=pending, out=out):
            pending()
            out.start()

        tasks.add(step)
        tasks.add(into.wait_recv)
        tasks.finals.append(out.wait_send)

    for j, (order, which, first, count) in enumerate(streams):
        one(j, ORDERS[order], FULL[which], first, count)


def dot(a, b):
    return jnp.dot(a, b, preferred_element_type=F32)


def dot_rows(a, b):
    return lax.dot_general(a, b, (((1,), (1,)), ((), ())), preferred_element_type=F32)


def dot_columns(a, b):
    return lax.dot_general(a, b, (((0,), (0,)), ((), ())), preferred_element_type=F32)


def tile(j, n):
    return pl.ds(pl.multiple_of(j * n, n), n)


def norm_parts(values):
    center = values - jnp.mean(values, -1, keepdims=True)
    inverse = lax.rsqrt(jnp.mean(center * center, -1, keepdims=True) + NORM_EPS)
    return center * inverse, inverse


def norm_rows(source, gain, target, n=256):
    @pl.loop(0, source.shape[0] // n)
    def _(i):
        unit, _ = norm_parts(source[tile(i, n), :].astype(F32))
        target[tile(i, n), :] = (unit * gain).astype(BF)


def lanes(n):
    return lax.broadcasted_iota(jnp.int32, (n, 128), 1)


def rotate(u, cosine, sine):
    partner = jnp.where(lanes(u.shape[0]) % HDIM < HDIM // 2, pltpu.roll(u, 96, 1), pltpu.roll(u, 32, 1))
    return u * cosine + partner * sine


def pair_rows(block):
    zero, first = jnp.zeros_like(block), lanes(block.shape[0]) < HDIM
    return jnp.concatenate([jnp.where(first, block, zero), jnp.where(first, zero, block)], 0)


def weight_tile(full, cols):
    block = full[:, :, :, :, cols]
    return block.reshape(1024, block.shape[-1])


def lay_out_gains(given, square, target):
    square[...] = jnp.zeros_like(square)
    for i, row in enumerate(given):
        square[i : i + 1, 0:32] = row[...].astype(F32)
    target[...] = square[...].T[:32].astype(BF)


def shifted(ref, t):
    return pltpu.roll(ref[:, t * 128 : (t + 1) * 128].astype(F32), HALF, 1)


def lay_out_wide(given, target):
    first, count = lanes(32) < HALF, FF // 128
    for t in range(count + 1):
        into = given[:, t * 128 : (t + 1) * 128].astype(F32)
        gate = jnp.where(first, shifted(given, count + t), 0.0 if t == count else shifted(given, min(count + 1 + t, 2 * count)))
        if t == count:
            into = jnp.where(first, into, 0.0)
        target[:, t * 256 : t * 256 + 128] = into.astype(BF)
        target[:, t * 256 + 128 : (t + 1) * 256] = gate.astype(BF)


def lay_out_narrow(given, target):
    even = FF // 128 * 128
    target[:, :even] = given[:, :even]
    target[:, even:] = jnp.zeros((32, PADDED - even), BF)
    target[:, even:FF] = given[:, even:]


def flip(source, target, c):
    for k in range(8):
        at = (k // 2) + 4 * jnp.where(c == k % 2, 0, 1)
        target[tile(at, 128), :] = source[:, k * 128 : (k + 1) * 128].T


def edge_exchange(tasks, sems, n_seq, up_src, up_dst, down_src, down_dst):
    b, z = lax.axis_index(BATCH), lax.axis_index(SEQ)
    i = tasks.take(2)
    up = remote(up_src, up_dst, sems, i, (b, jnp.minimum(z + 1, n_seq - 1)))
    down = remote(down_src, down_dst, sems, i + 1, (b, jnp.maximum(z - 1, 0)))

    def start():
        pl.when(z < n_seq - 1)(up.start)
        pl.when(z > 0)(down.start)

    def wait():
        pl.when(z > 0)(up.wait_recv)
        pl.when(z < n_seq - 1)(down.wait_recv)

    def final():
        pl.when(z < n_seq - 1)(up.wait_send)
        pl.when(z > 0)(down.wait_send)

    tasks.finals.append(final)
    return start, wait


HELD = ("normed", "queries", "keys", "values", "probs", "attended", "middle", "gains", "flip_normed", "flip_attended")


GROUPS = ((0, 3), (3, 3), (6, 3), (9, 3), (12, 3), (15, 3), (18, 2), (20, 1))


def forward_kernel(direct, n_seq, *refs):
    refs = list(refs)

    def pop(names):
        return {n: refs.pop(0) for n in names}

    given = pop(FULL)
    given_tokens, given_cotangent, all_cosine, all_sine, given_segments, given_padding, second_gain = pop(range(7)).values()
    saved = Saved(*[refs.pop(0) for _ in Saved._fields])
    fulls = pop(FULL)
    held = pop(HELD)
    normed, queries, keys, values, probs, attended, middle, gains, flip_normed, flip_attended = held.values()
    second, flip_second, flip_cotangent, total, final, active, bias = pop(range(7)).values()
    tag_rows, tag_edge, tag_prev, tag_next, cosine, sine = pop(range(6)).values()
    tokens, cotangent, segments, padding, halo, halo_normed = pop(range(6)).values()
    expanded_ring, narrow_ring, wide_ring = pop(range(3)).values()
    shards = dict(given)
    if direct:
        square, raw_first, raw_second, raw_wide, raw_narrow = pop(range(5)).values()
        shards.update(pop("gqown"))
    send_sems, recv_sems, local_sems, ring_sems = refs
    sems = (send_sems, recv_sems)
    held.update(fulls)
    b, z, y, x, c = place() if direct else (lax.axis_index(BATCH), lax.axis_index(SEQ), 0, 0, 0)
    rows, span = 2, 256
    tasks = Tasks()
    copies = {}
    pending_moves = []

    def save(name):
        target = getattr(saved, name)
        copies[name] = pltpu.make_async_copy(held[name], target, local_sems.at[Saved._fields.index(name)])
        copies[name].start()

    exchanges = [edge_exchange(tasks, sems, n_seq, tag_edge, tag_prev, tag_edge, tag_next)]
    for r in range(rows):
        ends = (pl.ds((r + 1) * span - HALF, HALF), pl.ds(r * HALF, HALF), pl.ds(r * span, HALF))
        ends += (pl.ds((rows + r) * HALF, HALF),)
        parts = (ref.at[end] for ref, end in zip((tokens, halo, tokens, halo), ends))
        exchanges.append(edge_exchange(tasks, sems, n_seq, *parts))

    def start_edges():
        for start, _ in exchanges:
            start()

    def wait_edges():
        for _, finish in exchanges:
            finish()

    tasks.add(start_edges)
    if direct:
        add_gather(tasks, GATHER_STREAMS, shards, fulls, sems)

    def prepare():
        pending_moves.pop().wait()
        flip(cotangent, flip_cotangent, c)
        @pl.when(z == 0)
        def _():
            tag_prev[...] = jnp.zeros_like(tag_prev)
            halo[0 : rows * HALF, :] = jnp.zeros((rows * HALF, 1024), BF)

        @pl.when(z == n_seq - 1)
        def _():
            tag_next[...] = jnp.zeros_like(tag_next)
            halo[rows * HALF :, :] = jnp.zeros((rows * HALF, 1024), BF)

    def gain_rows():
        columns = weight_tile(fulls["g"], slice(None)).astype(F32)
        gains[...] = columns.T[:8]
        save("gains")

    def halo_norm():
        norm_rows(halo, gains[0:1, :], halo_normed)

    def first_norm():
        norm_rows(tokens, gains[0:1, :], normed)
        flip(normed, flip_normed, c)
        save("flip_normed")

    def project(first, count, put, done=None):
        def run():
            @pl.loop(first, first + count)
            def _(j):
                weight = weight_tile(fulls["q"], tile(j, 512))
                put(j, dot(normed[...], weight))
                if put is not put_query:
                    put(j, dot(halo_normed[...], weight), True)

            if done:
                save(done)

        return run

    def put_query(j, out):
        for part in range(4):
            for r in range(rows):
                u = out[r * span : (r + 1) * span, part * 128 : (part + 1) * 128]
                u = rotate(u, cosine[HALF : HALF + span, :], sine[HALF : HALF + span, :]) * HDIM**-0.5
                queries[r * span : (r + 1) * span, tile(4 * j + part, 128)] = u.astype(BF)

    def places(outside):
        if outside:
            ends = ((0, 0), (1, HALF + span))
            return [(r, slice((e * rows + r) * HALF, (e * rows + r + 1) * HALF), slice(at, at + HALF)) for e, at in ends for r in range(rows)]
        return [(r, slice(r * span, (r + 1) * span), slice(HALF, HALF + span)) for r in range(rows)]

    def put_key(j, out, outside=False):
        for r, here, there in places(outside):
            for part in range(4):
                u = rotate(out[here, part * 128 : (part + 1) * 128], cosine[there, :], sine[there, :])
                keys[r, there, tile(4 * (j - 2) + part, 128)] = u.astype(BF)

    def put_value(j, out, outside=False):
        for r, here, there in places(outside):
            values[r, there, tile(j - 4, 512)] = out[here].astype(BF)

    tasks.add(prepare)
    tasks.add(gain_rows)
    tasks.add(first_norm)
    tasks.add(wait_edges)
    tasks.add(halo_norm)
    tasks.add(project(0, 2, put_query))
    tasks.add(project(2, 1, put_key))
    tasks.add(project(3, 1, put_key))
    tasks.add(project(4, 2, put_value, "q"))

    def masks():
        first = lanes(8) < HALF
        low, high = (pltpu.roll(tag_rows[:, t * 128 : (t + 1) * 128], HALF, 1) for t in range(2))
        ext = (jnp.where(first, tag_prev[...], low), jnp.where(first, low, high), jnp.where(first, high, tag_next[...]))
        ext = jnp.concatenate([jnp.concatenate([t, jnp.zeros((120, 128), F32)], 0).T for t in ext], 0)
        offset = lax.broadcasted_iota(jnp.int32, (256, 128), 0) - lax.broadcasted_iota(jnp.int32, (256, 128), 1)
        band, self_pair = (offset >= 0) & (offset <= 2 * HALF), offset == HALF
        for r in range(rows):
            for k in range(2):
                query_tag = (segments[r : r + 1, k * 128 : (k + 1) * 128] + 1).astype(F32)
                same = ext[k * 128 : k * 128 + 256, r : r + 1] == query_tag
                bias[r, k] = jnp.where(band & (same | self_pair), 0.0, MASK_FILL)
    tasks.add(masks)

    def attend_block(r, k, p):
        row, window = slice(r * span + k * 128, r * span + (k + 1) * 128), slice(k * 128, k * 128 + 256)
        cols = tile(p, 128)
        scores = dot_rows(pair_rows(keys[r, window, cols]), queries[row, cols])
        parts = []
        for h in range(2):
            s = scores[h * 256 : (h + 1) * 256] + bias[r, k]
            weights = jnp.exp(s - jnp.max(s, 0, keepdims=True))
            parts.append((weights * (1.0 / jnp.sum(weights, 0, keepdims=True))).astype(BF))
        pair = jnp.concatenate(parts, 0)
        probs[r, k, p] = pair
        attended[row, cols] = dot_columns(pair, pair_rows(values[r, window, cols])).astype(BF)

    def attend(first):
        def run():
            if first == 0:
                for name in ("queries", "keys", "values"):
                    save(name)

            @pl.loop(first, first + 2)
            def _(p):
                for r in range(rows):
                    for k in range(2):
                        attend_block(r, k, p)

        return run

    for i in range(4):
        tasks.add(attend(2 * i))

    def project_out():
        @pl.loop(0, 2)
        def _(j):
            cols = tile(j, 512)
            middle[:, cols] = tokens[:, cols].astype(F32) + dot(attended[...], weight_tile(fulls["o"], cols))

        for name in ("o", "probs", "middle"):
            save(name)

    def second_norm():
        norm_rows(middle, gains[1:2, :], second)
        flip(second, flip_second, c)
        total[...] = middle[...]

    def flip_late():
        flip(attended, flip_attended, c)
        save("flip_attended")

    tasks.add(project_out)
    tasks.add(second_norm)
    tasks.add(flip_late)

    streams = {}

    def stream(name, i, source, target):
        streams[name, i] = pltpu.make_async_copy(source, target, ring_sems.at[name, i % 2])
        streams[name, i].start()

    def free(name, i):
        if (name, i) in streams:
            streams.pop((name, i)).wait()

    def gate(i):
        pair, pairs = GROUPS[i]

        def run():
            free(0, i - 2)
            above = dot(cotangent[...], weight_tile(fulls["n"], pl.ds(pair * 128, pairs * 128)))
            out = dot(second[...], weight_tile(fulls["w"], pl.ds(pair * 256, pairs * 256)))
            for k in range(pairs):
                gate_in, gate_up = out[:, k * 256 : k * 256 + 128], out[:, k * 256 + 128 : (k + 1) * 256]
                mass = 0.5 * (1.0 + lax.erf(gate_in * 0.5**0.5))
                density = jnp.exp(-0.5 * gate_in * gate_in) * INV_SQRT_2PI
                gelu, up = gate_in * mass, above[:, k * 128 : (k + 1) * 128]
                slope = gate_up * (mass + gate_in * density)
                expanded_ring[i % 2, :, k * 256 : k * 256 + 128] = (up * slope).astype(BF)
                expanded_ring[i % 2, :, k * 256 + 128 : (k + 1) * 256] = (up * gelu).astype(BF)
                at = (i % 2) * GROUPS[i - 1][1] * 128 + k * 128
                active[:, at : at + 128] = (gelu * gate_up).astype(BF)
            cols = pl.ds(pair * 256, pairs * 256)
            stream(0, i, expanded_ring.at[i % 2, :, pl.ds(0, pairs * 256)], saved.grad_expanded.at[:, cols])
            free(4, i - 2)
            stream(4, i, fulls["w"].at[:, :, :, :, cols], saved.w.at[:, :, :, :, cols])

        return run

    def add_output(i):
        first, width = GROUPS[i - 1][0] * 128, (GROUPS[i - 1][1] + GROUPS[i][1]) * 128

        def run():
            @pl.loop(0, 2)
            def _(j):
                block = fulls["n"][j, :, :, :, pl.ds(first, width)].reshape(512, width)
                total[:, tile(j, 512)] += dot_rows(active[:, :width], block)

            if i == len(GROUPS) - 1:
                final[...] = total[...].astype(BF)
                stream(3, 0, final, saved.outputs)

        return run

    def grad_narrow(i):
        first, width = GROUPS[i - 1][0] * 128, (GROUPS[i - 1][1] + GROUPS[i][1]) * 128

        def run():
            free(1, i - 2)

            @pl.loop(0, 2)
            def _(j):
                narrow_ring[tile(j, 512), :width] = dot(flip_cotangent[tile(j, 512), :], active[:, :width]).astype(BF)

            stream(1, i, narrow_ring.at[:, pl.ds(0, width)], saved.grad_narrow.at[:, pl.ds(first, width)])

        return run

    def grad_wide(i):
        width = GROUPS[i][1] * 256

        def run():
            free(2, i - 2)

            @pl.loop(0, 2)
            def _(j):
                out = dot(flip_second[tile(j, 512), :], expanded_ring[i % 2, :, :width])
                wide_ring[i % 2, tile(j, 512), :width] = out.astype(BF)

            source = wide_ring.at[i % 2, :, pl.ds(0, width)]
            stream(2, i, source, saved.grad_wide.at[:, pl.ds(GROUPS[i][0] * 256, width)])

        return run

    for i in range(len(GROUPS)):
        tasks.add(gate(i))
        tasks.add(grad_wide(i))
        if i % 2:
            tasks.add(add_output(i))
            tasks.add(grad_narrow(i))

    base = len(Saved._fields)
    moves = [(given_segments, segments), (given_padding, padding)]
    if direct:
        moves += [(given["g"], raw_first), (second_gain, raw_second), (given["w"], raw_wide), (given["n"], raw_narrow)]
        moves += [(given[n], shards[n]) for n in "qo"]
    else:
        moves += [(given[n], fulls[n]) for n in FULL]
    here = pl.ds(pl.multiple_of(z * span, span), span + 2 * HALF)
    moves += [(given_tokens, tokens), (all_cosine.at[here, :], cosine), (all_sine.at[here, :], sine)]
    moves += [(given_cotangent, cotangent)]
    moves = [pltpu.make_async_copy(*move, local_sems.at[base + i]) for i, move in enumerate(moves)]
    for move in moves:
        move.start()
    arrived = greet(direct, n_seq)
    for move in moves[:-4]:
        move.wait()
    pending_moves.append(moves[-1])
    tag_rows[...] = jnp.zeros_like(tag_rows)
    tag_rows[0:rows, :] = jnp.where(padding[...] == 1, segments[...] + 1, 0).astype(F32)
    low, high = (pltpu.roll(tag_rows[:, t * 128 : (t + 1) * 128], HALF, 1) for t in range(2))
    tag_edge[...] = jnp.where(lanes(8) < HALF, high, low)
    if direct:
        lay_out_gains((raw_first, raw_second), square, shards["g"])
        lay_out_wide(raw_wide, shards["w"])
        lay_out_narrow(raw_narrow, shards["n"])
        own = [
            pltpu.make_async_copy(shards[n], fulls[n].at[y, x, c, piece(z), :], local_sems.at[base + i])
            for i, n in enumerate(FULL)
        ]
        for copy in own:
            copy.start()
        for copy in own:
            copy.wait()
    for move in moves[-4:-1]:
        move.wait()
    arrived()
    tasks.run(FORWARD_ORDER if direct else range(len(tasks.steps)))
    for copy in list(copies.values()) + list(streams.values()):
        copy.wait()


SHAPES = {
    "g": ((2, 2, 2, 128, 128), BF),
    "q": ((2, 2, 2, 128, 3072), BF),
    "o": ((2, 2, 2, 128, 1024), BF),
    "w": ((2, 2, 2, 128, 2 * PADDED), BF),
    "n": ((2, 2, 2, 128, PADDED), BF),
    "normed": ((512, 1024), BF),
    "queries": ((512, 1024), BF),
    "keys": ((2, 384, 1024), BF),
    "values": ((2, 384, 1024), BF),
    "probs": ((2, 2, 8, 512, 128), BF),
    "attended": ((512, 1024), BF),
    "middle": ((512, 1024), F32),
    "gains": ((8, 1024), F32),
    "flip_normed": ((1024, 512), BF),
    "flip_attended": ((1024, 512), BF),
    "grad_expanded": ((512, 2 * PADDED), BF),
    "grad_narrow": ((1024, PADDED), BF),
    "grad_wide": ((1024, 2 * PADDED), BF),
    "outputs": ((512, 1024), BF),
}
VMEM, ANY = pl.BlockSpec(memory_space=pltpu.VMEM), pl.BlockSpec(memory_space=pl.ANY)


def forward(direct, n_seq, shards, *inputs):
    results = Saved._fields
    count = 400 if direct else 16
    out = pl.pallas_call(
        functools.partial(forward_kernel, direct, n_seq),
        out_shape=tuple(jax.ShapeDtypeStruct(*SHAPES[n]) for n in results),
        in_specs=[ANY] * 12,
        out_specs=(ANY,) * len(results),
        scratch_shapes=[pltpu.VMEM(*SHAPES[n]) for n in FULL + HELD]
        + [
            pltpu.VMEM((512, 1024), BF),
            pltpu.VMEM((1024, 512), BF),
            pltpu.VMEM((1024, 512), BF),
            pltpu.VMEM((512, 1024), F32),
            pltpu.VMEM((512, 1024), BF),
            pltpu.VMEM((512, 768), BF),
            pltpu.VMEM((2, 2, 256, 128), F32),
            pltpu.VMEM((8, 256), F32),
            pltpu.VMEM((8, 128), F32),
            pltpu.VMEM((8, 128), F32),
            pltpu.VMEM((8, 128), F32),
            pltpu.VMEM((256 + 2 * HALF, 128), F32),
            pltpu.VMEM((256 + 2 * HALF, 128), F32),
            pltpu.VMEM((512, 1024), BF),
            pltpu.VMEM((512, 1024), BF),
            pltpu.VMEM((2, 256), jnp.int32),
            pltpu.VMEM((2, 256), jnp.int32),
            pltpu.VMEM((4 * HALF, 1024), BF),
            pltpu.VMEM((4 * HALF, 1024), BF),
            pltpu.VMEM((2, 512, 768), BF),
            pltpu.VMEM((1024, 768), BF),
            pltpu.VMEM((2, 1024, 768), BF),
            *([pltpu.VMEM((128, 128), F32), pltpu.VMEM((1, 32), BF), pltpu.VMEM((1, 32), BF)] if direct else []),
            *([pltpu.VMEM((32, n), BF) for n in (2 * FF, FF, 128, 3072, 1024, 2 * PADDED, PADDED)] if direct else []),
            pltpu.SemaphoreType.DMA((count,)),
            pltpu.SemaphoreType.DMA((count,)),
            pltpu.SemaphoreType.DMA((len(results) + 12,)),
            pltpu.SemaphoreType.DMA((5, 2)),
        ],
        compiler_params=pltpu.CompilerParams(collective_id=1, has_side_effects=True, vmem_limit_bytes=62 << 20),
    )(*shards, *inputs)
    return Saved(*out)


def add_into(target, a, b):
    count = target.shape[0]

    def part(i):
        at = pl.ds(pl.multiple_of(i * 32, 32), 32)
        target[at, :] = a[at, :] + b[at, :]

    if count == 32:
        part(0)
    else:
        pl.loop(0, count // 32)(part)


def landing_shapes(streams):
    result = []
    for order, _, _, count in streams:
        shapes, left, depth = {}, ["y", "x"], 128
        for axis in ORDERS[order][::-1]:
            if axis == "z":
                shapes["z"] = (2,) * len(left) + (160, count)
                depth = 32
            else:
                left.remove(axis)
                shapes[axis] = (2,) * len(left) + (depth, count)
        result.append(shapes)
    return result


def add_scatter(tasks, streams, chunks, sources, totals, slots, landed, sums, sems, credit, ready):
    b, z, y, x, c = place()
    for k, (which, first, count) in enumerate(chunks):
        name, cols = FULL[which], pl.ds(first, count)
        slot = slots.at[k % 2, :, :, :, pl.ds(0, count)]
        out = remote(sources[name].at[:, :, :, cols], slot, sems, tasks.take(), (b ^ 1, z))

        def start(k=k, out=out):
            if k >= 2:
                pl.semaphore_wait(credit.at[k % 2], 1)
            out.start()

        def arrive(k=k, out=out, name=name, cols=cols, slot=slot):
            ready(k)
            out.wait_recv()
            for yy in range(2):
                for xx in range(2):
                    total = totals[name].at[yy, xx, :, cols]
                    add_into(total, total, slot.at[yy, xx])
            if k + 2 < len(chunks):
                pl.semaphore_signal(credit.at[k % 2], inc=1, device_id=(b ^ 1, z), device_id_type=MESH)

        tasks.add(start)
        tasks.add(arrive)
        tasks.finals.append(out.wait_send)

    def one(j, order, name, first, count):
        cols, land = pl.ds(first, count), landed[j]

        def view(fixed, at=None):
            zz = fixed.get("z", slice(None)) if at is None else piece(at)
            return totals[name].at[fixed.get("y", slice(None)), fixed.get("x", slice(None)), zz, cols]

        def blocks(ref):
            if len(ref.shape) == 2:
                return [ref]
            return [r for i in range(ref.shape[0]) for r in blocks(ref.at[i])]

        def accumulate(target, source):
            for t, s in zip(blocks(target), blocks(source)):
                add_into(t, t, s)

        fixed, pending, sub = {}, None, 0
        for axis in order[::-1]:
            if axis in "xy":
                mine, device = (y if axis == "y" else x), (b ^ (2 if axis == "x" else 4), z)
                keep = dict(fixed)
                keep[axis] = mine
                give = dict(fixed)
                give[axis] = 1 - mine
                out = remote(view(give), land[axis], sems, tasks.take(), device)

                def step(pending=pending, out=out):
                    if pending:
                        pending()
                    out.start()

                def pending(out=out, keep=keep, axis=axis):
                    out.wait_recv()
                    accumulate(view(keep), land[axis])

                tasks.add(step)
                tasks.finals.append(out.wait_send)
                fixed, sub = keep, sub + 1
            else:
                left = [a for a in "yx" if a not in fixed]

                def spot(t, own_from_below):
                    at = jnp.where(own_from_below, 128, t * 32)
                    return land["z"].at[(slice(None),) * len(left) + (pl.ds(pl.multiple_of(at, 32), 32),)]

                for hop in (2, 1, 0):
                    i = tasks.take(2)
                    down_piece, up_piece = jnp.maximum(z - 1 - hop, 0), jnp.minimum(z + 1 + hop, 3)
                    has_down, has_up = z - 1 - hop >= 0, z + 1 + hop <= 3
                    below, above = (b, jnp.maximum(z - 1, 0)), (b, jnp.minimum(z + 1, 3))
                    down = remote(view(fixed, down_piece), spot(down_piece, False), sems, i, below)
                    up = remote(view(fixed, up_piece), spot(up_piece, hop == 0), sems, i + 1, above)
                    from_above, from_below = (z < 3) & (z - hop >= 0), (z > 0) & (z + hop <= 3)
                    low, high = jnp.maximum(z - hop, 0), jnp.minimum(z + hop, 3)
                    fall = remote(view(fixed, low), spot(low, False), sems, i, below)
                    rise = remote(view(fixed, high), spot(high, hop == 0), sems, i + 1, above)

                    def step(pending=pending, up=up, down=down, has_up=has_up, has_down=has_down):
                        if pending:
                            pending()
                        pl.when(has_down)(down.start)
                        pl.when(has_up)(up.start)

                    def pending(
                        fall=fall,
                        rise=rise,
                        from_above=from_above,
                        from_below=from_below,
                        low=low,
                        high=high,
                        hop=hop,
                        fixed=fixed,
                        spot=spot,
                    ):
                        @pl.when(from_above)
                        def _():
                            fall.wait_recv()
                            accumulate(view(fixed, low), spot(low, False))

                        @pl.when(from_below)
                        def _():
                            rise.wait_recv()
                            accumulate(view(fixed, high), spot(high, hop == 0))

                    def final(up=up, down=down, has_up=has_up, has_down=has_down):
                        pl.when(has_down)(down.wait_send)
                        pl.when(has_up)(up.wait_send)

                    tasks.add(step)
                    tasks.finals.append(final)
                    sub += 1
                fixed = dict(fixed)
                fixed["z"] = piece(z)

        def last(pending=pending, fixed=fixed):
            pending()
            sums[name][:, cols] = view(fixed)[...].astype(F32)

        tasks.add(last)

    for j, (order, which, first, count) in enumerate(streams):
        one(j, ORDERS[order], FULL[which], first, count)


class Scratch(NamedTuple):
    ring: Any
    expanded: Any
    second: Any
    middle: Any
    branch: Any
    flipped: Any
    keys: Any
    values: Any
    probs: Any
    projected: Any
    grad_v: Any
    edge: Any
    edge_landed: Any
    gains: Any
    cosine: Any
    sine: Any
    tokens: Any
    cotangent: Any


class Saved(NamedTuple):
    q: Any
    o: Any
    w: Any
    queries: Any
    keys: Any
    values: Any
    probs: Any
    middle: Any
    gains: Any
    flip_normed: Any
    flip_attended: Any
    grad_expanded: Any
    grad_narrow: Any
    grad_wide: Any
    outputs: Any


WEIGHTS = ("q", "o", "w", "n")


def lay_out_narrow_sum(held, narrow):
    even = FF // 128 * 128
    narrow[:, :even], narrow[:, even:] = held[:, :even], held[:, even:FF]


def lay_out_wide_sum(held, wide):
    even, first, count = FF // 128 * 128, lanes(32) < HALF, FF // 128

    def gate(t):
        return pltpu.roll(held[:, t * 256 + 128 : (t + 1) * 256], HALF, 1)

    for t in range(count):
        wide[:, t * 128 : (t + 1) * 128] = held[:, t * 256 : t * 256 + 128]
    wide[:, even : even + 128] = jnp.where(first, held[:, count * 256 : count * 256 + 128], gate(0))
    for t in range(count):
        wide[:, even + 128 + t * 128 : even + 256 + t * 128] = jnp.where(first, gate(t), gate(t + 1))


def grad_gain(weight, total, square, column):
    square[0:32, column : column + 1] = jnp.sum(weight[...].astype(F32) * total[...], -1, keepdims=True)


def backward_kernel(direct, n_seq, shapes, *refs):
    refs = list(refs)

    def pop(names):
        return {n: refs.pop(0) for n in names}

    src = Saved(*[refs.pop(0) for _ in Saved._fields])
    given_tokens, given_cotangent, all_cosine, all_sine = pop(range(4)).values()
    if direct:
        given_shards = list(pop(range(4)).values())
    grad_tokens = refs.pop(0)
    if direct:
        targets = list(pop(range(6)).values())
        sums = pop(WEIGHTS)
        square = refs.pop(0)
        laid_wide, laid_narrow, laid_first, laid_second, *own_shards = pop(range(8)).values()
        gain_one, gain_two, qkv_shard, wide_shard = own_shards
    else:
        sums = pop(range(4))
    totals = pop(WEIGHTS if direct else ("q", "o"))
    others = pop(("q", "o"))
    landed = [pop(s) for s in shapes]
    slots = refs.pop(0) if direct else None
    v = Scratch(*[refs.pop(0) for _ in Scratch._fields])
    cosine, sine, tokens, cotangent = v.cosine, v.sine, v.tokens, v.cotangent
    send_sems, recv_sems, local_sems, credit = refs
    sems = (send_sems, recv_sems)
    b, z, y, x, c = place() if direct else (lax.axis_index(BATCH), lax.axis_index(SEQ), 0, 0, 0)
    rows, span = 2, 256
    tasks = Tasks()
    local = {}

    def load(name, source, target):
        local[name] = pltpu.make_async_copy(source, target, local_sems.at[name])
        local[name].start()

    def wait(name):
        local.pop(name).wait()

    def load_group(i):
        cols = pl.ds(i * 768, 768)
        load(WIDE + i % 2, src.w.at[:, :, :, :, cols], v.ring.at[i % 2, :, :, :, :, pl.ds(0, 768)])
        load(EXPANDED + i % 2, src.grad_expanded.at[:, cols], v.expanded.at[i % 2])

    def grad_second(i):
        def run():
            wait(WIDE + i % 2)
            wait(EXPANDED + i % 2)

            @pl.loop(0, 2)
            def _(j):
                block = v.ring[i % 2, j, :, :, :, pl.ds(0, 768)].reshape(512, 768)
                part = dot_rows(v.expanded[i % 2], block)
                if i == 0:
                    v.second[:, tile(j, 512)] = part
                else:
                    v.second[:, tile(j, 512)] += part

            if i < 5:
                load_group(i + 2)
            elif i == 5:
                load(WIDE + 1, src.o, v.ring.at[1])
            else:
                load(WIDE, src.q.at[:, :, :, :, pl.ds(0, 1024)], v.ring.at[0])

        return run

    def load_rest():
        load_group(0)
        load_group(1)
        load(COTANGENT, given_cotangent, cotangent)
        load(MIDDLE, src.middle, v.middle)
        load(GAINS, src.gains, v.gains)
        load(QUERIES, src.queries, v.projected.at[:, pl.ds(0, 1024)])
        load(KEYS, src.keys, v.keys)
        load(VALUES, src.values, v.values)
        load(FLIPPED, src.flip_attended, v.flipped)
        for i in range(2):
            load_probs(i)
        here = pl.ds(pl.multiple_of(z * span + HALF, HALF), span)
        load(COSINE, all_cosine.at[here, :], v.cosine)
        load(SINE, all_sine.at[here, :], v.sine)
        load(TOKENS, given_tokens, tokens)
        if direct:
            for i, (given, held_here) in enumerate(zip(given_shards, own_shards)):
                load(SHARD + i, given, held_here)

    tasks.add(load_rest)
    for i in range(7):
        tasks.add(grad_second(i))

    def norm_back(values, upstream, gain):
        unit, inverse = norm_parts(values)
        scaled = upstream * gain
        return inverse * (
            scaled - jnp.mean(scaled, -1, keepdims=True) - unit * jnp.mean(scaled * unit, -1, keepdims=True)
        )

    def second_norm_back():
        for name in (MIDDLE, GAINS, COTANGENT):
            wait(name)

        @pl.loop(0, 4)
        def _(i):
            at = tile(i, 128)
            grad = norm_back(v.middle[at, :], v.second[at, :], v.gains[1:2, :])
            grad = grad + cotangent[at, :].astype(F32)
            v.middle[at, :] = grad
            v.branch[at, :] = grad.astype(BF)

    tasks.add(second_norm_back)

    def back_out():
        wait(WIDE + 1)

        @pl.loop(0, 2)
        def _(j):
            cols = pl.ds(pl.multiple_of(2048 + j * 512, 512), 512)
            v.projected[:, cols] = dot_rows(v.branch[...], v.ring[1, j].reshape(512, 1024)).astype(BF)

        load(WIDE + 1, src.q.at[:, :, :, :, pl.ds(1024, 1024)], v.ring.at[1])
        for name in (QUERIES, KEYS, VALUES, COSINE, SINE):
            wait(name)

    tasks.add(back_out)

    def grad_weight(name, first, count, source):
        def run():
            if name == "o":
                wait(FLIPPED)

            @pl.loop(first, first + count)
            def _(j):
                cols = tile(j, 512)
                out = dot(v.flipped[...], source(cols)).astype(BF).reshape(2, 2, 2, 128, 512)
                totals[name][:, :, :, cols], others[name][:, :, :, cols] = out[0], out[1]

            if name == "o":
                load(FLIPPED, src.flip_normed, v.flipped)
            if name == "q" and first == 0:
                pass

        return run

    tasks.add(grad_weight("o", 0, 2, lambda cols: v.branch[:, cols]))

    def attend_back_block(r, k, p, i):
        row, window = slice(r * span + k * 128, r * span + (k + 1) * 128), slice(k * 128, k * 128 + 256)
        cols, upper = tile(p, 128), pl.ds(pl.multiple_of(2048 + p * 128, 128), 128)
        half, local_cols = i // 2, tile(p - 4 * (i // 2), 128)
        side = lanes(256) < HDIM
        upstream, pair = v.projected[row, upper], v.probs[i % 2, r, k, p - 2 * i]
        key_pair = pair_rows(v.keys[r, window, cols])
        grad_p = dot_rows(pair_rows(v.values[r, window, cols]), upstream)
        parts = []
        for h in range(2):
            part = slice(h * 256, (h + 1) * 256)
            weights = pair[part].astype(F32)
            inner = jnp.sum(grad_p[part] * weights, 0, keepdims=True)
            parts.append((weights * (grad_p[part] - inner)).astype(BF))
        grad_s = jnp.concatenate(parts, 0)
        back_v = dot(pair, upstream)
        back_k = dot(grad_s, v.projected[row, cols])
        at = slice(k * 128, (k + 1) * 128)
        grad_q = rotate(dot_columns(grad_s, key_pair) * HDIM**-0.5, cosine[at, :], -sine[at, :])
        v.projected[row, cols] = grad_q.astype(BF)
        for which, back, out in ((0, back_k, v.second), (1, back_v, v.grad_v)):
            back = jnp.where(side, back[:256], back[256:])
            if k == 0:
                v.edge[half, 0, which, r, :, local_cols] = back[:HALF].astype(BF)
                out[r * span : r * span + 192, cols] = back[HALF:]
            else:
                out[r * span + 64 : r * span + 192, cols] += back[:128]
                out[r * span + 192 : (r + 1) * span, cols] = back[128:192]
                v.edge[half, 1, which, r, :, local_cols] = back[192:].astype(BF)

    def load_probs(i):
        load(PROBS + i % 2, src.probs.at[:, :, pl.ds(2 * i, 2)], v.probs.at[i % 2])

    def attend_back(i):
        def run():
            wait(PROBS + i % 2)

            @pl.loop(2 * i, 2 * i + 2)
            def _(p):
                for k in range(2):
                    for r in range(rows):
                        attend_back_block(r, k, p, i)

            if i < 2:
                load_probs(i + 2)

        return run

    waits = []
    for i in range(4):
        tasks.add(attend_back(i))
        if i % 2:
            edge, land = v.edge.at[i // 2], v.edge_landed.at[i // 2]
            start, finish = edge_exchange(tasks, sems, n_seq, edge.at[1], land.at[0], edge.at[0], land.at[1])
            tasks.add(start)
            waits.append(finish)
    for half in range(2):
        tasks.add(waits[half])

    def turn_back(half):
        def run():
            here = slice(half * 512, (half + 1) * 512)
            for part, out in ((0, v.second), (1, v.grad_v)):
                for r in range(rows):

                    @pl.when(z > 0)
                    def _():
                        out[r * span : r * span + HALF, here] += v.edge_landed[half, 0, part, r].astype(F32)

                    @pl.when(z < n_seq - 1)
                    def _():
                        at = slice((r + 1) * span - HALF, (r + 1) * span)
                        out[at, here] += v.edge_landed[half, 1, part, r].astype(F32)

            @pl.loop(4 * half, 4 * half + 4)
            def _(p):
                cols, middle_cols, upper = (pl.ds(pl.multiple_of(f + p * 128, 128), 128) for f in (0, 1024, 2048))
                for r in range(rows):
                    at = slice(r * span, (r + 1) * span)
                    turned = rotate(v.second[at, cols], cosine[...], -sine[...])
                    v.projected[at, middle_cols] = turned.astype(BF)
                    v.projected[at, upper] = v.grad_v[at, cols].astype(BF)

        return run

    for half in range(2):
        tasks.add(turn_back(half))

    def grad_qkv(first):
        inner = grad_weight("q", first, 2, lambda cols: v.projected[:, cols])

        def run():
            if first == 0:
                wait(FLIPPED)
            inner()

        return run

    for i, letter in enumerate("abc"):
        tasks.add(grad_qkv(2 * i))

    def grad_normed(i):
        def run():
            wait(WIDE + i % 2)

            @pl.loop(0, 2)
            def _(j):
                block = v.ring[i % 2, j].reshape(512, 1024)
                part = dot_rows(v.projected[:, i * 1024 : (i + 1) * 1024], block)
                if i == 0:
                    v.grad_v[:, tile(j, 512)] = part
                else:
                    v.grad_v[:, tile(j, 512)] += part

            if i == 0:
                load(WIDE, src.q.at[:, :, :, :, pl.ds(2048, 1024)], v.ring.at[0])

        return run

    for i in range(3):
        tasks.add(grad_normed(i))

    def first_norm_back():
        wait(TOKENS)

        @pl.loop(0, 4)
        def _(i):
            at = tile(i, 128)
            grad = norm_back(tokens[at, :].astype(F32), v.grad_v[at, :], v.gains[0:1, :])
            v.branch[at, :] = (v.middle[at, :] + grad).astype(BF)

        load(RESULT, v.branch, grad_tokens)

    tasks.add(first_norm_back)
    if direct:

        def finish(name):
            if name == "o":
                load(OWN + 1, sums["o"], targets[1])
            elif name == "n":
                lay_out_narrow_sum(sums["n"], laid_narrow)
                load(OWN + 3, laid_narrow, targets[3])
            else:
                for i in range(4):
                    wait(SHARD + i)
                square[...] = jnp.zeros_like(square)
                lay_out_wide_sum(sums["w"], laid_wide)
                grad_gain(wide_shard, laid_wide, square, 1)
                load(OWN + 2, laid_wide, targets[2])

        for name in "now":
            tasks.add(functools.partial(finish, name))

        sources = dict(others)
        sources.update({n: g.at[1] for n, g in (("n", src.grad_narrow), ("w", src.grad_wide))})

        def load_total(k):
            which, first, count = SCATTER_CHUNKS[k]
            if FULL[which] in sources and FULL[which] not in others:
                cols = pl.ds(first, count)
                source = (src.grad_narrow if FULL[which] == "n" else src.grad_wide).at[0, :, :, :, cols]
                load(LOADS + k, source, totals[FULL[which]].at[:, :, :, cols])

        def ready(k):
            if LOADS + k in local:
                wait(LOADS + k)

        add_scatter(tasks, SCATTER_STREAMS, SCATTER_CHUNKS, sources, totals, slots, landed, sums, sems, credit, ready)
        load_total(0)
    if direct:
        for k in range(1, len(SCATTER_CHUNKS)):
            load_total(k)
    greet(direct, n_seq)()
    tasks.run(BACKWARD_ORDER if direct else range(len(tasks.steps)))
    if direct:
        grad_gain(qkv_shard, sums["q"], square, 0)
        columns = square[...].T
        laid_first[...] = columns[0:1, 0:32] / gain_one[...].astype(F32)
        laid_second[...] = columns[1:2, 0:32] / gain_two[...].astype(F32)
        load(OWN, sums["q"], targets[0])
        load(OWN + 4, laid_first, targets[4])
        load(OWN + 5, laid_second, targets[5])
    else:
        for i, name in enumerate("qo"):
            load(OWN + i, totals[name], sums[i])
            load(OTHER + i, others[name], sums[2 + i])
    for copy in local.values():
        copy.wait()


WIDE, EXPANDED, PROBS, OWN, OTHER = 0, 2, 4, 6, 8
MIDDLE, GAINS, QUERIES, KEYS, VALUES, FLIPPED, RESULT, COSINE, SINE, TOKENS, COTANGENT, SHARD, _, _, _, LOADS = range(12, 28)


def backward(direct, n_seq, saved, *inputs):
    split = lambda a: a.reshape(2, 2, 2, 128, -1)
    saved = saved._replace(grad_narrow=split(saved.grad_narrow), grad_wide=split(saved.grad_wide))
    shapes = landing_shapes(SCATTER_STREAMS) if direct else []
    widths = {"q": 3072, "o": 1024, "w": 2 * PADDED, "n": PADDED}
    held = WEIGHTS if direct else ("q", "o")
    half = lambda n: (2, 2, 128, widths[n])
    if direct:
        sums = [jax.ShapeDtypeStruct(s, F32) for s in ((32, 3072), (32, 1024), (32, 2 * FF), (32, FF), (1, 32), (1, 32))]
    else:
        sums = [jax.ShapeDtypeStruct(half(n), BF) for n in ("q", "o", "q", "o")]
    largest = max(count for _, _, count in SCATTER_CHUNKS)
    count = 400 if direct else 16
    out = pl.pallas_call(
        functools.partial(backward_kernel, direct, n_seq, shapes),
        out_shape=(jax.ShapeDtypeStruct((512, 1024), BF), *sums),
        in_specs=[ANY] * (len(saved) + len(inputs)),
        out_specs=(ANY,) * (1 + len(sums)),
        scratch_shapes=([pltpu.VMEM((32, widths[n]), F32) for n in WEIGHTS] if direct else [])
        + ([pltpu.VMEM((128, 128), F32)] if direct else [])
        + ([pltpu.VMEM((32, n), F32) for n in (2 * FF, FF)] + [pltpu.VMEM((1, 32), F32)] * 2 if direct else [])
        + ([pltpu.VMEM((1, 32), BF)] * 2 + [pltpu.VMEM((32, n), BF) for n in (3072, 2 * FF)] if direct else [])
        + [pltpu.VMEM(half(n), BF) for n in held]
        + [pltpu.VMEM(half(n), BF) for n in ("q", "o")]
        + [pltpu.VMEM(s, BF) for stream in shapes for s in stream.values()]
        + ([pltpu.VMEM((2, 2, 2, 128, largest), BF)] if direct else [])
        + [
            pltpu.VMEM((2, 2, 2, 2, 128, 1024), BF),
            pltpu.VMEM((2, 512, 768), BF),
            pltpu.VMEM((512, 1024), F32),
            pltpu.VMEM((512, 1024), F32),
            pltpu.VMEM((512, 1024), BF),
            pltpu.VMEM((1024, 512), BF),
            pltpu.VMEM((2, 384, 1024), BF),
            pltpu.VMEM((2, 384, 1024), BF),
            pltpu.VMEM((2, 2, 2, 2, 512, 128), BF),
            pltpu.VMEM((512, 3072), BF),
            pltpu.VMEM((512, 1024), F32),
            pltpu.VMEM((2, 2, 2, 2, HALF, 512), BF),
            pltpu.VMEM((2, 2, 2, 2, HALF, 512), BF),
            pltpu.VMEM((8, 1024), F32),
            pltpu.VMEM((256, 128), F32),
            pltpu.VMEM((256, 128), F32),
            pltpu.VMEM((512, 1024), BF),
            pltpu.VMEM((512, 1024), BF),
            pltpu.SemaphoreType.DMA((count,)),
            pltpu.SemaphoreType.DMA((count,)),
            pltpu.SemaphoreType.DMA((LOADS + len(SCATTER_CHUNKS),)),
            pltpu.SemaphoreType.REGULAR((2,)),
        ],
        compiler_params=pltpu.CompilerParams(collective_id=2, has_side_effects=True, vmem_limit_bytes=63 << 20),
    )(*saved, *inputs)
    return out


def tables(length):
    frequency = np.float32(ROPE_BASE) ** (-(2.0 * np.arange(HDIM // 2, dtype=np.float32)) / np.float32(HDIM))
    angles = np.arange(-HALF, length + HALF, dtype=np.float32)[:, None] * frequency[None, :].astype(np.float32)
    cosine, sine = np.cos(angles), np.sin(angles)
    return np.concatenate([cosine] * 4, 1), np.concatenate([-sine, sine, -sine, sine], 1)


def interleave(wide):
    lead = wide.shape[0]
    wide = jnp.pad(wide.reshape(lead, 2, FF), ((0, 0), (0, 0), (0, PADDED - FF)))
    return wide.reshape(lead, 2, PADDED // 128, 128).swapaxes(1, 2).reshape(lead, 2 * PADDED)


def separate(wide):
    lead = wide.shape[0]
    wide = wide.reshape(lead, PADDED // 128, 2, 128).swapaxes(1, 2).reshape(lead, 2, PADDED)
    return wide[:, :, :FF].reshape(lead, 2 * FF)


def hand_over_kernel(*refs):
    count = (len(refs) - 2) // 3
    sources, targets, held = refs[:count], refs[count : 2 * count], refs[2 * count : 3 * count]
    arrive, leave = refs[3 * count :]
    moves = [pltpu.make_async_copy(s, h, arrive.at[i]) for i, (s, h) in enumerate(zip(sources, held))]
    for move in moves:
        move.start()
    backs = []
    for i, (h, t) in enumerate(zip(held, targets)):
        moves[i].wait()
        backs.append(pltpu.make_async_copy(h, t, leave.at[i]))
        backs[i].start()
    for back in backs:
        back.wait()


def hand_over(*arrays):
    count = len(arrays)
    return pl.pallas_call(
        hand_over_kernel,
        out_shape=tuple(jax.ShapeDtypeStruct(a.shape, a.dtype) for a in arrays),
        in_specs=[ANY] * count,
        out_specs=(ANY,) * count,
        scratch_shapes=[pltpu.VMEM(a.shape, a.dtype) for a in arrays] + [pltpu.SemaphoreType.DMA((count,))] * 2,
        compiler_params=pltpu.CompilerParams(vmem_limit_bytes=62 << 20),
    )(*arrays)


def body(
    tokens,
    segment_ids,
    padding_mask,
    qkv_weight,
    out_weight,
    wide_weight,
    narrow_weight,
    first_gain,
    second_gain,
    cotangent,
):
    row_count, span, width = tokens.shape
    count = row_count * span
    n_seq = lax.axis_size(SEQ)
    direct = (lax.axis_size(BATCH), n_seq) == (8, 4)
    gains = jnp.stack([first_gain, second_gain])
    gain_rows = (first_gain.reshape(1, -1), second_gain.reshape(1, -1))
    if direct:
        shards = (gain_rows[0], qkv_weight, out_weight, wide_weight, narrow_weight)
    else:
        shards = (
            jnp.pad(gains.T, ((0, 0), (0, 126))),
            qkv_weight,
            out_weight,
            interleave(wide_weight),
            jnp.pad(narrow_weight, ((0, 0), (0, PADDED - FF))),
        )
        shards = [lax.all_gather(s, (BATCH, SEQ), axis=0, tiled=True).reshape(2, 2, 2, 128, s.shape[-1]) for s in shards]
    cosine, sine = (jnp.asarray(t) for t in tables(n_seq * span))
    hidden, upstream = tokens.reshape(count, width), cotangent.reshape(count, width)
    saved = forward(direct, n_seq, shards, hidden, upstream, cosine, sine, segment_ids, padding_mask, gain_rows[1])
    if direct:
        grad_tokens, *weight_grads = backward(
            direct, n_seq, saved, hidden, upstream, cosine, sine, *gain_rows, qkv_weight, wide_weight
        )
        outputs, grad_tokens, grad_qkv, grad_out, grad_wide, grad_narrow, grad_first, grad_second = hand_over(
            saved.outputs, grad_tokens, *weight_grads
        )
        grad_first, grad_second = grad_first.reshape(-1), grad_second.reshape(-1)
    else:
        outputs = saved.outputs
        grad_tokens, own_q, own_o, other_q, other_o = backward(direct, n_seq, saved, hidden, upstream, cosine, sine)
        grads = [jnp.stack([own, other]) for own, other in ((own_q, other_q), (own_o, other_o))]
        sums = []
        for g in grads + [saved.grad_wide, saved.grad_narrow]:
            g = jnp.moveaxis(g.reshape(2, 4, 128, -1), 0, 1).reshape(width, -1)
            sums.append(lax.psum_scatter(g, (BATCH, SEQ), scatter_dimension=0, tiled=True).astype(F32))
        grad_qkv, grad_out, grad_wide, grad_narrow = sums
        grad_wide, grad_narrow = separate(grad_wide), grad_narrow[:, :FF]

        def gain_grad(weight, grad, gain):
            return jnp.sum(weight.astype(F32) * grad, 1) / gain.astype(F32)

        grad_first = gain_grad(qkv_weight, grad_qkv, first_gain)
        grad_second = gain_grad(wide_weight, grad_wide, second_gain)
    return (
        outputs.reshape(tokens.shape),
        grad_tokens.reshape(tokens.shape),
        grad_qkv,
        grad_out,
        grad_wide,
        grad_narrow,
        grad_first,
        grad_second,
    )


def solution(mesh):
    placed = (
        P(BATCH, SEQ, None),
        P(BATCH, SEQ),
        P(BATCH, SEQ),
        P((BATCH, SEQ), None),
        P((BATCH, SEQ), None),
        P((BATCH, SEQ), None),
        P((BATCH, SEQ), None),
        P((BATCH, SEQ)),
        P((BATCH, SEQ)),
        P(BATCH, SEQ, None),
    )
    return jax.shard_map(
        body,
        mesh=mesh,
        in_specs=placed,
        out_specs=(
            P(BATCH, SEQ, None),
            P(BATCH, SEQ, None),
            P((BATCH, SEQ), None),
            P((BATCH, SEQ), None),
            P((BATCH, SEQ), None),
            P((BATCH, SEQ), None),
            P((BATCH, SEQ)),
            P((BATCH, SEQ)),
        ),
        check_vma=False,
    )
```

```python
import functools
from typing import Any, NamedTuple

import jax
import jax.numpy as jnp
import numpy as np
from jax import lax
from jax.experimental import pallas as pl
from jax.experimental.pallas import tpu as pltpu
from jax.sharding import PartitionSpec as P

MESH = pl.DeviceIdType.MESH
HDIM = 64
FF = 2624
PADDED = 2688
HALF = 64
BATCH, SEQ = "batch", "seq"
ORDERS = ("zxy", "zyx", "xyz", "yxz", "xzy", "yzx")
FULL = ("g", "q", "o", "w", "n")
NORM_EPS = 1e-05
MASK_FILL = -1e30
ROPE_BASE = 10000.0
INV_SQRT_2PI = 0.3989422804014327
BF, F32 = jnp.bfloat16, jnp.float32

GATHER_STREAMS = (
    (4, 0, 0, 128),
    (0, 1, 0, 640),
    (1, 1, 640, 384),
    (0, 1, 1024, 896),
    (5, 1, 1920, 128),
    (0, 1, 2048, 256),
    (1, 1, 2304, 640),
    (2, 1, 2944, 128),
    (0, 2, 0, 128),
    (1, 2, 128, 384),
    (3, 2, 512, 128),
    (4, 2, 640, 128),
    (5, 2, 768, 256),
    (0, 4, 0, 128),
    (4, 4, 128, 512),
    (5, 4, 640, 128),
    (0, 3, 0, 128),
    (1, 3, 128, 512),
    (4, 3, 640, 640),
    (5, 3, 1280, 256),
    (1, 4, 768, 128),
    (5, 4, 896, 640),
    (0, 3, 1536, 512),
    (1, 3, 2048, 128),
    (2, 3, 2176, 512),
    (4, 3, 2688, 384),
    (0, 4, 1536, 384),
    (1, 4, 1920, 512),
    (5, 4, 2432, 256),
    (3, 3, 3072, 512),
    (4, 3, 3584, 384),
    (5, 3, 3968, 640),
    (1, 3, 4608, 128),
    (2, 3, 4736, 640),
)
FORWARD_ORDER = (
    1, 0, 239, 29, 50, 71, 78, 85, 99, 106, 127, 134, 148, 169, 197, 204, 176, 211, 218, 232, 51,
    72, 2, 8, 15, 170, 205, 22, 30, 233, 36, 43, 242, 248, 3, 9, 16, 52, 23, 31, 37, 44, 4, 10, 17,
    53, 24, 32, 38, 45, 5, 11, 18, 57, 64, 54, 79, 86, 73, 25, 6, 46, 92, 100, 55, 58, 65, 7, 240,
    241, 12, 80, 19, 87, 107, 56, 59, 243, 66, 74, 81, 113, 93, 120, 101, 88, 33, 75, 39, 26, 94,
    108, 114, 47, 128, 121, 20, 102, 34, 76, 13, 21, 109, 135, 115, 122, 35, 77, 129, 141, 149, 14,
    244, 60, 155, 40, 89, 136, 95, 130, 48, 110, 67, 142, 116, 150, 27, 61, 137, 90, 49, 162, 156,
    82, 41, 143, 96, 111, 177, 28, 245, 246, 42, 68, 62, 91, 103, 112, 151, 247, 163, 157, 171, 83,
    138, 97, 63, 249, 123, 84, 152, 164, 178, 98, 250, 183, 190, 198, 212, 69, 117, 251, 172, 104,
    131, 139, 252, 179, 184, 70, 124, 191, 118, 199, 253, 219, 105, 140, 173, 144, 254, 119, 153,
    165, 180, 255, 185, 192, 200, 158, 206, 132, 145, 154, 174, 125, 166, 193, 213, 133, 186, 220,
    159, 175, 181, 201, 207, 126, 256, 146, 257, 167, 258, 214, 147, 182, 194, 221, 259, 225, 234,
    168, 187, 260, 202, 261, 160, 215, 208, 222, 203, 161, 262, 263, 226, 188, 195, 235, 264, 265,
    209, 216, 227, 189, 266, 196, 267, 223, 228, 236, 210, 217, 268, 269, 229, 224, 270, 271, 237,
    272, 230, 273, 238, 231, 274, 275, 276, 277, 278, 279,
)
SCATTER_CHUNKS = (
    (4, 0, 896),
    (4, 896, 896),
    (4, 1792, 896),
    (3, 0, 1792),
    (3, 1792, 1792),
    (3, 3584, 1792),
    (2, 0, 1024),
    (1, 0, 1024),
    (1, 1024, 1024),
    (1, 2048, 1024),
)
SCATTER_STREAMS = (
    (1, 4, 0, 128),
    (2, 4, 128, 256),
    (4, 4, 384, 384),
    (5, 4, 768, 128),
    (1, 4, 896, 128),
    (2, 4, 1024, 128),
    (3, 4, 1152, 128),
    (4, 4, 1280, 128),
    (5, 4, 1408, 384),
    (0, 4, 1792, 384),
    (1, 4, 2176, 384),
    (4, 4, 2560, 128),
    (0, 3, 0, 1152),
    (1, 3, 1152, 512),
    (3, 3, 1664, 128),
    (0, 3, 1792, 1408),
    (3, 3, 3200, 384),
    (1, 3, 3584, 1152),
    (4, 3, 4736, 128),
    (5, 3, 4864, 512),
    (0, 2, 0, 128),
    (1, 2, 128, 640),
    (4, 2, 768, 256),
    (1, 1, 0, 640),
    (3, 1, 640, 256),
    (5, 1, 896, 128),
    (0, 1, 1024, 128),
    (1, 1, 1152, 512),
    (2, 1, 1664, 128),
    (5, 1, 1792, 256),
    (0, 1, 2048, 640),
    (2, 1, 2688, 128),
    (4, 1, 2816, 256),
)
BACKWARD_ORDER = (
    31, 33, 32, 51, 57, 63, 69, 35, 34, 75, 81, 87, 93, 99, 37, 52, 58, 36, 70, 105, 111, 39, 0, 1,
    117, 64, 76, 2, 59, 82, 88, 94, 53, 38, 123, 129, 135, 3, 41, 100, 4, 71, 65, 5, 83, 89, 106,
    40, 6, 54, 72, 95, 118, 77, 147, 7, 66, 136, 8, 55, 101, 90, 96, 42, 153, 9, 60, 119, 137, 73,
    56, 84, 112, 11, 78, 102, 107, 120, 91, 148, 130, 12, 13, 61, 67, 74, 103, 141, 14, 79, 85, 97,
    92, 113, 108, 121, 124, 149, 15, 16, 62, 104, 138, 10, 17, 68, 80, 86, 131, 98, 114, 122, 109,
    165, 43, 21, 45, 19, 150, 159, 125, 44, 177, 132, 139, 154, 18, 20, 115, 110, 46, 195, 22, 126,
    133, 47, 23, 116, 142, 166, 49, 24, 151, 140, 127, 160, 171, 183, 196, 25, 134, 48, 219, 26,
    167, 128, 207, 50, 231, 237, 27, 152, 161, 155, 197, 189, 28, 168, 220, 162, 184, 238, 178, 143,
    172, 221, 156, 239, 201, 163, 169, 198, 213, 222, 243, 185, 157, 190, 173, 186, 144, 225, 164,
    202, 179, 158, 240, 170, 199, 187, 174, 208, 223, 232, 203, 145, 244, 180, 175, 214, 204, 245,
    191, 200, 241, 146, 30, 181, 176, 188, 226, 205, 209, 224, 192, 246, 215, 206, 182, 29, 227,
    233, 193, 242, 247, 210, 216, 228, 194, 248, 211, 234, 217, 229, 212, 235, 218, 230, 236,
)


def place():
    b = lax.axis_index(BATCH)
    z = lax.axis_index(SEQ)
    return b, z, b // 4, (b // 2) % 2, b % 2


def remote(src, dst, sems, i, device):
    return pltpu.make_async_remote_copy(
        src_ref=src,
        dst_ref=dst,
        send_sem=sems[0].at[i],
        recv_sem=sems[1].at[i],
        device_id=device,
        device_id_type=MESH,
    )


def piece(t, n=32):
    return pl.ds(pl.multiple_of(t * n, n), n)


def greet(direct, n_seq):
    barrier = pltpu.get_barrier_semaphore()
    b, z = lax.axis_index(BATCH), lax.axis_index(SEQ)

    def signal(device):
        pl.semaphore_signal(barrier, inc=1, device_id=device, device_id_type=MESH)

    if direct:
        for bit in (1, 2, 4):
            signal((b ^ bit, z))
    pl.when(z < n_seq - 1)(lambda: signal((b, z + 1)))
    pl.when(z > 0)(lambda: signal((b, z - 1)))
    near = (z < n_seq - 1).astype(jnp.int32) + (z > 0).astype(jnp.int32)
    return lambda: pl.semaphore_wait(barrier, near + (3 if direct else 0))


class Tasks:
    def __init__(self):
        self.steps, self.finals, self.semaphores = [], [], 0

    def take(self, count=1):
        first = self.semaphores
        self.semaphores += count
        return first

    def add(self, step):
        self.steps.append(step)

    def run(self, order):
        for i in order:
            self.steps[i]()
        for final in self.finals:
            final()


def add_gather(tasks, streams, shards, fulls, sems):
    b, z, y, x, c = place()

    def one(j, order, name, first, count):
        full, cols = fulls[name], pl.ds(first, count)
        whole = set()

        def view(at=None, other=None):
            yy = slice(None) if "y" in whole else (1 - y if other == "y" else y)
            xx = slice(None) if "x" in whole else (1 - x if other == "x" else x)
            zz = piece(z if at is None else at) if "z" not in whole else slice(None)
            return full.at[yy, xx, c, zz, cols]

        pending, sub = None, 0
        for axis in order:
            own = None if whole else shards[name].at[:, cols]
            if axis in "xy":
                i, device = tasks.take(), (b ^ (2 if axis == "x" else 4), z)
                out = remote(view() if own is None else own, view(), sems, i, device)
                into = remote(view(other=axis), view(other=axis), sems, i, device)

                def step(pending=pending, out=out):
                    if pending:
                        pending()
                    out.start()

                tasks.add(step)
                tasks.finals.append(out.wait_send)
                pending, sub = into.wait_recv, sub + 1
            else:
                for hop in range(3):
                    i = tasks.take(2)
                    has_up, has_down = (z >= hop) & (z < 3), (z + hop <= 3) & (z > 0)
                    up_piece, down_piece = jnp.maximum(z - hop, 0), jnp.minimum(z + hop, 3)
                    above, below = (b, jnp.minimum(z + 1, 3)), (b, jnp.maximum(z - 1, 0))
                    start = own if hop == 0 else None
                    up = remote(view(up_piece) if start is None else start, view(up_piece), sems, i, above)
                    down = remote(
                        view(down_piece) if start is None else start, view(down_piece), sems, i + 1, below
                    )
                    from_below, from_above = z - 1 - hop >= 0, z + 1 + hop <= 3
                    low, high = jnp.maximum(z - 1 - hop, 0), jnp.minimum(z + 1 + hop, 3)
                    rise = remote(view(low), view(low), sems, i, above)
                    fall = remote(view(high), view(high), sems, i + 1, below)

                    def step(pending=pending, up=up, down=down, has_up=has_up, has_down=has_down):
                        if pending:
                            pending()
                        pl.when(has_up)(up.start)
                        pl.when(has_down)(down.start)

                    def pending(rise=rise, fall=fall, from_below=from_below, from_above=from_above):
                        pl.when(from_below)(rise.wait_recv)
                        pl.when(from_above)(fall.wait_recv)

                    def final(up=up, down=down, has_up=has_up, has_down=has_down):
                        pl.when(has_up)(up.wait_send)
                        pl.when(has_down)(down.wait_send)

                    tasks.add(step)
                    tasks.finals.append(final)
                    sub += 1
            whole.add(axis)
        i, device = tasks.take(), (b ^ 1, z)
        out = remote(full.at[:, :, c, :, cols], full.at[:, :, c, :, cols], sems, i, device)
        into = remote(full.at[:, :, 1 - c, :, cols], full.at[:, :, 1 - c, :, cols], sems, i, device)

        def step(pending=pending, out=out):
            pending()
            out.start()

        tasks.add(step)
        tasks.add(into.wait_recv)
        tasks.finals.append(out.wait_send)

    for j, (order, which, first, count) in enumerate(streams):
        one(j, ORDERS[order], FULL[which], first, count)


def dot(a, b):
    return jnp.dot(a, b, preferred_element_type=F32)


def dot_rows(a, b):
    return lax.dot_general(a, b, (((1,), (1,)), ((), ())), preferred_element_type=F32)


def dot_columns(a, b):
    return lax.dot_general(a, b, (((0,), (0,)), ((), ())), preferred_element_type=F32)


def tile(j, n):
    return pl.ds(pl.multiple_of(j * n, n), n)


def norm_parts(values):
    center = values - jnp.mean(values, -1, keepdims=True)
    inverse = lax.rsqrt(jnp.mean(center * center, -1, keepdims=True) + NORM_EPS)
    return center * inverse, inverse


def norm_rows(source, gain, target, n=256):
    @pl.loop(0, source.shape[0] // n)
    def _(i):
        unit, _ = norm_parts(source[tile(i, n), :].astype(F32))
        target[tile(i, n), :] = (unit * gain).astype(BF)


def lanes(n):
    return lax.broadcasted_iota(jnp.int32, (n, 128), 1)


def rotate(u, cosine, sine):
    partner = jnp.where(lanes(u.shape[0]) % HDIM < HDIM // 2, pltpu.roll(u, 96, 1), pltpu.roll(u, 32, 1))
    return u * cosine + partner * sine


def pair_rows(block):
    zero, first = jnp.zeros_like(block), lanes(block.shape[0]) < HDIM
    return jnp.concatenate([jnp.where(first, block, zero), jnp.where(first, zero, block)], 0)


def weight_tile(full, cols):
    block = full[:, :, :, :, cols]
    return block.reshape(1024, block.shape[-1])


def lay_out_gains(given, square, target):
    square[...] = jnp.zeros_like(square)
    for i, row in enumerate(given):
        square[i : i + 1, 0:32] = row[...].astype(F32)
    target[...] = square[...].T[:32].astype(BF)


def shifted(ref, t):
    return pltpu.roll(ref[:, t * 128 : (t + 1) * 128].astype(F32), HALF, 1)


def lay_out_wide(given, target):
    first, count = lanes(32) < HALF, FF // 128
    for t in range(count + 1):
        into = given[:, t * 128 : (t + 1) * 128].astype(F32)
        gate = jnp.where(first, shifted(given, count + t), 0.0 if t == count else shifted(given, min(count + 1 + t, 2 * count)))
        if t == count:
            into = jnp.where(first, into, 0.0)
        target[:, t * 256 : t * 256 + 128] = into.astype(BF)
        target[:, t * 256 + 128 : (t + 1) * 256] = gate.astype(BF)


def lay_out_narrow(given, target):
    even = FF // 128 * 128
    target[:, :even] = given[:, :even]
    target[:, even:] = jnp.zeros((32, PADDED - even), BF)
    target[:, even:FF] = given[:, even:]


def flip(source, target, c):
    for k in range(8):
        at = (k // 2) + 4 * jnp.where(c == k % 2, 0, 1)
        target[tile(at, 128), :] = source[:, k * 128 : (k + 1) * 128].T


def edge_exchange(tasks, sems, n_seq, up_src, up_dst, down_src, down_dst):
    b, z = lax.axis_index(BATCH), lax.axis_index(SEQ)
    i = tasks.take(2)
    up = remote(up_src, up_dst, sems, i, (b, jnp.minimum(z + 1, n_seq - 1)))
    down = remote(down_src, down_dst, sems, i + 1, (b, jnp.maximum(z - 1, 0)))

    def start():
        pl.when(z < n_seq - 1)(up.start)
        pl.when(z > 0)(down.start)

    def wait():
        pl.when(z > 0)(up.wait_recv)
        pl.when(z < n_seq - 1)(down.wait_recv)

    def final():
        pl.when(z < n_seq - 1)(up.wait_send)
        pl.when(z > 0)(down.wait_send)

    tasks.finals.append(final)
    return start, wait


HELD = ("normed", "queries", "keys", "values", "probs", "attended", "middle", "gains", "flip_normed", "flip_attended")


GROUPS = ((0, 3), (3, 3), (6, 3), (9, 3), (12, 3), (15, 3), (18, 2), (20, 1))


def forward_kernel(direct, n_seq, *refs):
    refs = list(refs)

    def pop(names):
        return {n: refs.pop(0) for n in names}

    given = pop(FULL)
    given_tokens, given_cotangent, all_cosine, all_sine, given_segments, given_padding, second_gain = pop(range(7)).values()
    saved = Saved(*[refs.pop(0) for _ in Saved._fields])
    fulls = pop(FULL)
    held = pop(HELD)
    normed, queries, keys, values, probs, attended, middle, gains, flip_normed, flip_attended = held.values()
    second, flip_second, flip_cotangent, total, final, active, bias = pop(range(7)).values()
    tag_rows, tag_edge, tag_prev, tag_next, cosine, sine = pop(range(6)).values()
    tokens, cotangent, segments, padding, halo, halo_normed = pop(range(6)).values()
    expanded_ring, narrow_ring, wide_ring = pop(range(3)).values()
    shards = dict(given)
    if direct:
        square, raw_first, raw_second, raw_wide, raw_narrow = pop(range(5)).values()
        shards.update(pop("gqown"))
    send_sems, recv_sems, local_sems, ring_sems = refs
    sems = (send_sems, recv_sems)
    held.update(fulls)
    b, z, y, x, c = place() if direct else (lax.axis_index(BATCH), lax.axis_index(SEQ), 0, 0, 0)
    rows, span = 2, 256
    tasks = Tasks()
    copies = {}
    pending_moves = []

    def save(name):
        target = getattr(saved, name)
        copies[name] = pltpu.make_async_copy(held[name], target, local_sems.at[Saved._fields.index(name)])
        copies[name].start()

    exchanges = [edge_exchange(tasks, sems, n_seq, tag_edge, tag_prev, tag_edge, tag_next)]
    for r in range(rows):
        ends = (pl.ds((r + 1) * span - HALF, HALF), pl.ds(r * HALF, HALF), pl.ds(r * span, HALF))
        ends += (pl.ds((rows + r) * HALF, HALF),)
        parts = (ref.at[end] for ref, end in zip((tokens, halo, tokens, halo), ends))
        exchanges.append(edge_exchange(tasks, sems, n_seq, *parts))

    def start_edges():
        for start, _ in exchanges:
            start()

    def wait_edges():
        for _, finish in exchanges:
            finish()

    tasks.add(start_edges)
    if direct:
        add_gather(tasks, GATHER_STREAMS, shards, fulls, sems)

    def prepare():
        pending_moves.pop().wait()
        flip(cotangent, flip_cotangent, c)
        @pl.when(z == 0)
        def _():
            tag_prev[...] = jnp.zeros_like(tag_prev)
            halo[0 : rows * HALF, :] = jnp.zeros((rows * HALF, 1024), BF)

        @pl.when(z == n_seq - 1)
        def _():
            tag_next[...] = jnp.zeros_like(tag_next)
            halo[rows * HALF :, :] = jnp.zeros((rows * HALF, 1024), BF)

    def gain_rows():
        columns = weight_tile(fulls["g"], slice(None)).astype(F32)
        gains[...] = columns.T[:8]
        save("gains")

    def halo_norm():
        norm_rows(halo, gains[0:1, :], halo_normed)

    def first_norm():
        norm_rows(tokens, gains[0:1, :], normed)
        flip(normed, flip_normed, c)
        save("flip_normed")

    def project(first, count, put, done=None):
        def run():
            @pl.loop(first, first + count)
            def _(j):
                weight = weight_tile(fulls["q"], tile(j, 512))
                put(j, dot(normed[...], weight))
                if put is not put_query:
                    put(j, dot(halo_normed[...], weight), True)

            if done:
                save(done)

        return run

    def put_query(j, out):
        for part in range(4):
            for r in range(rows):
                u = out[r * span : (r + 1) * span, part * 128 : (part + 1) * 128]
                u = rotate(u, cosine[HALF : HALF + span, :], sine[HALF : HALF + span, :]) * HDIM**-0.5
                queries[r * span : (r + 1) * span, tile(4 * j + part, 128)] = u.astype(BF)

    def places(outside):
        if outside:
            ends = ((0, 0), (1, HALF + span))
            return [(r, slice((e * rows + r) * HALF, (e * rows + r + 1) * HALF), slice(at, at + HALF)) for e, at in ends for r in range(rows)]
        return [(r, slice(r * span, (r + 1) * span), slice(HALF, HALF + span)) for r in range(rows)]

    def put_key(j, out, outside=False):
        for r, here, there in places(outside):
            for part in range(4):
                u = rotate(out[here, part * 128 : (part + 1) * 128], cosine[there, :], sine[there, :])
                keys[r, there, tile(4 * (j - 2) + part, 128)] = u.astype(BF)

    def put_value(j, out, outside=False):
        for r, here, there in places(outside):
            values[r, there, tile(j - 4, 512)] = out[here].astype(BF)

    tasks.add(prepare)
    tasks.add(gain_rows)
    tasks.add(first_norm)
    tasks.add(wait_edges)
    tasks.add(halo_norm)
    tasks.add(project(0, 2, put_query))
    tasks.add(project(2, 1, put_key))
    tasks.add(project(3, 1, put_key))
    tasks.add(project(4, 2, put_value, "q"))

    def masks():
        first = lanes(8) < HALF
        low, high = (pltpu.roll(tag_rows[:, t * 128 : (t + 1) * 128], HALF, 1) for t in range(2))
        ext = (jnp.where(first, tag_prev[...], low), jnp.where(first, low, high), jnp.where(first, high, tag_next[...]))
        ext = jnp.concatenate([jnp.concatenate([t, jnp.zeros((120, 128), F32)], 0).T for t in ext], 0)
        offset = lax.broadcasted_iota(jnp.int32, (256, 128), 0) - lax.broadcasted_iota(jnp.int32, (256, 128), 1)
        band, self_pair = (offset >= 0) & (offset <= 2 * HALF), offset == HALF
        for r in range(rows):
            for k in range(2):
                query_tag = (segments[r : r + 1, k * 128 : (k + 1) * 128] + 1).astype(F32)
                same = ext[k * 128 : k * 128 + 256, r : r + 1] == query_tag
                bias[r, k] = jnp.where(band & (same | self_pair), 0.0, MASK_FILL)
    tasks.add(masks)

    def attend_block(r, k, p):
        row, window = slice(r * span + k * 128, r * span + (k + 1) * 128), slice(k * 128, k * 128 + 256)
        cols = tile(p, 128)
        scores = dot_rows(pair_rows(keys[r, window, cols]), queries[row, cols])
        parts = []
        for h in range(2):
            s = scores[h * 256 : (h + 1) * 256] + bias[r, k]
            weights = jnp.exp(s - jnp.max(s, 0, keepdims=True))
            parts.append((weights * (1.0 / jnp.sum(weights, 0, keepdims=True))).astype(BF))
        pair = jnp.concatenate(parts, 0)
        probs[r, k, p] = pair
        attended[row, cols] = dot_columns(pair, pair_rows(values[r, window, cols])).astype(BF)

    def attend(first):
        def run():
            if first == 0:
                for name in ("queries", "keys", "values"):
                    save(name)

            @pl.loop(first, first + 2)
            def _(p):
                for r in range(rows):
                    for k in range(2):
                        attend_block(r, k, p)

        return run

    for i in range(4):
        tasks.add(attend(2 * i))

    def project_out():
        @pl.loop(0, 2)
        def _(j):
            cols = tile(j, 512)
            middle[:, cols] = tokens[:, cols].astype(F32) + dot(attended[...], weight_tile(fulls["o"], cols))

        for name in ("o", "probs", "middle"):
            save(name)

    def second_norm():
        norm_rows(middle, gains[1:2, :], second)
        flip(second, flip_second, c)
        total[...] = middle[...]

    def flip_late():
        flip(attended, flip_attended, c)
        save("flip_attended")

    tasks.add(project_out)
    tasks.add(second_norm)
    tasks.add(flip_late)

    streams = {}

    def stream(name, i, source, target):
        streams[name, i] = pltpu.make_async_copy(source, target, ring_sems.at[name, i % 2])
        streams[name, i].start()

    def free(name, i):
        if (name, i) in streams:
            streams.pop((name, i)).wait()

    def gate(i):
        pair, pairs = GROUPS[i]

        def run():
            free(0, i - 2)
            above = dot(cotangent[...], weight_tile(fulls["n"], pl.ds(pair * 128, pairs * 128)))
            out = dot(second[...], weight_tile(fulls["w"], pl.ds(pair * 256, pairs * 256)))
            for k in range(pairs):
                gate_in, gate_up = out[:, k * 256 : k * 256 + 128], out[:, k * 256 + 128 : (k + 1) * 256]
                mass = 0.5 * (1.0 + lax.erf(gate_in * 0.5**0.5))
                density = jnp.exp(-0.5 * gate_in * gate_in) * INV_SQRT_2PI
                gelu, up = gate_in * mass, above[:, k * 128 : (k + 1) * 128]
                slope = gate_up * (mass + gate_in * density)
                expanded_ring[i % 2, :, k * 256 : k * 256 + 128] = (up * slope).astype(BF)
                expanded_ring[i % 2, :, k * 256 + 128 : (k + 1) * 256] = (up * gelu).astype(BF)
                at = (i % 2) * GROUPS[i - 1][1] * 128 + k * 128
                active[:, at : at + 128] = (gelu * gate_up).astype(BF)
            cols = pl.ds(pair * 256, pairs * 256)
            stream(0, i, expanded_ring.at[i % 2, :, pl.ds(0, pairs * 256)], saved.grad_expanded.at[:, cols])
            free(4, i - 2)
            stream(4, i, fulls["w"].at[:, :, :, :, cols], saved.w.at[:, :, :, :, cols])

        return run

    def add_output(i):
        first, width = GROUPS[i - 1][0] * 128, (GROUPS[i - 1][1] + GROUPS[i][1]) * 128

        def run():
            @pl.loop(0, 2)
            def _(j):
                block = fulls["n"][j, :, :, :, pl.ds(first, width)].reshape(512, width)
                total[:, tile(j, 512)] += dot_rows(active[:, :width], block)

            if i == len(GROUPS) - 1:
                final[...] = total[...].astype(BF)
                stream(3, 0, final, saved.outputs)

        return run

    def grad_narrow(i):
        first, width = GROUPS[i - 1][0] * 128, (GROUPS[i - 1][1] + GROUPS[i][1]) * 128

        def run():
            free(1, i - 2)

            @pl.loop(0, 2)
            def _(j):
                narrow_ring[tile(j, 512), :width] = dot(flip_cotangent[tile(j, 512), :], active[:, :width]).astype(BF)

            stream(1, i, narrow_ring.at[:, pl.ds(0, width)], saved.grad_narrow.at[:, pl.ds(first, width)])

        return run

    def grad_wide(i):
        width = GROUPS[i][1] * 256

        def run():
            free(2, i - 2)

            @pl.loop(0, 2)
            def _(j):
                out = dot(flip_second[tile(j, 512), :], expanded_ring[i % 2, :, :width])
                wide_ring[i % 2, tile(j, 512), :width] = out.astype(BF)

            source = wide_ring.at[i % 2, :, pl.ds(0, width)]
            stream(2, i, source, saved.grad_wide.at[:, pl.ds(GROUPS[i][0] * 256, width)])

        return run

    for i in range(len(GROUPS)):
        tasks.add(gate(i))
        tasks.add(grad_wide(i))
        if i % 2:
            tasks.add(add_output(i))
            tasks.add(grad_narrow(i))

    base = len(Saved._fields)
    moves = [(given_segments, segments), (given_padding, padding)]
    if direct:
        moves += [(given["g"], raw_first), (second_gain, raw_second), (given["w"], raw_wide), (given["n"], raw_narrow)]
        moves += [(given[n], shards[n]) for n in "qo"]
    else:
        moves += [(given[n], fulls[n]) for n in FULL]
    here = pl.ds(pl.multiple_of(z * span, span), span + 2 * HALF)
    moves += [(given_tokens, tokens), (all_cosine.at[here, :], cosine), (all_sine.at[here, :], sine)]
    moves += [(given_cotangent, cotangent)]
    moves = [pltpu.make_async_copy(*move, local_sems.at[base + i]) for i, move in enumerate(moves)]
    for move in moves:
        move.start()
    arrived = greet(direct, n_seq)
    for move in moves[:-4]:
        move.wait()
    pending_moves.append(moves[-1])
    tag_rows[...] = jnp.zeros_like(tag_rows)
    tag_rows[0:rows, :] = jnp.where(padding[...] == 1, segments[...] + 1, 0).astype(F32)
    low, high = (pltpu.roll(tag_rows[:, t * 128 : (t + 1) * 128], HALF, 1) for t in range(2))
    tag_edge[...] = jnp.where(lanes(8) < HALF, high, low)
    if direct:
        lay_out_gains((raw_first, raw_second), square, shards["g"])
        lay_out_wide(raw_wide, shards["w"])
        lay_out_narrow(raw_narrow, shards["n"])
        own = [
            pltpu.make_async_copy(shards[n], fulls[n].at[y, x, c, piece(z), :], local_sems.at[base + i])
            for i, n in enumerate(FULL)
        ]
        for copy in own:
            copy.start()
        for copy in own:
            copy.wait()
    for move in moves[-4:-1]:
        move.wait()
    arrived()
    tasks.run(FORWARD_ORDER if direct else range(len(tasks.steps)))
    for copy in list(copies.values()) + list(streams.values()):
        copy.wait()


SHAPES = {
    "g": ((2, 2, 2, 128, 128), BF),
    "q": ((2, 2, 2, 128, 3072), BF),
    "o": ((2, 2, 2, 128, 1024), BF),
    "w": ((2, 2, 2, 128, 2 * PADDED), BF),
    "n": ((2, 2, 2, 128, PADDED), BF),
    "normed": ((512, 1024), BF),
    "queries": ((512, 1024), BF),
    "keys": ((2, 384, 1024), BF),
    "values": ((2, 384, 1024), BF),
    "probs": ((2, 2, 8, 512, 128), BF),
    "attended": ((512, 1024), BF),
    "middle": ((512, 1024), F32),
    "gains": ((8, 1024), F32),
    "flip_normed": ((1024, 512), BF),
    "flip_attended": ((1024, 512), BF),
    "grad_expanded": ((512, 2 * PADDED), BF),
    "grad_narrow": ((1024, PADDED), BF),
    "grad_wide": ((1024, 2 * PADDED), BF),
    "outputs": ((512, 1024), BF),
}
VMEM, ANY = pl.BlockSpec(memory_space=pltpu.VMEM), pl.BlockSpec(memory_space=pl.ANY)


def forward(direct, n_seq, shards, *inputs):
    results = Saved._fields
    count = 400 if direct else 16
    out = pl.pallas_call(
        functools.partial(forward_kernel, direct, n_seq),
        out_shape=tuple(jax.ShapeDtypeStruct(*SHAPES[n]) for n in results),
        in_specs=[ANY] * 12,
        out_specs=(ANY,) * len(results),
        scratch_shapes=[pltpu.VMEM(*SHAPES[n]) for n in FULL + HELD]
        + [
            pltpu.VMEM((512, 1024), BF),
            pltpu.VMEM((1024, 512), BF),
            pltpu.VMEM((1024, 512), BF),
            pltpu.VMEM((512, 1024), F32),
            pltpu.VMEM((512, 1024), BF),
            pltpu.VMEM((512, 768), BF),
            pltpu.VMEM((2, 2, 256, 128), F32),
            pltpu.VMEM((8, 256), F32),
            pltpu.VMEM((8, 128), F32),
            pltpu.VMEM((8, 128), F32),
            pltpu.VMEM((8, 128), F32),
            pltpu.VMEM((256 + 2 * HALF, 128), F32),
            pltpu.VMEM((256 + 2 * HALF, 128), F32),
            pltpu.VMEM((512, 1024), BF),
            pltpu.VMEM((512, 1024), BF),
            pltpu.VMEM((2, 256), jnp.int32),
            pltpu.VMEM((2, 256), jnp.int32),
            pltpu.VMEM((4 * HALF, 1024), BF),
            pltpu.VMEM((4 * HALF, 1024), BF),
            pltpu.VMEM((2, 512, 768), BF),
            pltpu.VMEM((1024, 768), BF),
            pltpu.VMEM((2, 1024, 768), BF),
            *([pltpu.VMEM((128, 128), F32), pltpu.VMEM((1, 32), BF), pltpu.VMEM((1, 32), BF)] if direct else []),
            *([pltpu.VMEM((32, n), BF) for n in (2 * FF, FF, 128, 3072, 1024, 2 * PADDED, PADDED)] if direct else []),
            pltpu.SemaphoreType.DMA((count,)),
            pltpu.SemaphoreType.DMA((count,)),
            pltpu.SemaphoreType.DMA((len(results) + 12,)),
            pltpu.SemaphoreType.DMA((5, 2)),
        ],
        compiler_params=pltpu.CompilerParams(collective_id=1, has_side_effects=True, vmem_limit_bytes=62 << 20),
    )(*shards, *inputs)
    return Saved(*out)


def add_into(target, a, b):
    count = target.shape[0]

    def part(i):
        at = pl.ds(pl.multiple_of(i * 32, 32), 32)
        target[at, :] = a[at, :] + b[at, :]

    if count == 32:
        part(0)
    else:
        pl.loop(0, count // 32)(part)


def landing_shapes(streams):
    result = []
    for order, _, _, count in streams:
        shapes, left, depth = {}, ["y", "x"], 128
        for axis in ORDERS[order][::-1]:
            if axis == "z":
                shapes["z"] = (2,) * len(left) + (160, count)
                depth = 32
            else:
                left.remove(axis)
                shapes[axis] = (2,) * len(left) + (depth, count)
        result.append(shapes)
    return result


def add_scatter(tasks, streams, chunks, sources, totals, slots, landed, sums, sems, credit, ready):
    b, z, y, x, c = place()
    for k, (which, first, count) in enumerate(chunks):
        name, cols = FULL[which], pl.ds(first, count)
        slot = slots.at[k % 2, :, :, :, pl.ds(0, count)]
        out = remote(sources[name].at[:, :, :, cols], slot, sems, tasks.take(), (b ^ 1, z))

        def start(k=k, out=out):
            if k >= 2:
                pl.semaphore_wait(credit.at[k % 2], 1)
            out.start()

        def arrive(k=k, out=out, name=name, cols=cols, slot=slot):
            ready(k)
            out.wait_recv()
            for yy in range(2):
                for xx in range(2):
                    total = totals[name].at[yy, xx, :, cols]
                    add_into(total, total, slot.at[yy, xx])
            if k + 2 < len(chunks):
                pl.semaphore_signal(credit.at[k % 2], inc=1, device_id=(b ^ 1, z), device_id_type=MESH)

        tasks.add(start)
        tasks.add(arrive)
        tasks.finals.append(out.wait_send)

    def one(j, order, name, first, count):
        cols, land = pl.ds(first, count), landed[j]

        def view(fixed, at=None):
            zz = fixed.get("z", slice(None)) if at is None else piece(at)
            return totals[name].at[fixed.get("y", slice(None)), fixed.get("x", slice(None)), zz, cols]

        def blocks(ref):
            if len(ref.shape) == 2:
                return [ref]
            return [r for i in range(ref.shape[0]) for r in blocks(ref.at[i])]

        def accumulate(target, source):
            for t, s in zip(blocks(target), blocks(source)):
                add_into(t, t, s)

        fixed, pending, sub = {}, None, 0
        for axis in order[::-1]:
            if axis in "xy":
                mine, device = (y if axis == "y" else x), (b ^ (2 if axis == "x" else 4), z)
                keep = dict(fixed)
                keep[axis] = mine
                give = dict(fixed)
                give[axis] = 1 - mine
                out = remote(view(give), land[axis], sems, tasks.take(), device)

                def step(pending=pending, out=out):
                    if pending:
                        pending()
                    out.start()

                def pending(out=out, keep=keep, axis=axis):
                    out.wait_recv()
                    accumulate(view(keep), land[axis])

                tasks.add(step)
                tasks.finals.append(out.wait_send)
                fixed, sub = keep, sub + 1
            else:
                left = [a for a in "yx" if a not in fixed]

                def spot(t, own_from_below):
                    at = jnp.where(own_from_below, 128, t * 32)
                    return land["z"].at[(slice(None),) * len(left) + (pl.ds(pl.multiple_of(at, 32), 32),)]

                for hop in (2, 1, 0):
                    i = tasks.take(2)
                    down_piece, up_piece = jnp.maximum(z - 1 - hop, 0), jnp.minimum(z + 1 + hop, 3)
                    has_down, has_up = z - 1 - hop >= 0, z + 1 + hop <= 3
                    below, above = (b, jnp.maximum(z - 1, 0)), (b, jnp.minimum(z + 1, 3))
                    down = remote(view(fixed, down_piece), spot(down_piece, False), sems, i, below)
                    up = remote(view(fixed, up_piece), spot(up_piece, hop == 0), sems, i + 1, above)
                    from_above, from_below = (z < 3) & (z - hop >= 0), (z > 0) & (z + hop <= 3)
                    low, high = jnp.maximum(z - hop, 0), jnp.minimum(z + hop, 3)
                    fall = remote(view(fixed, low), spot(low, False), sems, i, below)
                    rise = remote(view(fixed, high), spot(high, hop == 0), sems, i + 1, above)

                    def step(pending=pending, up=up, down=down, has_up=has_up, has_down=has_down):
                        if pending:
                            pending()
                        pl.when(has_down)(down.start)
                        pl.when(has_up)(up.start)

                    def pending(
                        fall=fall,
                        rise=rise,
                        from_above=from_above,
                        from_below=from_below,
                        low=low,
                        high=high,
                        hop=hop,
                        fixed=fixed,
                        spot=spot,
                    ):
                        @pl.when(from_above)
                        def _():
                            fall.wait_recv()
                            accumulate(view(fixed, low), spot(low, False))

                        @pl.when(from_below)
                        def _():
                            rise.wait_recv()
                            accumulate(view(fixed, high), spot(high, hop == 0))

                    def final(up=up, down=down, has_up=has_up, has_down=has_down):
                        pl.when(has_down)(down.wait_send)
                        pl.when(has_up)(up.wait_send)

                    tasks.add(step)
                    tasks.finals.append(final)
                    sub += 1
                fixed = dict(fixed)
                fixed["z"] = piece(z)

        def last(pending=pending, fixed=fixed):
            pending()
            sums[name][:, cols] = view(fixed)[...].astype(F32)

        tasks.add(last)

    for j, (order, which, first, count) in enumerate(streams):
        one(j, ORDERS[order], FULL[which], first, count)


class Scratch(NamedTuple):
    ring: Any
    expanded: Any
    second: Any
    middle: Any
    branch: Any
    flipped: Any
    keys: Any
    values: Any
    probs: Any
    projected: Any
    grad_v: Any
    edge: Any
    edge_landed: Any
    gains: Any
    cosine: Any
    sine: Any
    tokens: Any
    cotangent: Any


class Saved(NamedTuple):
    q: Any
    o: Any
    w: Any
    queries: Any
    keys: Any
    values: Any
    probs: Any
    middle: Any
    gains: Any
    flip_normed: Any
    flip_attended: Any
    grad_expanded: Any
    grad_narrow: Any
    grad_wide: Any
    outputs: Any


WEIGHTS = ("q", "o", "w", "n")


def lay_out_narrow_sum(held, narrow):
    even = FF // 128 * 128
    narrow[:, :even], narrow[:, even:] = held[:, :even], held[:, even:FF]


def lay_out_wide_sum(held, wide):
    even, first, count = FF // 128 * 128, lanes(32) < HALF, FF // 128

    def gate(t):
        return pltpu.roll(held[:, t * 256 + 128 : (t + 1) * 256], HALF, 1)

    for t in range(count):
        wide[:, t * 128 : (t + 1) * 128] = held[:, t * 256 : t * 256 + 128]
    wide[:, even : even + 128] = jnp.where(first, held[:, count * 256 : count * 256 + 128], gate(0))
    for t in range(count):
        wide[:, even + 128 + t * 128 : even + 256 + t * 128] = jnp.where(first, gate(t), gate(t + 1))


def grad_gain(weight, total, square, column):
    square[0:32, column : column + 1] = jnp.sum(weight[...].astype(F32) * total[...], -1, keepdims=True)


def backward_kernel(direct, n_seq, shapes, *refs):
    refs = list(refs)

    def pop(names):
        return {n: refs.pop(0) for n in names}

    src = Saved(*[refs.pop(0) for _ in Saved._fields])
    given_tokens, given_cotangent, all_cosine, all_sine = pop(range(4)).values()
    if direct:
        given_shards = list(pop(range(4)).values())
    grad_tokens = refs.pop(0)
    if direct:
        targets = list(pop(range(6)).values())
        sums = pop(WEIGHTS)
        square = refs.pop(0)
        laid_wide, laid_narrow, laid_first, laid_second, *own_shards = pop(range(8)).values()
        gain_one, gain_two, qkv_shard, wide_shard = own_shards
    else:
        sums = pop(range(4))
    totals = pop(WEIGHTS if direct else ("q", "o"))
    others = pop(("q", "o"))
    landed = [pop(s) for s in shapes]
    slots = refs.pop(0) if direct else None
    v = Scratch(*[refs.pop(0) for _ in Scratch._fields])
    cosine, sine, tokens, cotangent = v.cosine, v.sine, v.tokens, v.cotangent
    send_sems, recv_sems, local_sems, credit = refs
    sems = (send_sems, recv_sems)
    b, z, y, x, c = place() if direct else (lax.axis_index(BATCH), lax.axis_index(SEQ), 0, 0, 0)
    rows, span = 2, 256
    tasks = Tasks()
    local = {}

    def load(name, source, target):
        local[name] = pltpu.make_async_copy(source, target, local_sems.at[name])
        local[name].start()

    def wait(name):
        local.pop(name).wait()

    def load_group(i):
        cols = pl.ds(i * 768, 768)
        load(WIDE + i % 2, src.w.at[:, :, :, :, cols], v.ring.at[i % 2, :, :, :, :, pl.ds(0, 768)])
        load(EXPANDED + i % 2, src.grad_expanded.at[:, cols], v.expanded.at[i % 2])

    def grad_second(i):
        def run():
            wait(WIDE + i % 2)
            wait(EXPANDED + i % 2)

            @pl.loop(0, 2)
            def _(j):
                block = v.ring[i % 2, j, :, :, :, pl.ds(0, 768)].reshape(512, 768)
                part = dot_rows(v.expanded[i % 2], block)
                if i == 0:
                    v.second[:, tile(j, 512)] = part
                else:
                    v.second[:, tile(j, 512)] += part

            if i < 5:
                load_group(i + 2)
            elif i == 5:
                load(WIDE + 1, src.o, v.ring.at[1])
            else:
                load(WIDE, src.q.at[:, :, :, :, pl.ds(0, 1024)], v.ring.at[0])

        return run

    def load_rest():
        load_group(0)
        load_group(1)
        load(COTANGENT, given_cotangent, cotangent)
        load(MIDDLE, src.middle, v.middle)
        load(GAINS, src.gains, v.gains)
        load(QUERIES, src.queries, v.projected.at[:, pl.ds(0, 1024)])
        load(KEYS, src.keys, v.keys)
        load(VALUES, src.values, v.values)
        load(FLIPPED, src.flip_attended, v.flipped)
        for i in range(2):
            load_probs(i)
        here = pl.ds(pl.multiple_of(z * span + HALF, HALF), span)
        load(COSINE, all_cosine.at[here, :], v.cosine)
        load(SINE, all_sine.at[here, :], v.sine)
        load(TOKENS, given_tokens, tokens)
        if direct:
            for i, (given, held_here) in enumerate(zip(given_shards, own_shards)):
                load(SHARD + i, given, held_here)

    tasks.add(load_rest)
    for i in range(7):
        tasks.add(grad_second(i))

    def norm_back(values, upstream, gain):
        unit, inverse = norm_parts(values)
        scaled = upstream * gain
        return inverse * (
            scaled - jnp.mean(scaled, -1, keepdims=True) - unit * jnp.mean(scaled * unit, -1, keepdims=True)
        )

    def second_norm_back():
        for name in (MIDDLE, GAINS, COTANGENT):
            wait(name)

        @pl.loop(0, 4)
        def _(i):
            at = tile(i, 128)
            grad = norm_back(v.middle[at, :], v.second[at, :], v.gains[1:2, :])
            grad = grad + cotangent[at, :].astype(F32)
            v.middle[at, :] = grad
            v.branch[at, :] = grad.astype(BF)

    tasks.add(second_norm_back)

    def back_out():
        wait(WIDE + 1)

        @pl.loop(0, 2)
        def _(j):
            cols = pl.ds(pl.multiple_of(2048 + j * 512, 512), 512)
            v.projected[:, cols] = dot_rows(v.branch[...], v.ring[1, j].reshape(512, 1024)).astype(BF)

        load(WIDE + 1, src.q.at[:, :, :, :, pl.ds(1024, 1024)], v.ring.at[1])
        for name in (QUERIES, KEYS, VALUES, COSINE, SINE):
            wait(name)

    tasks.add(back_out)

    def grad_weight(name, first, count, source):
        def run():
            if name == "o":
                wait(FLIPPED)

            @pl.loop(first, first + count)
            def _(j):
                cols = tile(j, 512)
                out = dot(v.flipped[...], source(cols)).astype(BF).reshape(2, 2, 2, 128, 512)
                totals[name][:, :, :, cols], others[name][:, :, :, cols] = out[0], out[1]

            if name == "o":
                load(FLIPPED, src.flip_normed, v.flipped)
            if name == "q" and first == 0:
                pass

        return run

    tasks.add(grad_weight("o", 0, 2, lambda cols: v.branch[:, cols]))

    def attend_back_block(r, k, p, i):
        row, window = slice(r * span + k * 128, r * span + (k + 1) * 128), slice(k * 128, k * 128 + 256)
        cols, upper = tile(p, 128), pl.ds(pl.multiple_of(2048 + p * 128, 128), 128)
        half, local_cols = i // 2, tile(p - 4 * (i // 2), 128)
        side = lanes(256) < HDIM
        upstream, pair = v.projected[row, upper], v.probs[i % 2, r, k, p - 2 * i]
        key_pair = pair_rows(v.keys[r, window, cols])
        grad_p = dot_rows(pair_rows(v.values[r, window, cols]), upstream)
        parts = []
        for h in range(2):
            part = slice(h * 256, (h + 1) * 256)
            weights = pair[part].astype(F32)
            inner = jnp.sum(grad_p[part] * weights, 0, keepdims=True)
            parts.append((weights * (grad_p[part] - inner)).astype(BF))
        grad_s = jnp.concatenate(parts, 0)
        back_v = dot(pair, upstream)
        back_k = dot(grad_s, v.projected[row, cols])
        at = slice(k * 128, (k + 1) * 128)
        grad_q = rotate(dot_columns(grad_s, key_pair) * HDIM**-0.5, cosine[at, :], -sine[at, :])
        v.projected[row, cols] = grad_q.astype(BF)
        for which, back, out in ((0, back_k, v.second), (1, back_v, v.grad_v)):
            back = jnp.where(side, back[:256], back[256:])
            if k == 0:
                v.edge[half, 0, which, r, :, local_cols] = back[:HALF].astype(BF)
                out[r * span : r * span + 192, cols] = back[HALF:]
            else:
                out[r * span + 64 : r * span + 192, cols] += back[:128]
                out[r * span + 192 : (r + 1) * span, cols] = back[128:192]
                v.edge[half, 1, which, r, :, local_cols] = back[192:].astype(BF)

    def load_probs(i):
        load(PROBS + i % 2, src.probs.at[:, :, pl.ds(2 * i, 2)], v.probs.at[i % 2])

    def attend_back(i):
        def run():
            wait(PROBS + i % 2)

            @pl.loop(2 * i, 2 * i + 2)
            def _(p):
                for k in range(2):
                    for r in range(rows):
                        attend_back_block(r, k, p, i)

            if i < 2:
                load_probs(i + 2)

        return run

    waits = []
    for i in range(4):
        tasks.add(attend_back(i))
        if i % 2:
            edge, land = v.edge.at[i // 2], v.edge_landed.at[i // 2]
            start, finish = edge_exchange(tasks, sems, n_seq, edge.at[1], land.at[0], edge.at[0], land.at[1])
            tasks.add(start)
            waits.append(finish)
    for half in range(2):
        tasks.add(waits[half])

    def turn_back(half):
        def run():
            here = slice(half * 512, (half + 1) * 512)
            for part, out in ((0, v.second), (1, v.grad_v)):
                for r in range(rows):

                    @pl.when(z > 0)
                    def _():
                        out[r * span : r * span + HALF, here] += v.edge_landed[half, 0, part, r].astype(F32)

                    @pl.when(z < n_seq - 1)
                    def _():
                        at = slice((r + 1) * span - HALF, (r + 1) * span)
                        out[at, here] += v.edge_landed[half, 1, part, r].astype(F32)

            @pl.loop(4 * half, 4 * half + 4)
            def _(p):
                cols, middle_cols, upper = (pl.ds(pl.multiple_of(f + p * 128, 128), 128) for f in (0, 1024, 2048))
                for r in range(rows):
                    at = slice(r * span, (r + 1) * span)
                    turned = rotate(v.second[at, cols], cosine[...], -sine[...])
                    v.projected[at, middle_cols] = turned.astype(BF)
                    v.projected[at, upper] = v.grad_v[at, cols].astype(BF)

        return run

    for half in range(2):
        tasks.add(turn_back(half))

    def grad_qkv(first):
        inner = grad_weight("q", first, 2, lambda cols: v.projected[:, cols])

        def run():
            if first == 0:
                wait(FLIPPED)
            inner()

        return run

    for i, letter in enumerate("abc"):
        tasks.add(grad_qkv(2 * i))

    def grad_normed(i):
        def run():
            wait(WIDE + i % 2)

            @pl.loop(0, 2)
            def _(j):
                block = v.ring[i % 2, j].reshape(512, 1024)
                part = dot_rows(v.projected[:, i * 1024 : (i + 1) * 1024], block)
                if i == 0:
                    v.grad_v[:, tile(j, 512)] = part
                else:
                    v.grad_v[:, tile(j, 512)] += part

            if i == 0:
                load(WIDE, src.q.at[:, :, :, :, pl.ds(2048, 1024)], v.ring.at[0])

        return run

    for i in range(3):
        tasks.add(grad_normed(i))

    def first_norm_back():
        wait(TOKENS)

        @pl.loop(0, 4)
        def _(i):
            at = tile(i, 128)
            grad = norm_back(tokens[at, :].astype(F32), v.grad_v[at, :], v.gains[0:1, :])
            v.branch[at, :] = (v.middle[at, :] + grad).astype(BF)

        load(RESULT, v.branch, grad_tokens)

    tasks.add(first_norm_back)
    if direct:

        def finish(name):
            if name == "o":
                load(OWN + 1, sums["o"], targets[1])
            elif name == "n":
                lay_out_narrow_sum(sums["n"], laid_narrow)
                load(OWN + 3, laid_narrow, targets[3])
            else:
                for i in range(4):
                    wait(SHARD + i)
                square[...] = jnp.zeros_like(square)
                lay_out_wide_sum(sums["w"], laid_wide)
                grad_gain(wide_shard, laid_wide, square, 1)
                load(OWN + 2, laid_wide, targets[2])

        for name in "now":
            tasks.add(functools.partial(finish, name))

        sources = dict(others)
        sources.update({n: g.at[1] for n, g in (("n", src.grad_narrow), ("w", src.grad_wide))})

        def load_total(k):
            which, first, count = SCATTER_CHUNKS[k]
            if FULL[which] in sources and FULL[which] not in others:
                cols = pl.ds(first, count)
                source = (src.grad_narrow if FULL[which] == "n" else src.grad_wide).at[0, :, :, :, cols]
                load(LOADS + k, source, totals[FULL[which]].at[:, :, :, cols])

        def ready(k):
            if LOADS + k in local:
                wait(LOADS + k)

        add_scatter(tasks, SCATTER_STREAMS, SCATTER_CHUNKS, sources, totals, slots, landed, sums, sems, credit, ready)
        load_total(0)
    if direct:
        for k in range(1, len(SCATTER_CHUNKS)):
            load_total(k)
    greet(direct, n_seq)()
    tasks.run(BACKWARD_ORDER if direct else range(len(tasks.steps)))
    if direct:
        grad_gain(qkv_shard, sums["q"], square, 0)
        columns = square[...].T
        laid_first[...], laid_second[...] = columns[0:8], columns[0:8]
        laid_first[0:1, 0:32] = columns[0:1, 0:32] / gain_one[...].astype(F32)
        laid_second[0:1, 0:32] = columns[1:2, 0:32] / gain_two[...].astype(F32)
        load(OWN, sums["q"], targets[0])
        load(OWN + 4, laid_first, targets[4])
        load(OWN + 5, laid_second, targets[5])
    else:
        for i, name in enumerate("qo"):
            load(OWN + i, totals[name], sums[i])
            load(OTHER + i, others[name], sums[2 + i])
    for copy in local.values():
        copy.wait()


WIDE, EXPANDED, PROBS, OWN, OTHER = 0, 2, 4, 6, 8
MIDDLE, GAINS, QUERIES, KEYS, VALUES, FLIPPED, RESULT, COSINE, SINE, TOKENS, COTANGENT, SHARD, _, _, _, LOADS = range(12, 28)


def backward(direct, n_seq, saved, *inputs):
    split = lambda a: a.reshape(2, 2, 2, 128, -1)
    saved = saved._replace(grad_narrow=split(saved.grad_narrow), grad_wide=split(saved.grad_wide))
    shapes = landing_shapes(SCATTER_STREAMS) if direct else []
    widths = {"q": 3072, "o": 1024, "w": 2 * PADDED, "n": PADDED}
    held = WEIGHTS if direct else ("q", "o")
    half = lambda n: (2, 2, 128, widths[n])
    if direct:
        sums = [jax.ShapeDtypeStruct(s, F32) for s in ((32, 3072), (32, 1024), (32, 2 * FF), (32, FF), (8, 128), (8, 128))]
    else:
        sums = [jax.ShapeDtypeStruct(half(n), BF) for n in ("q", "o", "q", "o")]
    largest = max(count for _, _, count in SCATTER_CHUNKS)
    count = 400 if direct else 16
    out = pl.pallas_call(
        functools.partial(backward_kernel, direct, n_seq, shapes),
        out_shape=(jax.ShapeDtypeStruct((512, 1024), BF), *sums),
        in_specs=[ANY] * (len(saved) + len(inputs)),
        out_specs=(ANY,) * (1 + len(sums)),
        scratch_shapes=([pltpu.VMEM((32, widths[n]), F32) for n in WEIGHTS] if direct else [])
        + ([pltpu.VMEM((128, 128), F32)] if direct else [])
        + ([pltpu.VMEM((32, n), F32) for n in (2 * FF, FF)] + [pltpu.VMEM((8, 128), F32)] * 2 if direct else [])
        + ([pltpu.VMEM((1, 32), BF)] * 2 + [pltpu.VMEM((32, n), BF) for n in (3072, 2 * FF)] if direct else [])
        + [pltpu.VMEM(half(n), BF) for n in held]
        + [pltpu.VMEM(half(n), BF) for n in ("q", "o")]
        + [pltpu.VMEM(s, BF) for stream in shapes for s in stream.values()]
        + ([pltpu.VMEM((2, 2, 2, 128, largest), BF)] if direct else [])
        + [
            pltpu.VMEM((2, 2, 2, 2, 128, 1024), BF),
            pltpu.VMEM((2, 512, 768), BF),
            pltpu.VMEM((512, 1024), F32),
            pltpu.VMEM((512, 1024), F32),
            pltpu.VMEM((512, 1024), BF),
            pltpu.VMEM((1024, 512), BF),
            pltpu.VMEM((2, 384, 1024), BF),
            pltpu.VMEM((2, 384, 1024), BF),
            pltpu.VMEM((2, 2, 2, 2, 512, 128), BF),
            pltpu.VMEM((512, 3072), BF),
            pltpu.VMEM((512, 1024), F32),
            pltpu.VMEM((2, 2, 2, 2, HALF, 512), BF),
            pltpu.VMEM((2, 2, 2, 2, HALF, 512), BF),
            pltpu.VMEM((8, 1024), F32),
            pltpu.VMEM((256, 128), F32),
            pltpu.VMEM((256, 128), F32),
            pltpu.VMEM((512, 1024), BF),
            pltpu.VMEM((512, 1024), BF),
            pltpu.SemaphoreType.DMA((count,)),
            pltpu.SemaphoreType.DMA((count,)),
            pltpu.SemaphoreType.DMA((LOADS + len(SCATTER_CHUNKS),)),
            pltpu.SemaphoreType.REGULAR((2,)),
        ],
        compiler_params=pltpu.CompilerParams(collective_id=2, has_side_effects=True, vmem_limit_bytes=63 << 20),
    )(*saved, *inputs)
    return out


def tables(length):
    frequency = np.float32(ROPE_BASE) ** (-(2.0 * np.arange(HDIM // 2, dtype=np.float32)) / np.float32(HDIM))
    angles = np.arange(-HALF, length + HALF, dtype=np.float32)[:, None] * frequency[None, :].astype(np.float32)
    cosine, sine = np.cos(angles), np.sin(angles)
    return np.concatenate([cosine] * 4, 1), np.concatenate([-sine, sine, -sine, sine], 1)


def interleave(wide):
    lead = wide.shape[0]
    wide = jnp.pad(wide.reshape(lead, 2, FF), ((0, 0), (0, 0), (0, PADDED - FF)))
    return wide.reshape(lead, 2, PADDED // 128, 128).swapaxes(1, 2).reshape(lead, 2 * PADDED)


def separate(wide):
    lead = wide.shape[0]
    wide = wide.reshape(lead, PADDED // 128, 2, 128).swapaxes(1, 2).reshape(lead, 2, PADDED)
    return wide[:, :, :FF].reshape(lead, 2 * FF)


def hand_over_kernel(*refs):
    count = (len(refs) - 2) // 3
    sources, targets, held = refs[:count], refs[count : 2 * count], refs[2 * count : 3 * count]
    arrive, leave = refs[3 * count :]
    moves = [pltpu.make_async_copy(s, h, arrive.at[i]) for i, (s, h) in enumerate(zip(sources, held))]
    for move in moves:
        move.start()
    backs = []
    for i, (h, t) in enumerate(zip(held, targets)):
        moves[i].wait()
        backs.append(pltpu.make_async_copy(h, t, leave.at[i]))
        backs[i].start()
    for back in backs:
        back.wait()


def hand_over(*arrays):
    count = len(arrays)
    return pl.pallas_call(
        hand_over_kernel,
        out_shape=tuple(jax.ShapeDtypeStruct(a.shape, a.dtype) for a in arrays),
        in_specs=[ANY] * count,
        out_specs=(ANY,) * count,
        scratch_shapes=[pltpu.VMEM(a.shape, a.dtype) for a in arrays] + [pltpu.SemaphoreType.DMA((count,))] * 2,
        compiler_params=pltpu.CompilerParams(vmem_limit_bytes=62 << 20),
    )(*arrays)


def body(
    tokens,
    segment_ids,
    padding_mask,
    qkv_weight,
    out_weight,
    wide_weight,
    narrow_weight,
    first_gain,
    second_gain,
    cotangent,
):
    row_count, span, width = tokens.shape
    count = row_count * span
    n_seq = lax.axis_size(SEQ)
    direct = (lax.axis_size(BATCH), n_seq) == (8, 4)
    gains = jnp.stack([first_gain, second_gain])
    gain_rows = (first_gain.reshape(1, -1), second_gain.reshape(1, -1))
    if direct:
        shards = (gain_rows[0], qkv_weight, out_weight, wide_weight, narrow_weight)
    else:
        shards = (
            jnp.pad(gains.T, ((0, 0), (0, 126))),
            qkv_weight,
            out_weight,
            interleave(wide_weight),
            jnp.pad(narrow_weight, ((0, 0), (0, PADDED - FF))),
        )
        shards = [lax.all_gather(s, (BATCH, SEQ), axis=0, tiled=True).reshape(2, 2, 2, 128, s.shape[-1]) for s in shards]
    cosine, sine = (jnp.asarray(t) for t in tables(n_seq * span))
    hidden, upstream = tokens.reshape(count, width), cotangent.reshape(count, width)
    saved = forward(direct, n_seq, shards, hidden, upstream, cosine, sine, segment_ids, padding_mask, gain_rows[1])
    if direct:
        grad_tokens, *weight_grads = backward(
            direct, n_seq, saved, hidden, upstream, cosine, sine, *gain_rows, qkv_weight, wide_weight
        )
        outputs, grad_tokens, grad_qkv, grad_out, grad_wide, grad_narrow, grad_first, grad_second = hand_over(
            saved.outputs, grad_tokens, *weight_grads
        )
        grad_first, grad_second = (g[0, : first_gain.shape[0]] for g in (grad_first, grad_second))
    else:
        outputs = saved.outputs
        grad_tokens, own_q, own_o, other_q, other_o = backward(direct, n_seq, saved, hidden, upstream, cosine, sine)
        grads = [jnp.stack([own, other]) for own, other in ((own_q, other_q), (own_o, other_o))]
        sums = []
        for g in grads + [saved.grad_wide, saved.grad_narrow]:
            g = jnp.moveaxis(g.reshape(2, 4, 128, -1), 0, 1).reshape(width, -1)
            sums.append(lax.psum_scatter(g, (BATCH, SEQ), scatter_dimension=0, tiled=True).astype(F32))
        grad_qkv, grad_out, grad_wide, grad_narrow = sums
        grad_wide, grad_narrow = separate(grad_wide), grad_narrow[:, :FF]

        def gain_grad(weight, grad, gain):
            return jnp.sum(weight.astype(F32) * grad, 1) / gain.astype(F32)

        grad_first = gain_grad(qkv_weight, grad_qkv, first_gain)
        grad_second = gain_grad(wide_weight, grad_wide, second_gain)
    return (
        outputs.reshape(tokens.shape),
        grad_tokens.reshape(tokens.shape),
        grad_qkv,
        grad_out,
        grad_wide,
        grad_narrow,
        grad_first,
        grad_second,
    )


def solution(mesh):
    placed = (
        P(BATCH, SEQ, None),
        P(BATCH, SEQ),
        P(BATCH, SEQ),
        P((BATCH, SEQ), None),
        P((BATCH, SEQ), None),
        P((BATCH, SEQ), None),
        P((BATCH, SEQ), None),
        P((BATCH, SEQ)),
        P((BATCH, SEQ)),
        P(BATCH, SEQ, None),
    )
    return jax.shard_map(
        body,
        mesh=mesh,
        in_specs=placed,
        out_specs=(
            P(BATCH, SEQ, None),
            P(BATCH, SEQ, None),
            P((BATCH, SEQ), None),
            P((BATCH, SEQ), None),
            P((BATCH, SEQ), None),
            P((BATCH, SEQ), None),
            P((BATCH, SEQ)),
            P((BATCH, SEQ)),
        ),
        check_vma=False,
    )
```
